256 devices in a mesh: ctx: 32 (over y, z), exp: 8 (over x, core).
Axes of the slice: x: 4, y: 4, z: 8, core: 2. Of those that a mesh axis runs over, the one named last changes fastest.
Arguments:
- query_rows: bfloat16 [8, 4096, 4096], P('exp', 'ctx'), may hold values from -150 to 150, as said below
- key_matrix_all: bfloat16 [8, 4096, 512], P('exp', 'ctx'), may hold values from -5 to 5
- value_matrix_all: bfloat16 [8, 4096, 512], P('exp', 'ctx'), may hold values from -6 to 6
- context_grad: bfloat16 [8, 4096, 4096], P('exp', 'ctx'), may hold values from -6 to 6
- mixture_input: bfloat16 [8, 4096, 2048], P('exp', 'ctx'), may hold values from -6 to 6
- mixture_grad: bfloat16 [8, 4096, 2048], P('exp', 'ctx'), may hold values from -6 to 6
- expert_ids: int32 [8, 4096, 8], P('exp', 'ctx'), may hold values from 0 to 127, as said below
- route_weight: bfloat16 [8, 4096, 8], P('exp', 'ctx'), may hold values from 0.049804688 to 0.5
- gate_weight: bfloat16 [8, 2048, 768], P('exp', 'ctx'), may hold values from -0.125 to 0.125
- up_weight: bfloat16 [8, 2048, 768], P('exp', 'ctx'), may hold values from -0.125 to 0.125
- down_weight: bfloat16 [8, 2048, 768], P('exp', 'ctx'), may hold values from -0.21875 to 0.21875
Outputs:
- query_grad: bfloat16 [8, 4096, 4096], P('exp', 'ctx')
- key_grad: bfloat16 [8, 4096, 512], P('exp', 'ctx')
- value_grad: bfloat16 [8, 4096, 512], P('exp', 'ctx')
- input_grad: bfloat16 [8, 4096, 2048], P('exp', 'ctx')
- route_grad: bfloat16 [8, 4096, 8], P('exp', 'ctx')
- gate_grad: bfloat16 [8, 2048, 768], P('exp', 'ctx')
- up_grad: bfloat16 [8, 2048, 768], P('exp', 'ctx')
- down_grad: bfloat16 [8, 2048, 768], P('exp', 'ctx')
The draws below stay inside these ranges and needn't reach their ends.
Inputs may be any that keep to these rules, and one draw needn't show every extreme that they name: query_rows and key_matrix_all may have rows aligned with each other. `expert_ids`: each token names 8 different experts. Among the 128 tokens of one device at most 8 name any one expert of the window, and in every draw one expert of the window is named by exactly 8 tokens of every device.
All inputs are finite; a program needn't handle non-finite values.
Results may differ from the reference program's by a relative error of at most 0.025.
Values may be sent and summed in bfloat16 or wider, within the bound.
A program may use at most 192 MiB of HBM per device.

```python
import math
import jax
import jax.numpy as jnp
from jax import lax

D = 2048
QUERY_HEADS = 32
KEY_VALUE_HEADS = 4
HEAD_SIZE = 128
FF = 768
EXPERTS = 128
TOPK = 8
TOK_DEV = 128
GROUP_TOKENS = 4096
SEQUENCE_LENGTH = 4096
GROUPS = 8
SEQUENCE_COUNT = 8
WINDOW = 8
EXP_PER = 16
CAP = 8
N_CTX = 32


def key_base(key):
    return jnp.clip(jax.random.normal(key, (GROUPS, GROUP_TOKENS, KEY_VALUE_HEADS, HEAD_SIZE), jnp.float32), -5.0, 5.0)


def draw_key_matrix_all(key, part):
    starting_rows = key_base(key)
    return starting_rows.reshape(GROUPS, GROUP_TOKENS, KEY_VALUE_HEADS * HEAD_SIZE).astype(jnp.bfloat16)


def draw_query_rows(key, part):
    key = jax.random.fold_in(key, 7)
    values = jnp.clip(jax.random.normal(key, (GROUPS, GROUP_TOKENS, QUERY_HEADS, HEAD_SIZE), jnp.float32), -6.0, 6.0)
    return values.reshape(GROUPS, GROUP_TOKENS, QUERY_HEADS * HEAD_SIZE).astype(jnp.bfloat16)


def draw_expert_ids(key, part):
    key = jax.random.fold_in(key, 11)
    key_list = jax.random.split(key, 5)
    total_rows = GROUPS * GROUP_TOKENS
    blocks = total_rows // TOK_DEV
    full_owner = jax.random.randint(key_list[0], (), 0, WINDOW)
    counts = jax.random.randint(key_list[1], (blocks, WINDOW), 0, CAP + 1)
    counts = jnp.where(jnp.arange(WINDOW)[None, :] == full_owner, CAP, counts)
    orders = jax.vmap(lambda sub_key: jax.random.permutation(sub_key, TOK_DEV))(jax.random.split(key_list[2], blocks * WINDOW))
    rank_rows = jnp.argsort(orders.reshape(blocks, WINDOW, TOK_DEV), axis=-1)
    carried = (rank_rows < counts[:, :, None]).transpose(0, 2, 1).reshape(total_rows, WINDOW).astype(jnp.int32)
    others = EXPERTS - WINDOW
    fill_order = jax.vmap(lambda sub_key: jax.random.permutation(sub_key, others)[:TOPK])(jax.random.split(key_list[3], total_rows))
    fill_ids = fill_order // (EXP_PER - 1) * EXP_PER + 1 + fill_order % (EXP_PER - 1)
    count_row = jnp.sum(carried, axis=1)
    place_index = jnp.cumsum(carried, axis=1) - 1
    slot_iota = jnp.arange(TOPK)
    window_ids = jnp.arange(WINDOW) * EXP_PER
    from_window = jnp.sum(carried[:, None, :] * (place_index[:, None, :] == slot_iota[None, :, None]).astype(jnp.int32) * window_ids[None, None, :], axis=2)
    fill_pick = jnp.take_along_axis(fill_ids, jnp.clip(slot_iota[None, :] - count_row[:, None], 0, TOPK - 1), axis=1)
    row_ids = jnp.where(slot_iota[None, :] < count_row[:, None], from_window, fill_pick)
    shuffle = jax.vmap(lambda sub_key: jax.random.permutation(sub_key, TOPK))(jax.random.split(key_list[4], total_rows))
    chosen_ids = jnp.take_along_axis(row_ids, shuffle, axis=1)
    return chosen_ids.reshape(GROUPS, GROUP_TOKENS, TOPK).astype(jnp.int32)


def level_of(rng, dims, cuts, low, top_value):
    loudness = 1.0
    for dim, blocks in cuts:
        heights = jax.random.uniform(jax.random.fold_in(jax.random.fold_in(rng, 6), dim), (blocks,), jnp.float32, low / len(cuts), top_value / len(cuts))
        loudness = loudness * jnp.repeat(jnp.exp(heights), dims[dim] // blocks).reshape((-1,) + (1,) * (len(dims) - 1 - dim))
    return loudness


def centred(stream_key, shape, deviation, most, pieces=(), held_as=jnp.bfloat16):
    drawn = deviation * jax.random.normal(stream_key, shape, jnp.float32)
    if pieces:
        drawn = drawn * level_of(stream_key, shape, pieces, -0.22, 0.18)
    return jnp.clip(drawn, -most, most).astype(held_as)


def setup_inputs(seed: int = 0) -> dict:
    streams_of = jax.random.split(jax.random.key(seed), 12)
    query_rows = draw_query_rows(jax.random.fold_in(streams_of[11], 71), 0)
    key_matrix_all = draw_key_matrix_all(jax.random.fold_in(streams_of[11], 71), 0)
    value_matrix_all = centred(streams_of[2], (GROUPS, GROUP_TOKENS, KEY_VALUE_HEADS * HEAD_SIZE), 1.0, 6.0, ((0, 8), (1, 32)))
    context_grad = centred(streams_of[3], (GROUPS, GROUP_TOKENS, QUERY_HEADS * HEAD_SIZE), 1.0, 6.0, ((0, 8), (1, 32)))
    mixture_input = centred(streams_of[4], (GROUPS, GROUP_TOKENS, D), 1.0, 6.0, ((0, 8), (1, 32)))
    mixture_grad = centred(streams_of[5], (GROUPS, GROUP_TOKENS, D), 1.0, 6.0, ((0, 8), (1, 32)))
    expert_ids = draw_expert_ids(jax.random.fold_in(streams_of[11], 71), 0)
    route_weight = jnp.clip(jnp.exp(math.log(0.5) - 2.306499 * jax.random.uniform(streams_of[7], (GROUPS, GROUP_TOKENS, TOPK), jnp.float32) ** level_of(streams_of[7], (GROUPS, GROUP_TOKENS, TOPK), ((0, 8), (1, 32)), -0.2, 0.2)), 0.049804688, 0.5).astype(jnp.bfloat16)
    gate_weight = centred(streams_of[8], (WINDOW, D, FF), D ** -0.5, 0.125, ((0, 8), (1, 32)))
    up_weight = centred(streams_of[9], (WINDOW, D, FF), D ** -0.5, 0.125, ((0, 8), (1, 32)))
    down_weight = centred(streams_of[10], (WINDOW, D, FF), FF ** -0.5, 0.21875, ((0, 8), (1, 32)))
    return dict(query_rows=query_rows, key_matrix_all=key_matrix_all, value_matrix_all=value_matrix_all, context_grad=context_grad, mixture_input=mixture_input, mixture_grad=mixture_grad, expert_ids=expert_ids, route_weight=route_weight, gate_weight=gate_weight, up_weight=up_weight, down_weight=down_weight)


def rounded_length(values):
    return lax.optimization_barrier(values.astype(jnp.bfloat16)).astype(jnp.float32)

def sequence_attention(operands):
    query_one, single_key_head, single_value_head, cot_one = operands
    span_length = query_one.shape[0]
    query_group_width = QUERY_HEADS // KEY_VALUE_HEADS
    score_scale = 1.0 / math.sqrt(HEAD_SIZE)
    queries = query_one.reshape(span_length, QUERY_HEADS, HEAD_SIZE).astype(jnp.float32)
    every_key_head = jnp.repeat(single_key_head.reshape(span_length, KEY_VALUE_HEADS, HEAD_SIZE), query_group_width, axis=1).astype(jnp.float32)
    every_value_head = jnp.repeat(single_value_head.reshape(span_length, KEY_VALUE_HEADS, HEAD_SIZE), query_group_width, axis=1).astype(jnp.float32)
    cotangent = cot_one.reshape(span_length, QUERY_HEADS, HEAD_SIZE).astype(jnp.float32)
    blocks = max(1, min(8, span_length // 512))
    block_rows = span_length // blocks
    key_running_sum = jnp.zeros((span_length, QUERY_HEADS, HEAD_SIZE), jnp.float32)
    value_running_sum = jnp.zeros((span_length, QUERY_HEADS, HEAD_SIZE), jnp.float32)
    query_parts = []
    for block_index in range(blocks):
        first_row = block_index * block_rows
        stop_row = first_row + block_rows
        query_block = queries[first_row:stop_row]
        cot_block = cotangent[first_row:stop_row]
        keys_seen = every_key_head[:stop_row]
        values_seen = every_value_head[:stop_row]
        scores = jnp.einsum('qhd,khd->hqk', query_block, keys_seen) * score_scale
        allowed = jnp.arange(stop_row)[None, :] <= (first_row + jnp.arange(block_rows))[:, None]
        scores = jnp.where(allowed[None], scores, -jnp.inf)
        row_peak = lax.optimization_barrier(jnp.max(scores, axis=-1, keepdims=True))
        shifted_exp = jnp.exp(scores - row_peak)
        prob_rows = shifted_exp / lax.optimization_barrier(jnp.sum(shifted_exp, axis=-1, keepdims=True))
        prob_grad = jnp.einsum('qhd,khd->hqk', cot_block, values_seen)
        row_dot = lax.optimization_barrier(jnp.sum(prob_rows * prob_grad, axis=-1, keepdims=True))
        score_grad = rounded_length(prob_rows * (prob_grad - row_dot))
        value_running_sum = value_running_sum.at[:stop_row].add(jnp.einsum('hqk,qhd->khd', rounded_length(prob_rows), cot_block))
        key_running_sum = key_running_sum.at[:stop_row].add(jnp.einsum('hqk,qhd->khd', score_grad, query_block) * score_scale)
        query_parts.append(jnp.einsum('hqk,khd->qhd', score_grad, keys_seen) * score_scale)
    query_out = jnp.concatenate(query_parts, axis=0).reshape(span_length, QUERY_HEADS * HEAD_SIZE).astype(jnp.bfloat16)
    key_result = rounded_length(key_running_sum).reshape(span_length, KEY_VALUE_HEADS, query_group_width, HEAD_SIZE).sum(axis=2).reshape(span_length, KEY_VALUE_HEADS * HEAD_SIZE).astype(jnp.bfloat16)
    value_result = rounded_length(value_running_sum).reshape(span_length, KEY_VALUE_HEADS, query_group_width, HEAD_SIZE).sum(axis=2).reshape(span_length, KEY_VALUE_HEADS * HEAD_SIZE).astype(jnp.bfloat16)
    return (query_out, key_result, value_result)

def reference(query_rows, key_matrix_all, value_matrix_all, context_grad, mixture_input, mixture_grad, expert_ids, route_weight, gate_weight, up_weight, down_weight):

    def by_sequence(values):
        return values.reshape(SEQUENCE_COUNT, SEQUENCE_LENGTH, values.shape[2])

    def by_group(values):
        return values.reshape(GROUPS, GROUP_TOKENS, values.shape[2])
    query_seq, key_seq, value_seq = lax.map(sequence_attention, (by_sequence(query_rows), by_sequence(key_matrix_all), by_sequence(value_matrix_all), by_sequence(context_grad)))
    query_grad = by_group(query_seq)
    key_grad = by_group(key_seq)
    value_grad = by_group(value_seq)
    total_rows = GROUPS * GROUP_TOKENS
    tokens = mixture_input.reshape(total_rows, D).astype(jnp.float32)
    cotangent = mixture_grad.reshape(total_rows, D).astype(jnp.float32)
    routes = expert_ids.reshape(total_rows, TOPK)
    weights_flat = route_weight.reshape(total_rows, TOPK).astype(jnp.float32)
    by_context = jnp.arange(total_rows, dtype=jnp.int32).reshape(GROUPS, N_CTX, TOK_DEV).transpose(1, 0, 2).reshape(N_CTX, GROUPS * TOK_DEV)
    slot_count = GROUPS * CAP
    input_acc = jnp.zeros((total_rows, D), jnp.float32)
    route_acc = jnp.zeros((total_rows, TOPK), jnp.float32)
    gate_list = []
    up_list = []
    down_list = []
    for owner_index in range(WINDOW):
        expert_number = owner_index * EXP_PER
        hit_mask = routes == expert_number
        live_weight = lax.optimization_barrier(jnp.sum(jnp.where(hit_mask, weights_flat, 0.0), axis=1))
        live_rows = jnp.any(hit_mask, axis=1)

        def pick_rows(row_ids):
            return jnp.nonzero(live_rows[row_ids], size=slot_count, fill_value=0)[0].astype(jnp.int32)
        local_index = jax.vmap(pick_rows)(by_context)
        counts = lax.optimization_barrier(jnp.sum(live_rows[by_context].astype(jnp.int32), axis=1))
        valid_slot = jnp.arange(slot_count)[None, :] < counts[:, None]
        picked = jnp.take_along_axis(by_context, local_index, axis=1)
        keep_slot = valid_slot.astype(jnp.float32)
        rows_in = tokens[picked]
        cot_in = cotangent[picked]
        weight_in = live_weight[picked] * keep_slot
        gate_mat = gate_weight[owner_index].astype(jnp.float32)
        up_mat = up_weight[owner_index].astype(jnp.float32)
        down_mat = down_weight[owner_index].astype(jnp.float32)
        gate_act = jnp.einsum('cmd,df->cmf', rows_in, gate_mat)
        up_act = jnp.einsum('cmd,df->cmf', rows_in, up_mat)
        sigma_gate = jax.nn.sigmoid(gate_act)
        silu_gate = gate_act * sigma_gate
        hidden = rounded_length(silu_gate * up_act)
        expert_out = jnp.einsum('cmf,df->cmd', hidden, down_mat)
        route_val = rounded_length(lax.optimization_barrier(jnp.sum(cot_in * expert_out, axis=-1)))
        scaled_cot = rounded_length(weight_in[..., None] * cot_in)
        hidden_grad = jnp.einsum('cmd,df->cmf', scaled_cot, down_mat)
        gate_pre = rounded_length(hidden_grad * up_act * sigma_gate * (1.0 + gate_act * (1.0 - sigma_gate)))
        up_pre = rounded_length(hidden_grad * silu_gate)
        row_grad = rounded_length(jnp.einsum('cmf,df->cmd', gate_pre, gate_mat) + jnp.einsum('cmf,df->cmd', up_pre, up_mat))
        input_acc = input_acc.at[picked].add(row_grad * keep_slot[..., None])
        route_token = jnp.zeros((total_rows,), jnp.float32).at[picked].add(route_val * keep_slot)
        route_acc = route_acc + hit_mask.astype(jnp.float32) * route_token[:, None]
        gate_list.append(lax.optimization_barrier(jnp.sum(rounded_length(jnp.einsum('cmd,cmf->cdf', rows_in, gate_pre)), axis=0)).astype(jnp.bfloat16))
        up_list.append(lax.optimization_barrier(jnp.sum(rounded_length(jnp.einsum('cmd,cmf->cdf', rows_in, up_pre)), axis=0)).astype(jnp.bfloat16))
        down_list.append(lax.optimization_barrier(jnp.sum(rounded_length(jnp.einsum('cmd,cmf->cdf', scaled_cot, hidden)), axis=0)).astype(jnp.bfloat16))
    input_grad = input_acc.astype(jnp.bfloat16).reshape(GROUPS, GROUP_TOKENS, D)
    route_grad = route_acc.astype(jnp.bfloat16).reshape(GROUPS, GROUP_TOKENS, TOPK)
    return (query_grad, key_grad, value_grad, input_grad, route_grad, jnp.stack(gate_list), jnp.stack(up_list), jnp.stack(down_list))
```

```python
import functools
import math

import jax
import jax.numpy as jnp
from jax import lax
from jax.experimental import pallas as pl
from jax.experimental.pallas import tpu as pltpu
from jax.sharding import PartitionSpec as P

D = 2048
QUERY_HEADS = 32
KEY_VALUE_HEADS = 4
HEAD_SIZE = 128
FF = 768
EXPERTS = 128
TOPK = 8
CAP = 8
NY = 4
NZ = 8
NE = 8
TOK = 128
GW = QUERY_HEADS // KEY_VALUE_HEADS * HEAD_SIZE
DS = D // NY
WD = D // (NY * NZ)
KC = 512
HALF = 4
ROWS = HALF * TOK
MESH = pl.DeviceIdType.MESH
VMEM_MOST = 56 * 1024 * 1024
BF = jnp.bfloat16
F32 = jnp.float32


def places():
    ctx = lax.axis_index("ctx")
    return lax.div(ctx, NZ), lax.rem(ctx, NZ), lax.axis_index("exp")


def at_y(y, z, e, shift):
    peer = lax.rem(y + shift, NY)
    return peer, (peer * NZ + z, e)


def at_z(y, z, e, shift):
    peer = lax.rem(z + shift + NZ, NZ)
    return peer, (y * NZ + peer, e)


def at_e(y, z, e, shift):
    peer = lax.rem(e + shift, NE)
    return peer, (y * NZ + z, peer)


def greet(peers):
    barrier = pltpu.get_barrier_semaphore()
    for peer in peers:
        pl.semaphore_signal(barrier, inc=1, device_id=peer, device_id_type=MESH)
    pl.semaphore_wait(barrier, len(peers))


def remote(src, dst, send, recv, index, peer):
    return pltpu.make_async_remote_copy(
        src_ref=src,
        dst_ref=dst,
        send_sem=send.at[index],
        recv_sem=recv.at[index],
        device_id=peer,
        device_id_type=MESH,
    )


def columns(index, width):
    return pl.ds(pl.multiple_of(index * width, width), width)


def inbound_kernel(
    q, do, k, v, rows, wg, wu, wd,
    q_all, do_all, k_all, v_all, rows_own, xc, wg_all, wu_all, wd_all,
    local_sem, y_send, y_recv, e_send, e_recv, x_send, x_recv, r_send, r_recv, l_send, l_recv,
):
    y, z, e = places()
    greet(
        [at_y(y, z, e, d)[1] for d in range(1, NY)]
        + [at_z(y, z, e, d)[1] for d in (1, -1)]
        + [at_e(y, z, e, d)[1] for d in range(1, NE)]
    )
    right = at_z(y, z, e, 1)[1]
    left = at_z(y, z, e, -1)[1]

    token_copies = []
    for d in range(1, NE):
        peer, dev = at_e(y, z, e, d)
        token_copies.append(remote(rows.at[peer], rows_own.at[e], e_send, e_recv, d - 1, dev))
    for c in token_copies:
        c.start()
    own_rows = pltpu.make_async_copy(rows.at[e], rows_own.at[e], local_sem.at[0])
    own_rows.start()

    def y_exchange(src, dst_of, width, base):
        copies = []
        for d in range(1, NY):
            peer, dev = at_y(y, z, e, d)
            copies.append(
                remote(src.at[:, columns(peer, width)], dst_of(y), y_send, y_recv, base + d - 1, dev)
            )
        for c in copies:
            c.start()
        return copies

    k_copies = y_exchange(k, lambda s: k_all.at[s, z], HEAD_SIZE, 0)
    v_copies = y_exchange(v, lambda s: v_all.at[s, z], HEAD_SIZE, 3)
    own = [
        pltpu.make_async_copy(k.at[:, columns(y, HEAD_SIZE)], k_all.at[y, z], local_sem.at[1]),
        pltpu.make_async_copy(v.at[:, columns(y, HEAD_SIZE)], v_all.at[y, z], local_sem.at[2]),
    ]
    for c in own:
        c.start()

    weights = ((wg, wg_all), (wu, wu_all), (wd, wd_all))
    ring = []

    def ring_step(index, step, source, target):
        pair = []
        c = remote(
            source(step, 1), target(lax.rem(z - step + NZ, NZ)), r_send, r_recv, index * 4 + step, right
        )
        c.start()
        pair.append(c)
        if step < 3:
            c = remote(
                source(step, -1), target(lax.rem(z + step, NZ)), l_send, l_recv, index * 3 + step, left
            )
            c.start()
            pair.append(c)
        return pair

    held = {}
    for index, (part, whole) in enumerate(weights):
        held[index] = ring_step(index, 0, lambda s, w, p=part: p, lambda b, a=whole: a.at[b])
        ring += held[index]
    for c in k_copies + v_copies:
        c.wait_recv()
    for c in own:
        c.wait()
    for index, whole in ((3, k_all), (4, v_all)):
        held[index] = ring_step(index, 0, lambda s, w, a=whole: a.at[:, z], lambda b, a=whole: a.at[:, b])
        ring += held[index]

    q_copies = y_exchange(q, lambda s: q_all.at[s], GW, 6)
    do_copies = y_exchange(do, lambda s: do_all.at[s], GW, 9)
    late = [
        pltpu.make_async_copy(q.at[:, columns(y, GW)], q_all.at[y], local_sem.at[3]),
        pltpu.make_async_copy(do.at[:, columns(y, GW)], do_all.at[y], local_sem.at[4]),
        pltpu.make_async_copy(wg, wg_all.at[z], local_sem.at[5]),
        pltpu.make_async_copy(wu, wu_all.at[z], local_sem.at[6]),
        pltpu.make_async_copy(wd, wd_all.at[z], local_sem.at[7]),
    ]
    for c in late:
        c.start()

    for c in token_copies:
        c.wait_recv()
    own_rows.wait()
    xc_copies = []
    for d in range(1, NY):
        peer, dev = at_y(y, z, e, d)
        xc_copies.append(
            remote(rows_own.at[:, :, columns(peer, DS)], xc.at[y], x_send, x_recv, d - 1, dev)
        )
    for c in xc_copies:
        c.start()
    own_xc = pltpu.make_async_copy(rows_own.at[:, :, columns(y, DS)], xc.at[y], local_sem.at[8])
    own_xc.start()

    targets = (
        lambda b: wg_all.at[b],
        lambda b: wu_all.at[b],
        lambda b: wd_all.at[b],
        lambda b: k_all.at[:, b],
        lambda b: v_all.at[:, b],
    )
    for step in range(1, 4):
        for index in range(5):
            for c in held[index]:
                c.wait_recv()
            t = targets[index]

            def source(s, way, t=t):
                return t(lax.rem(z - s + NZ, NZ)) if way == 1 else t(lax.rem(z + s, NZ))

            held[index] = ring_step(index, step, source, t)
            ring += held[index]
    for index in range(5):
        for c in held[index]:
            c.wait_recv()
    for c in xc_copies + q_copies + do_copies:
        c.wait_recv()
    for c in late + [own_xc]:
        c.wait()
    for c in token_copies + k_copies + v_copies + q_copies + do_copies + xc_copies + ring:
        c.wait_send()


def inbound(q, do, k, v, rows, wg, wu, wd):
    sd = jax.ShapeDtypeStruct
    any_spec = pl.BlockSpec(memory_space=pl.ANY)
    dma = pltpu.SemaphoreType.DMA
    return pl.pallas_call(
        inbound_kernel,
        out_shape=[
            sd((NY, TOK, GW), BF),
            sd((NY, TOK, GW), BF),
            sd((NY, NZ, TOK, HEAD_SIZE), BF),
            sd((NY, NZ, TOK, HEAD_SIZE), BF),
            sd((NE, 16, D + 128), BF),
            sd((NY, NE, 16, DS), BF),
            sd((NZ, WD, FF), BF),
            sd((NZ, WD, FF), BF),
            sd((NZ, WD, FF), BF),
        ],
        in_specs=[any_spec] * 8,
        out_specs=[any_spec] * 9,
        scratch_shapes=[
            dma((9,)), dma((12,)), dma((12,)), dma((7,)), dma((7,)), dma((3,)), dma((3,)),
            dma((20,)), dma((20,)), dma((15,)), dma((15,)),
        ],
        compiler_params=pltpu.CompilerParams(
            collective_id=0, has_side_effects=True, vmem_limit_bytes=VMEM_MOST
        ),
        name="inbound",
    )(q, do, k, v, rows, wg, wu, wd)


def dot(a, b, left, right):
    return lax.dot_general(a, b, (((left,), (right,)), ((), ())), preferred_element_type=F32)


def experts_kernel(
    xc, wg, wu, wd, weight, rb, gg, gu, gd, route_home,
    part, parts, act, route, sem, s_send, s_recv, a_send, a_recv, e_send, e_recv,
):
    y, z, e = places()
    greet(
        [at_y(y, z, e, d)[1] for d in range(1, NY)] + [at_e(y, z, e, d)[1] for d in range(1, NE)]
    )
    both = xc[...].astype(F32)
    count = NY * NE * CAP
    x = both[:, :, :CAP, :].reshape(count, DS)
    c = both[:, :, CAP:, :].reshape(count, DS)
    for index, (rows, w) in enumerate(((x, wg), (x, wu), (c, wd))):
        product = dot(rows.astype(BF), w[...], 1, 0)
        part[:, :, index * FF : (index + 1) * FF] = product.reshape(NY, NE * CAP, FF).astype(BF)
    swaps = []
    for d in range(1, NY):
        peer, dev = at_y(y, z, e, d)
        swaps.append(remote(part.at[peer], parts.at[d - 1], s_send, s_recv, d - 1, dev))
    for copy in swaps:
        copy.start()
    x_t = x.T.astype(BF)
    c_t = c.T.astype(BF)
    for copy in swaps:
        copy.wait_recv()
    sums = part[y].astype(F32)
    for d in range(NY - 1):
        sums = sums + parts[d].astype(F32)
    gate_act = sums[:, :FF]
    up_act = sums[:, FF : 2 * FF]
    cot_down = sums[:, 2 * FF :]
    w = weight[...]
    sigma = 1.0 / (1.0 + jnp.exp(-gate_act))
    silu = gate_act * sigma
    hidden = (silu * up_act).astype(BF).astype(F32)
    hidden_grad = w * cot_down
    act[y, :, :FF] = (hidden_grad * up_act * sigma * (1.0 + gate_act * (1.0 - sigma))).astype(BF)
    act[y, :, FF : 2 * FF] = (hidden_grad * silu).astype(BF)
    act[y, :, 2 * FF :] = (w * hidden).astype(BF)
    spreads = []
    for d in range(1, NY):
        spreads.append(remote(act.at[y], act.at[y], a_send, a_recv, d - 1, at_y(y, z, e, d)[1]))
    for copy in spreads:
        copy.start()
    values = jnp.sum(hidden * cot_down, axis=1, keepdims=True)
    route[...] = jnp.broadcast_to(values, (NE * CAP, 128)).reshape(NE, CAP, 128)
    routes = []
    for d in range(1, NE):
        peer, dev = at_e(y, z, e, d)
        routes.append(remote(route.at[peer], route_home.at[e], e_send, e_recv, d - 1, dev))
    for copy in routes:
        copy.start()
    own = pltpu.make_async_copy(route.at[e], route_home.at[e], sem.at[0])
    own.start()
    for copy in spreads:
        copy.wait_recv()
    act_all = act[...].reshape(count, 3 * FF)
    gate_pre = act_all[:, :FF]
    up_pre = act_all[:, FF : 2 * FF]
    row_grad = dot(gate_pre, wg[...], 1, 1) + dot(up_pre, wu[...], 1, 1)
    row_grad = row_grad.reshape(NY, NE, CAP, DS)
    rb[...] = jnp.concatenate(
        [row_grad[:, :, :, i * 128 : (i + 1) * 128] for i in range(DS // 128)], axis=2
    ).astype(BF)
    gg[...] = dot(x_t, gate_pre, 1, 0).astype(BF)
    gu[...] = dot(x_t, up_pre, 1, 0).astype(BF)
    gd[...] = dot(c_t, act_all[:, 2 * FF :], 1, 0).astype(BF)
    own.wait()
    for copy in routes:
        copy.wait()
    for copy in swaps + spreads:
        copy.wait_send()


def experts(xc, wg, wu, wd, weight):
    sd = jax.ShapeDtypeStruct
    vmem = pl.BlockSpec(memory_space=pltpu.VMEM)
    dma = pltpu.SemaphoreType.DMA
    rows = NE * CAP
    return pl.pallas_call(
        experts_kernel,
        out_shape=[
            sd((NY, NE, 32, 128), BF),
            sd((DS, FF), BF),
            sd((DS, FF), BF),
            sd((DS, FF), BF),
            sd((NE, CAP, 128), F32),
        ],
        in_specs=[vmem] * 5,
        out_specs=[vmem] * 5,
        scratch_shapes=[
            pltpu.VMEM((NY, rows, 3 * FF), BF),
            pltpu.VMEM((NY - 1, rows, 3 * FF), BF),
            pltpu.VMEM((NY, rows, 3 * FF), BF),
            pltpu.VMEM((NE, CAP, 128), F32),
            dma((1,)), dma((3,)), dma((3,)), dma((3,)), dma((3,)), dma((7,)), dma((7,)),
        ],
        compiler_params=pltpu.CompilerParams(
            collective_id=1, has_side_effects=True, vmem_limit_bytes=VMEM_MOST
        ),
        name="experts",
    )(xc, wg, wu, wd, weight)


def outbound_kernel(
    dq, rb, dk, dv, gg, gu, gd, dispatch,
    dq_home, dk_home, dv_home, gg_out, gu_out, gd_out, input_grad,
    back, rbuf, k_right, k_left, v_right, v_left, g_right, g_left, u_right, u_left, d_right, d_left,
    k_sum, v_sum,
    local_sem, q_send, q_recv, b_send, b_recv, e_send, e_recv, h_send, h_recv,
    r_send, r_recv, l_send, l_recv,
):
    y, z, e = places()
    greet(
        [at_y(y, z, e, d)[1] for d in range(1, NY)]
        + [at_z(y, z, e, d)[1] for d in (1, -1)]
        + [at_e(y, z, e, d)[1] for d in range(1, NE)]
    )
    right = at_z(y, z, e, 1)[1]
    left = at_z(y, z, e, -1)[1]

    arrays = (
        (lambda b: gg.at[b], g_right, g_left),
        (lambda b: gu.at[b], u_right, u_left),
        (lambda b: gd.at[b], d_right, d_left),
        (lambda b: dk.at[:, b], k_right, k_left),
        (lambda b: dv.at[:, b], v_right, v_left),
    )
    held = {}
    ring = []
    for index, (part, to_right, to_left) in enumerate(arrays):
        a = remote(
            part(lax.rem(z + 4, NZ)), to_right.at[0], r_send, r_recv, index * 4, right
        )
        b = remote(
            part(lax.rem(z + NZ - 3, NZ)), to_left.at[0], l_send, l_recv, index * 3, left
        )
        a.start()
        b.start()
        held[index] = (a, b)
        ring += [a, b]

    rb_copies = []
    q_copies = []
    for d in range(1, NY):
        peer, dev = at_y(y, z, e, d)
        rb_copies.append(remote(rb.at[peer], rbuf.at[y], b_send, b_recv, d - 1, dev))
        q_copies.append(
            remote(dq.at[peer], dq_home.at[:, columns(y, GW)], q_send, q_recv, d - 1, dev)
        )
    for c in rb_copies + q_copies:
        c.start()
    own_rb = pltpu.make_async_copy(rb.at[y], rbuf.at[y], local_sem.at[0])
    own_q = pltpu.make_async_copy(dq.at[y], dq_home.at[:, columns(y, GW)], local_sem.at[1])
    own_rb.start()
    own_q.start()

    own_rb.wait()
    for c in rb_copies:
        c.wait_recv()
    e_copies = []
    for d in range(1, NE):
        peer, dev = at_e(y, z, e, d)
        e_copies.append(remote(rbuf.at[:, peer], back.at[e], e_send, e_recv, d - 1, dev))
    for c in e_copies:
        c.start()
    own_back = pltpu.make_async_copy(rbuf.at[:, e], back.at[e], local_sem.at[2])
    own_back.start()

    for step in range(1, 4):
        for index, (part, to_right, to_left) in enumerate(arrays):
            a, b = held[index]
            a.wait_recv()
            got = to_right.at[step - 1]
            got[...] = (
                got[...].astype(F32) + part(lax.rem(z + 4 - step, NZ))[...].astype(F32)
            ).astype(BF)
            a = remote(got, to_right.at[step], r_send, r_recv, index * 4 + step, right)
            a.start()
            ring.append(a)
            if step < 3:
                b.wait_recv()
                got = to_left.at[step - 1]
                got[...] = (
                    got[...].astype(F32) + part(lax.rem(z + NZ - 3 + step, NZ))[...].astype(F32)
                ).astype(BF)
                b = remote(got, to_left.at[step], l_send, l_recv, index * 3 + step, left)
                b.start()
                ring.append(b)
            held[index] = (a, b)

    own_back.wait()
    for c in e_copies:
        c.wait_recv()
    pieces = back[...].astype(F32).reshape(NE, NY, DS // 128, CAP, 128)
    for block in range(NY):
        for i in range(DS // 128):
            piece = pieces[:, block, i].reshape(NE * CAP, 128).astype(BF)
            start = block * DS + i * 128
            input_grad[:, start : start + 128] = dot(dispatch[...], piece, 1, 0).astype(BF)

    home = []
    for index in (3, 4, 0, 1, 2):
        part, to_right, to_left = arrays[index]
        a, b = held[index]
        a.wait_recv()
        b.wait_recv()
        total = (
            part(z)[...].astype(F32) + to_right[3].astype(F32) + to_left[2].astype(F32)
        ).astype(BF)
        if index < 3:
            (gg_out, gu_out, gd_out)[index][...] = total
        else:
            mine = (k_sum, v_sum)[index - 3]
            out = (dk_home, dv_home)[index - 3]
            mine[...] = total
            for d in range(1, NY):
                peer, dev = at_y(y, z, e, d)
                c = remote(
                    mine.at[peer], out.at[:, columns(y, HEAD_SIZE)], h_send, h_recv,
                    (index - 3) * 3 + d - 1, dev,
                )
                c.start()
                home.append(c)
            c = pltpu.make_async_copy(
                mine.at[y], out.at[:, columns(y, HEAD_SIZE)], local_sem.at[index]
            )
            c.start()
            home.append(c)
    for c in home:
        c.wait()
    own_q.wait()
    for c in q_copies:
        c.wait()
    for c in rb_copies + e_copies + ring:
        c.wait_send()


def outbound(dq, rb, dk, dv, gg, gu, gd, dispatch):
    sd = jax.ShapeDtypeStruct
    any_spec = pl.BlockSpec(memory_space=pl.ANY)
    vmem = pl.BlockSpec(memory_space=pltpu.VMEM)
    dma = pltpu.SemaphoreType.DMA
    kv = (NY, TOK, HEAD_SIZE)
    rings = []
    for shape in (kv, kv, (WD, FF), (WD, FF), (WD, FF)):
        rings += [pltpu.VMEM((4,) + shape, BF), pltpu.VMEM((3,) + shape, BF)]
    return pl.pallas_call(
        outbound_kernel,
        out_shape=[
            sd((TOK, QUERY_HEADS * HEAD_SIZE), BF),
            sd((TOK, KEY_VALUE_HEADS * HEAD_SIZE), BF),
            sd((TOK, KEY_VALUE_HEADS * HEAD_SIZE), BF),
            sd((WD, FF), BF),
            sd((WD, FF), BF),
            sd((WD, FF), BF),
            sd((TOK, D), BF),
        ],
        in_specs=[any_spec] * 2 + [vmem] * 6,
        out_specs=[any_spec] * 3 + [vmem] * 4,
        scratch_shapes=[pltpu.VMEM((NE, NY, 32, 128), BF), pltpu.VMEM((NY, NE, 32, 128), BF)]
        + rings
        + [
            pltpu.VMEM(kv, BF), pltpu.VMEM(kv, BF),
            dma((5,)), dma((3,)), dma((3,)), dma((3,)), dma((3,)), dma((7,)), dma((7,)),
            dma((6,)), dma((6,)), dma((20,)), dma((20,)), dma((15,)), dma((15,)),
        ],
        compiler_params=pltpu.CompilerParams(
            collective_id=3, has_side_effects=True, vmem_limit_bytes=VMEM_MOST
        ),
        name="outbound",
    )(dq, rb, dk, dv, gg, gu, gd, dispatch)


def attention_kernel(
    z_ref, q_ref, do_ref, k_ref, v_ref, kt_ref, dq_ref, dk_ref, dv_ref,
    q_st, do_st, s_scr, g_scr, dk_acc, dv_acc, dqt,
):
    block = pl.program_id(0)
    part = pl.program_id(1)
    z = z_ref[0]
    position = block * NZ + z
    chunks = lax.div(position * TOK + TOK + KC - 1, KC)
    scale = 1.0 / math.sqrt(HEAD_SIZE)
    factor = scale * math.log2(math.e)

    @pl.when((block == 0) & (part == 0))
    def _():
        dk_acc[...] = jnp.zeros_like(dk_acc)
        dv_acc[...] = jnp.zeros_like(dv_acc)

    for h in range(HALF):
        q_st[h * TOK : (h + 1) * TOK, :] = q_ref[0, :, h * HEAD_SIZE : (h + 1) * HEAD_SIZE]
        do_st[h * TOK : (h + 1) * TOK, :] = do_ref[0, :, h * HEAD_SIZE : (h + 1) * HEAD_SIZE]

    def at(c):
        return pl.ds(pl.multiple_of(c * KC, KC), KC)

    nt = (((1,), (1,)), ((), ()))
    nn = (((1,), (0,)), ((), ()))

    def fold(values, op):
        return op(values.reshape(KC // 8, 8, ROWS), axis=0)

    def scores(c, peak, masked):
        s = lax.dot_general(k_ref[at(c), :], q_st[...], nt, preferred_element_type=F32) * factor
        if masked:
            key_pos = c * KC + lax.broadcasted_iota(jnp.int32, (KC, ROWS), 0)
            query_pos = position * TOK + lax.rem(
                lax.broadcasted_iota(jnp.int32, (KC, ROWS), 1), TOK
            )
            s = jnp.where(key_pos <= query_pos, s, -1e30)
        s_scr[at(c), :] = s
        return jnp.maximum(peak, fold(s, jnp.max))

    peak = lax.fori_loop(
        0, chunks - 1, lambda c, m: scores(c, m, False), jnp.full((8, ROWS), -1e30, F32)
    )
    peak = scores(chunks - 1, peak, True)
    peak = jnp.max(peak, axis=0, keepdims=True)

    def weigh(c, carry):
        total, dot = carry
        p = jnp.exp2(s_scr[at(c), :] - peak)
        g = lax.dot_general(v_ref[at(c), :], do_st[...], nt, preferred_element_type=F32)
        s_scr[at(c), :] = p
        g_scr[at(c), :] = g
        return total + fold(p, jnp.sum), dot + fold(p * g, jnp.sum)

    zero = jnp.zeros((8, ROWS), F32)
    total, dot = lax.fori_loop(0, chunks, weigh, (zero, zero))
    inverse = 1.0 / jnp.sum(total, axis=0, keepdims=True)
    row_dot = jnp.sum(dot, axis=0, keepdims=True) * inverse

    dqt[...] = jnp.zeros_like(dqt)

    def gradients(c, carry):
        p = s_scr[at(c), :] * inverse
        ds = (p * (g_scr[at(c), :] - row_dot)).astype(BF)
        dv_acc[at(c), :] += lax.dot_general(
            p.astype(BF), do_st[...], nn, preferred_element_type=F32
        )
        dk_acc[at(c), :] += lax.dot_general(ds, q_st[...], nn, preferred_element_type=F32)
        dqt[...] += lax.dot_general(kt_ref[:, at(c)], ds, nn, preferred_element_type=F32)
        return carry

    lax.fori_loop(0, chunks, gradients, 0)
    for h in range(HALF):
        dq_ref[0, :, h * HEAD_SIZE : (h + 1) * HEAD_SIZE] = (
            (dqt[:, h * TOK : (h + 1) * TOK] * scale).T.astype(BF)
        )

    @pl.when((block == NY - 1) & (part == pl.num_programs(1) - 1))
    def _():
        dk_ref[...] = (dk_acc[...] * scale).astype(BF)
        dv_ref[...] = dv_acc[...].astype(BF)


def attention(z, q_all, do_all, k_all, v_all):
    tokens = k_all.shape[0]
    width = HALF * HEAD_SIZE
    whole = pl.BlockSpec(memory_space=pltpu.VMEM)
    rows = pl.BlockSpec((1, TOK, width), lambda b, p: (b, 0, p))
    sd = jax.ShapeDtypeStruct
    return pl.pallas_call(
        attention_kernel,
        grid=(NY, GW // width),
        out_shape=[
            sd((NY, TOK, GW), BF),
            sd((tokens, HEAD_SIZE), BF),
            sd((tokens, HEAD_SIZE), BF),
        ],
        in_specs=[pl.BlockSpec(memory_space=pltpu.SMEM), rows, rows, whole, whole, whole],
        out_specs=[rows, whole, whole],
        scratch_shapes=[
            pltpu.VMEM((ROWS, HEAD_SIZE), BF),
            pltpu.VMEM((ROWS, HEAD_SIZE), BF),
            pltpu.VMEM((tokens, ROWS), F32),
            pltpu.VMEM((tokens, ROWS), F32),
            pltpu.VMEM((tokens, HEAD_SIZE), F32),
            pltpu.VMEM((tokens, HEAD_SIZE), F32),
            pltpu.VMEM((HEAD_SIZE, ROWS), F32),
        ],
        compiler_params=pltpu.CompilerParams(
            dimension_semantics=("arbitrary", "arbitrary"), vmem_limit_bytes=48 * 1024 * 1024
        ),
        name="attention",
    )(z, q_all, do_all, k_all, v_all, k_all.T)


def per_device(
    query_rows,
    key_matrix_all,
    value_matrix_all,
    context_grad,
    mixture_input,
    mixture_grad,
    expert_ids,
    route_weight,
    gate_weight,
    up_weight,
    down_weight,
):
    y, z, e = places()
    per_owner = EXPERTS // NE
    tokens = mixture_input[0]
    cotangent = mixture_grad[0]
    routes = expert_ids[0]
    in_window = routes % per_owner == 0
    route_owner = (
        in_window[:, :, None]
        & ((routes // per_owner)[:, :, None] == jnp.arange(NE)[None, None, :])
    ).astype(F32)
    token_owner = jnp.sum(route_owner, axis=1)
    earlier = (jnp.arange(TOK)[:, None] > jnp.arange(TOK)[None, :]).astype(BF)
    slot_index = jnp.dot(earlier, token_owner.astype(BF), preferred_element_type=F32)
    placement = token_owner[:, :, None] * (
        slot_index[:, :, None] == jnp.arange(CAP, dtype=F32)[None, None, :]
    ).astype(F32)
    dispatch = placement.reshape(TOK, NE * CAP).astype(BF)
    weight_owner = jnp.sum(route_owner * route_weight[0].astype(F32)[:, :, None], axis=1)
    slot_weight = jnp.sum(placement * weight_owner[:, :, None], axis=0).astype(BF)
    x_rows = jnp.einsum("tr,td->rd", dispatch, tokens, preferred_element_type=F32).astype(BF)
    c_rows = jnp.einsum("tr,td->rd", dispatch, cotangent, preferred_element_type=F32).astype(BF)
    rows = jnp.concatenate(
        (x_rows.reshape(NE, CAP, D), c_rows.reshape(NE, CAP, D)), axis=1
    )
    weight_cols = jnp.broadcast_to(
        jnp.concatenate((slot_weight, slot_weight), axis=1)[:, :, None], (NE, 2 * CAP, 128)
    )
    rows = jnp.concatenate((rows, weight_cols), axis=2)

    q_all, do_all, k_all, v_all, rows_own, xc, wg_all, wu_all, wd_all = inbound(
        query_rows[0], context_grad[0], key_matrix_all[0], value_matrix_all[0], rows,
        gate_weight[0], up_weight[0], down_weight[0],
    )
    weight = rows_own[:, :CAP, D].reshape(NE * CAP, 1).astype(F32)
    rb, gg, gu, gd, route_home = experts(
        xc, wg_all.reshape(DS, FF), wu_all.reshape(DS, FF), wd_all.reshape(DS, FF), weight
    )
    length = NY * NZ * TOK
    dq, dk, dv = attention(
        z.reshape(1).astype(jnp.int32),
        q_all,
        do_all,
        k_all.reshape(length, HEAD_SIZE),
        v_all.reshape(length, HEAD_SIZE),
    )
    kv_blocks = (NY, NZ, TOK, HEAD_SIZE)
    blocks = (NZ, WD, FF)
    dq_home, dk_home, dv_home, gate_grad, up_grad, down_grad, input_grad = outbound(
        dq, rb, dk.reshape(kv_blocks), dv.reshape(kv_blocks),
        gg.reshape(blocks), gu.reshape(blocks), gd.reshape(blocks), dispatch,
    )
    back_route = route_home[:, :, 0].astype(BF).astype(F32)
    route_token = jnp.sum(placement * back_route[None], axis=2)
    route_grad = jnp.sum(route_owner * route_token[:, None, :], axis=2).astype(BF)
    return (
        dq_home[None],
        dk_home[None],
        dv_home[None],
        input_grad[None],
        route_grad[None],
        gate_grad[None],
        up_grad[None],
        down_grad[None],
    )


def solution(mesh):
    spec = P("exp", "ctx", None)
    return jax.shard_map(
        per_device,
        mesh=mesh,
        in_specs=(spec,) * 11,
        out_specs=(spec,) * 8,
        check_vma=False,
    )
```

```python
import math

import jax
import jax.numpy as jnp
from jax import lax
from jax.experimental import pallas as pl
from jax.experimental.pallas import tpu as pltpu
from jax.sharding import PartitionSpec as P

D = 2048
QUERY_HEADS = 32
KEY_VALUE_HEADS = 4
HEAD_SIZE = 128
FF = 768
EXPERTS = 128
TOPK = 8
CAP = 8
NY = 4
NZ = 8
NE = 8
TOK = 128
GW = QUERY_HEADS // KEY_VALUE_HEADS * HEAD_SIZE
DS = D // NY
WD = D // (NY * NZ)
KC = 512
HALF = 4
ROWS = HALF * TOK
EVENTS = (1, 2, 3, 4, 5, 6)
MESH = pl.DeviceIdType.MESH
VMEM_MOST = 60 * 1024 * 1024
BF = jnp.bfloat16
F32 = jnp.float32


def places():
    ctx = lax.axis_index("ctx")
    return lax.div(ctx, NZ), lax.rem(ctx, NZ), lax.axis_index("exp")


def at_y(y, z, e, shift):
    peer = lax.rem(y + shift, NY)
    return peer, (peer * NZ + z, e)


def at_z(y, z, e, shift):
    peer = lax.rem(z + shift + NZ, NZ)
    return peer, (y * NZ + peer, e)


def at_e(y, z, e, shift):
    peer = lax.rem(e + shift, NE)
    return peer, (y * NZ + z, peer)


def greet(peers):
    barrier = pltpu.get_barrier_semaphore()
    for peer in peers:
        pl.semaphore_signal(barrier, inc=1, device_id=peer, device_id_type=MESH)
    pl.semaphore_wait(barrier, len(peers))


def remote(src, dst, send, recv, index, peer):
    return pltpu.make_async_remote_copy(
        src_ref=src,
        dst_ref=dst,
        send_sem=send.at[index],
        recv_sem=recv.at[index],
        device_id=peer,
        device_id_type=MESH,
    )


def columns(index, width):
    return pl.ds(pl.multiple_of(index * width, width), width)


def dot(a, b, left, right):
    return lax.dot_general(a, b, (((left,), (right,)), ((), ())), preferred_element_type=F32)


def layer_kernel(
    q, do, k, v, rows, wg, wu, wd, dispatch,
    dq_home, dk_home, dv_home, gg_out, gu_out, gd_out, input_grad, route_home,
    q_all, do_all, k_all, v_all, kt, q_st, do_st, s_scr, g_scr, dk_acc, dv_acc, dqt, dq,
    rows_own, xc, x_t, c_t, wg_all, wu_all, wd_all, part, parts, act, route,
    rb, rbuf, back, gg, gu, gd,
    k_right, k_left, v_right, v_left, g_right, g_left, u_right, u_left, d_right, d_left,
    k_first, v_first, k_sum, v_sum,
    local_sem, y_send, y_recv, e_send, e_recv, x_send, x_recv, r_send, r_recv, l_send, l_recv,
    s_send, s_recv, a_send, a_recv, t_send, t_recv, q_send, q_recv, b_send, b_recv,
    i_send, i_recv, h_send, h_recv, gr_send, gr_recv, gl_send, gl_recv,
):
    y, z, e = places()
    count = NY * NE * CAP
    scale = 1.0 / math.sqrt(HEAD_SIZE)
    factor = scale * math.log2(math.e)
    greet(
        [at_y(y, z, e, d)[1] for d in range(1, NY)]
        + [at_z(y, z, e, d)[1] for d in (1, -1)]
        + [at_e(y, z, e, d)[1] for d in range(1, NE)]
    )
    right = at_z(y, z, e, 1)[1]
    left = at_z(y, z, e, -1)[1]

    def tokens():
        return [
            remote(rows.at[at_e(y, z, e, d)[0]], rows_own.at[e], e_send, e_recv, d - 1,
                   at_e(y, z, e, d)[1])
            for d in range(1, NE)
        ]

    def slices():
        return [
            remote(rows_own.at[:, :, columns(at_y(y, z, e, d)[0], DS)], xc.at[y], x_send, x_recv,
                   d - 1, at_y(y, z, e, d)[1])
            for d in range(1, NY)
        ]

    def y_exchange(src, target, width, base):
        return [
            remote(src.at[:, columns(at_y(y, z, e, d)[0], width)], target, y_send, y_recv,
                   base + d - 1, at_y(y, z, e, d)[1])
            for d in range(1, NY)
        ]

    def kv_exchange():
        return y_exchange(k, k_all.at[y, z], HEAD_SIZE, 0) + y_exchange(
            v, v_all.at[y, z], HEAD_SIZE, 3
        )

    def q_exchange():
        return y_exchange(q, q_all.at[y], GW, 6) + y_exchange(do, do_all.at[y], GW, 9)

    gathered = (
        lambda b: wg_all.at[b],
        lambda b: wu_all.at[b],
        lambda b: wd_all.at[b],
        lambda b: k_all.at[:, b],
        lambda b: v_all.at[:, b],
    )

    def gather(index, step):
        block = gathered[index]
        here = block(lax.rem(z - step + NZ, NZ))
        pair = [remote(here, here, r_send, r_recv, index * 4 + step, right)]
        if step < 3:
            there = block(lax.rem(z + step, NZ))
            pair.append(remote(there, there, l_send, l_recv, index * 3 + step, left))
        return pair

    def gather_step(indices, step):
        for index in indices:
            if step > 0:
                for c in gather(index, step - 1):
                    c.wait_recv()
            if step < 4:
                for c in gather(index, step):
                    c.start()

    def here(src, dst, index):
        return pltpu.make_async_copy(src, dst, local_sem.at[index])

    for c in tokens() + kv_exchange():
        c.start()
    own = [
        here(rows.at[e], rows_own.at[e], 0),
        here(k.at[:, columns(y, HEAD_SIZE)], k_all.at[y, z], 1),
        here(v.at[:, columns(y, HEAD_SIZE)], v_all.at[y, z], 2),
        here(q.at[:, columns(y, GW)], q_all.at[y], 3),
        here(do.at[:, columns(y, GW)], do_all.at[y], 4),
        here(wg, wg_all.at[z], 5),
        here(wu, wu_all.at[z], 6),
        here(wd, wd_all.at[z], 7),
    ]
    for c in own:
        c.start()
    for c in q_exchange():
        c.start()
    for c in kv_exchange():
        c.wait_recv()
    for c in own:
        c.wait()
    gather_step((3, 4), 0)
    for c in tokens():
        c.wait_recv()
    for c in slices():
        c.start()
    own_xc = here(rows_own.at[:, :, columns(y, DS)], xc.at[y], 8)
    own_xc.start()
    dk_acc[...] = jnp.zeros_like(dk_acc)
    dv_acc[...] = jnp.zeros_like(dv_acc)
    for step in range(1, 4):
        gather_step((3, 4), step)
    gather_step((0, 1, 2), 0)
    own_xc.wait()
    for c in slices():
        c.wait_recv()
    both = xc[...].astype(F32)
    x_t[...] = both[:, :, :CAP, :].reshape(count, DS).T.astype(BF)
    c_t[...] = both[:, :, CAP:, :].reshape(count, DS).T.astype(BF)
    gather_step((3, 4), 4)
    for c in q_exchange():
        c.wait_recv()

    def chunk(c):
        return lax.div(c, 2), pl.ds(lax.rem(c, 2) * (KC // TOK), KC // TOK)

    def chunk_rows(ref, c):
        a, b = chunk(c)
        return ref[a, b].reshape(KC, HEAD_SIZE)

    def at(c):
        return pl.ds(pl.multiple_of(c * KC, KC), KC)

    def turn(c, carry):
        kt[:, at(c)] = chunk_rows(k_all, c).astype(F32).T.astype(BF)
        return carry

    lax.fori_loop(0, NY * NZ * TOK // KC, turn, 0)

    def fold(values, op):
        return op(values.reshape(KC // 8, 8, ROWS), axis=0)

    def attend(block, half):
        position = block * NZ + z
        chunks = lax.div(position * TOK + TOK + KC - 1, KC)
        for h in range(HALF):
            cols = pl.ds(
                pl.multiple_of(half * (HALF * HEAD_SIZE) + h * HEAD_SIZE, HEAD_SIZE), HEAD_SIZE
            )
            q_st[h * TOK : (h + 1) * TOK, :] = q_all[block, :, cols]
            do_st[h * TOK : (h + 1) * TOK, :] = do_all[block, :, cols]

        def scores(c, peak, masked):
            s = dot(chunk_rows(k_all, c), q_st[...], 1, 1) * factor
            if masked:
                key_pos = c * KC + lax.broadcasted_iota(jnp.int32, (KC, ROWS), 0)
                query_pos = position * TOK + lax.rem(
                    lax.broadcasted_iota(jnp.int32, (KC, ROWS), 1), TOK
                )
                s = jnp.where(key_pos <= query_pos, s, -1e30)
            s_scr[at(c), :] = s
            return jnp.maximum(peak, fold(s, jnp.max))

        peak = lax.fori_loop(
            0, chunks - 1, lambda c, m: scores(c, m, False), jnp.full((8, ROWS), -1e30, F32)
        )
        peak = scores(chunks - 1, peak, True)
        peak = jnp.max(peak, axis=0, keepdims=True)

        def weigh(c, carry):
            total, paired = carry
            p = jnp.exp2(s_scr[at(c), :] - peak)
            g = dot(chunk_rows(v_all, c), do_st[...], 1, 1)
            s_scr[at(c), :] = p
            g_scr[at(c), :] = g
            return total + fold(p, jnp.sum), paired + fold(p * g, jnp.sum)

        zero = jnp.zeros((8, ROWS), F32)
        total, paired = lax.fori_loop(0, chunks, weigh, (zero, zero))
        inverse = 1.0 / jnp.sum(total, axis=0, keepdims=True)
        row_dot = jnp.sum(paired, axis=0, keepdims=True) * inverse

        dqt[...] = jnp.zeros_like(dqt)

        def gradients(c, carry):
            a, b = chunk(c)
            p = s_scr[at(c), :] * inverse
            ds = (p * (g_scr[at(c), :] - row_dot)).astype(BF)
            shape = (KC // TOK, TOK, HEAD_SIZE)
            dv_acc[a, b] += dot(p.astype(BF), do_st[...], 1, 0).reshape(shape)
            dk_acc[a, b] += dot(ds, q_st[...], 1, 0).reshape(shape)
            dqt[...] += dot(kt[:, at(c)], ds, 1, 0)
            return carry

        lax.fori_loop(0, chunks, gradients, 0)
        for h in range(HALF):
            cols = pl.ds(
                pl.multiple_of(half * (HALF * HEAD_SIZE) + h * HEAD_SIZE, HEAD_SIZE), HEAD_SIZE
            )
            dq[block, :, cols] = (dqt[:, h * TOK : (h + 1) * TOK] * scale).T.astype(BF)

    def swaps():
        return [
            remote(part.at[at_y(y, z, e, d)[0]], parts.at[d - 1], s_send, s_recv, d - 1,
                   at_y(y, z, e, d)[1])
            for d in range(1, NY)
        ]

    def spreads():
        return [
            remote(act.at[y], act.at[y], a_send, a_recv, d - 1, at_y(y, z, e, d)[1])
            for d in range(1, NY)
        ]

    def routes():
        return [
            remote(route.at[at_e(y, z, e, d)[0]], route_home.at[e], t_send, t_recv, d - 1,
                   at_e(y, z, e, d)[1])
            for d in range(1, NE)
        ]

    def row_swaps():
        return [
            remote(rb.at[at_y(y, z, e, d)[0]], rbuf.at[y], b_send, b_recv, d - 1,
                   at_y(y, z, e, d)[1])
            for d in range(1, NY)
        ]

    summed = (
        (lambda b: gg[b].astype(F32), g_right, g_left, gg_out),
        (lambda b: gu[b].astype(F32), u_right, u_left, gu_out),
        (lambda b: gd[b].astype(F32), d_right, d_left, gd_out),
        (lambda b: dk_acc[:, b] * scale, k_right, k_left, k_sum),
        (lambda b: dv_acc[:, b], v_right, v_left, v_sum),
    )
    first = (
        lambda way: gg.at[lax.rem(z + (4, NZ - 3)[way], NZ)],
        lambda way: gu.at[lax.rem(z + (4, NZ - 3)[way], NZ)],
        lambda way: gd.at[lax.rem(z + (4, NZ - 3)[way], NZ)],
        lambda way: k_first.at[way],
        lambda way: v_first.at[way],
    )

    def to_right(index, step):
        buffer = summed[index][1]
        src = first[index](0) if step == 0 else buffer.at[step - 1]
        return remote(src, buffer.at[step], gr_send, gr_recv, index * 4 + step, right)

    def to_left(index, step):
        buffer = summed[index][2]
        src = first[index](1) if step == 0 else buffer.at[step - 1]
        return remote(src, buffer.at[step], gl_send, gl_recv, index * 3 + step, left)

    def ring_first(index):
        to_right(index, 0).start()
        to_left(index, 0).start()

    def ring_next(index, step):
        value, r_buffer, l_buffer, _ = summed[index]
        to_right(index, step - 1).wait_recv()
        r_buffer[step - 1] = (
            r_buffer[step - 1].astype(F32) + value(lax.rem(z + 4 - step, NZ))
        ).astype(BF)
        to_right(index, step).start()
        if step < 3:
            to_left(index, step - 1).wait_recv()
            l_buffer[step - 1] = (
                l_buffer[step - 1].astype(F32) + value(lax.rem(z + NZ - 3 + step, NZ))
            ).astype(BF)
            to_left(index, step).start()

    def ring_last(index):
        value, r_buffer, l_buffer, out = summed[index]
        to_right(index, 3).wait_recv()
        to_left(index, 2).wait_recv()
        out[...] = (value(z) + r_buffer[3].astype(F32) + l_buffer[2].astype(F32)).astype(BF)

    def project():
        gather_step((0, 1, 2), 4)
        rows_in = xc[...].astype(F32)
        x = rows_in[:, :, :CAP, :].reshape(count, DS).astype(BF)
        c = rows_in[:, :, CAP:, :].reshape(count, DS).astype(BF)
        for index, (left_side, w) in enumerate(((x, wg_all), (x, wu_all), (c, wd_all))):
            product = dot(left_side, w[...].reshape(DS, FF), 1, 0)
            part[:, :, index * FF : (index + 1) * FF] = product.reshape(
                NY, NE * CAP, FF
            ).astype(BF)
        for copy in swaps():
            copy.start()

    def activate():
        for copy in swaps():
            copy.wait_recv()
        sums = part[y].astype(F32)
        for d in range(NY - 1):
            sums = sums + parts[d].astype(F32)
        gate_act = sums[:, :FF]
        up_act = sums[:, FF : 2 * FF]
        cot_down = sums[:, 2 * FF :]
        w = rows_own[:, :, D:].astype(F32)[:, :CAP, :].reshape(NE * CAP, 128)[:, :1]
        sigma = 1.0 / (1.0 + jnp.exp(-gate_act))
        silu = gate_act * sigma
        hidden = (silu * up_act).astype(BF).astype(F32)
        hidden_grad = w * cot_down
        act[y, :, :FF] = (
            hidden_grad * up_act * sigma * (1.0 + gate_act * (1.0 - sigma))
        ).astype(BF)
        act[y, :, FF : 2 * FF] = (hidden_grad * silu).astype(BF)
        act[y, :, 2 * FF :] = (w * hidden).astype(BF)
        for copy in spreads():
            copy.start()
        values = jnp.sum(hidden * cot_down, axis=1, keepdims=True)
        route[...] = jnp.broadcast_to(values, (NE * CAP, 128)).reshape(NE, CAP, 128)
        for copy in routes():
            copy.start()
        here(route.at[e], route_home.at[e], 9).start()

    def differentiate():
        for copy in spreads():
            copy.wait_recv()
        blocks = (NZ, WD, FF)
        act_all = act[...].reshape(count, 3 * FF)
        gate_pre = act_all[:, :FF]
        up_pre = act_all[:, FF : 2 * FF]
        gg[...] = dot(x_t[...], gate_pre, 1, 0).astype(BF).reshape(blocks)
        ring_first(0)
        gu[...] = dot(x_t[...], up_pre, 1, 0).astype(BF).reshape(blocks)
        ring_first(1)
        gd[...] = dot(c_t[...], act_all[:, 2 * FF :], 1, 0).astype(BF).reshape(blocks)
        ring_first(2)
        row_grad = dot(gate_pre, wg_all[...].reshape(DS, FF), 1, 1) + dot(
            up_pre, wu_all[...].reshape(DS, FF), 1, 1
        )
        row_grad = row_grad.reshape(NY, NE, CAP, DS)
        rb[...] = jnp.concatenate(
            [row_grad[:, :, :, i * 128 : (i + 1) * 128] for i in range(DS // 128)], axis=2
        ).astype(BF)
        for copy in row_swaps():
            copy.start()
        here(rb.at[y], rbuf.at[y], 10).start()

    events = {
        EVENTS[0]: lambda: gather_step((0, 1, 2), 1),
        EVENTS[1]: lambda: gather_step((0, 1, 2), 2),
        EVENTS[2]: lambda: gather_step((0, 1, 2), 3),
        EVENTS[3]: project,
        EVENTS[4]: activate,
        EVENTS[5]: differentiate,
    }

    def work(i, carry):
        attend(lax.div(i, 2), lax.rem(i, 2))
        for when, event in events.items():
            pl.when(i == when)(event)
        return carry

    lax.fori_loop(0, NY * (GW // (HALF * HEAD_SIZE)), work, 0)

    for way in range(2):
        block = lax.rem(z + (4, NZ - 3)[way], NZ)
        k_first[way] = (dk_acc[:, block] * scale).astype(BF)
        v_first[way] = dv_acc[:, block].astype(BF)
    ring_first(3)
    ring_first(4)

    def q_homes():
        return [
            remote(dq.at[at_y(y, z, e, d)[0]], dq_home.at[:, columns(y, GW)], q_send, q_recv,
                   d - 1, at_y(y, z, e, d)[1])
            for d in range(1, NY)
        ]

    def row_homes():
        return [
            remote(rbuf.at[:, at_e(y, z, e, d)[0]], back.at[e], i_send, i_recv, d - 1,
                   at_e(y, z, e, d)[1])
            for d in range(1, NE)
        ]

    for c in q_homes():
        c.start()
    own_q = here(dq.at[y], dq_home.at[:, columns(y, GW)], 11)
    own_q.start()
    here(rb.at[y], rbuf.at[y], 10).wait()
    for c in row_swaps():
        c.wait_recv()
    for c in row_homes():
        c.start()
    own_back = here(rbuf.at[:, e], back.at[e], 12)
    own_back.start()

    for step in range(1, 4):
        for index in (0, 1, 2, 3, 4):
            ring_next(index, step)

    own_back.wait()
    for c in row_homes():
        c.wait_recv()
    pieces = back[...].astype(F32).reshape(NE, NY, DS // 128, CAP, 128)
    for block in range(NY):
        for i in range(DS // 128):
            piece = pieces[:, block, i].reshape(NE * CAP, 128).astype(BF)
            start = block * DS + i * 128
            input_grad[:, start : start + 128] = dot(dispatch[...], piece, 1, 0).astype(BF)

    def homes(index):
        mine = summed[index][3]
        out = (dk_home, dv_home)[index - 3].at[:, columns(y, HEAD_SIZE)]
        return [
            remote(mine.at[at_y(y, z, e, d)[0]], out, h_send, h_recv, (index - 3) * 3 + d - 1,
                   at_y(y, z, e, d)[1])
            for d in range(1, NY)
        ], here(mine.at[y], out, 10 + index)

    for index in (3, 4):
        ring_last(index)
        copies, mine = homes(index)
        for c in copies + [mine]:
            c.start()
    for index in (0, 1, 2):
        ring_last(index)
    for index in (3, 4):
        copies, mine = homes(index)
        mine.wait()
        for c in copies:
            c.wait()
    own_q.wait()
    here(route.at[e], route_home.at[e], 9).wait()
    for c in q_homes() + routes():
        c.wait()
    for c in tokens() + kv_exchange() + q_exchange() + slices() + swaps() + spreads():
        c.wait_send()
    for c in row_swaps() + row_homes():
        c.wait_send()
    for index in range(5):
        for step in range(4):
            for c in gather(index, step):
                c.wait_send()
            to_right(index, step).wait_send()
            if step < 3:
                to_left(index, step).wait_send()


def layer(q, do, k, v, rows, wg, wu, wd, dispatch):
    sd = jax.ShapeDtypeStruct
    any_spec = pl.BlockSpec(memory_space=pl.ANY)
    vmem = pl.BlockSpec(memory_space=pltpu.VMEM)
    dma = pltpu.SemaphoreType.DMA
    scratch = pltpu.VMEM
    kv = (NY, TOK, HEAD_SIZE)
    whole = (NY, NZ, TOK, HEAD_SIZE)
    length = NY * NZ * TOK
    slots = NE * CAP
    blocks = (NZ, WD, FF)
    rings = []
    for shape in (kv, kv, (WD, FF), (WD, FF), (WD, FF)):
        rings += [scratch((4,) + shape, BF), scratch((3,) + shape, BF)]
    return pl.pallas_call(
        layer_kernel,
        out_shape=[
            sd((TOK, QUERY_HEADS * HEAD_SIZE), BF),
            sd((TOK, KEY_VALUE_HEADS * HEAD_SIZE), BF),
            sd((TOK, KEY_VALUE_HEADS * HEAD_SIZE), BF),
            sd((WD, FF), BF),
            sd((WD, FF), BF),
            sd((WD, FF), BF),
            sd((TOK, D), BF),
            sd((NE, CAP, 128), F32),
        ],
        in_specs=[any_spec] * 8 + [vmem],
        out_specs=[any_spec] * 3 + [vmem] * 5,
        scratch_shapes=[
            scratch((NY, TOK, GW), BF), scratch((NY, TOK, GW), BF),
            scratch(whole, BF), scratch(whole, BF), scratch((HEAD_SIZE, length), BF),
            scratch((ROWS, HEAD_SIZE), BF), scratch((ROWS, HEAD_SIZE), BF),
            scratch((length, ROWS), F32), scratch((length, ROWS), F32),
            scratch(whole, F32), scratch(whole, F32), scratch((HEAD_SIZE, ROWS), F32),
            scratch((NY, TOK, GW), BF),
            scratch((NE, 16, D + 128), BF), scratch((NY, NE, 16, DS), BF),
            scratch((DS, NY * slots), BF), scratch((DS, NY * slots), BF),
            scratch(blocks, BF), scratch(blocks, BF), scratch(blocks, BF),
            scratch((NY, slots, 3 * FF), BF), scratch((NY - 1, slots, 3 * FF), BF),
            scratch((NY, slots, 3 * FF), BF), scratch((NE, CAP, 128), F32),
            scratch((NY, NE, 32, 128), BF), scratch((NY, NE, 32, 128), BF),
            scratch((NE, NY, 32, 128), BF),
            scratch(blocks, BF), scratch(blocks, BF), scratch(blocks, BF),
        ]
        + rings
        + [
            scratch((2,) + kv, BF), scratch((2,) + kv, BF), scratch(kv, BF), scratch(kv, BF),
            dma((16,)), dma((12,)), dma((12,)), dma((7,)), dma((7,)), dma((3,)), dma((3,)),
            dma((20,)), dma((20,)), dma((15,)), dma((15,)),
            dma((3,)), dma((3,)), dma((3,)), dma((3,)), dma((7,)), dma((7,)),
            dma((3,)), dma((3,)), dma((3,)), dma((3,)), dma((7,)), dma((7,)), dma((6,)), dma((6,)),
            dma((20,)), dma((20,)), dma((15,)), dma((15,)),
        ],
        compiler_params=pltpu.CompilerParams(
            collective_id=0, has_side_effects=True, vmem_limit_bytes=VMEM_MOST
        ),
        name="layer",
    )(q, do, k, v, rows, wg, wu, wd, dispatch)


def per_device(
    query_rows,
    key_matrix_all,
    value_matrix_all,
    context_grad,
    mixture_input,
    mixture_grad,
    expert_ids,
    route_weight,
    gate_weight,
    up_weight,
    down_weight,
):
    per_owner = EXPERTS // NE
    tokens = mixture_input[0]
    cotangent = mixture_grad[0]
    routes = expert_ids[0]
    in_window = routes % per_owner == 0
    route_owner = (
        in_window[:, :, None]
        & ((routes // per_owner)[:, :, None] == jnp.arange(NE)[None, None, :])
    ).astype(F32)
    token_owner = jnp.sum(route_owner, axis=1)
    earlier = (jnp.arange(TOK)[:, None] > jnp.arange(TOK)[None, :]).astype(BF)
    slot_index = jnp.dot(earlier, token_owner.astype(BF), preferred_element_type=F32)
    placement = token_owner[:, :, None] * (
        slot_index[:, :, None] == jnp.arange(CAP, dtype=F32)[None, None, :]
    ).astype(F32)
    dispatch = placement.reshape(TOK, NE * CAP).astype(BF)
    weight_owner = jnp.sum(route_owner * route_weight[0].astype(F32)[:, :, None], axis=1)
    slot_weight = jnp.sum(placement * weight_owner[:, :, None], axis=0).astype(BF)
    x_rows = jnp.einsum("tr,td->rd", dispatch, tokens, preferred_element_type=F32).astype(BF)
    c_rows = jnp.einsum("tr,td->rd", dispatch, cotangent, preferred_element_type=F32).astype(BF)
    rows = jnp.concatenate(
        (x_rows.reshape(NE, CAP, D), c_rows.reshape(NE, CAP, D)), axis=1
    )
    weight_cols = jnp.broadcast_to(
        jnp.concatenate((slot_weight, slot_weight), axis=1)[:, :, None], (NE, 2 * CAP, 128)
    )
    rows = jnp.concatenate((rows, weight_cols), axis=2)

    (
        dq_home, dk_home, dv_home, gate_grad, up_grad, down_grad, input_grad, route_home,
    ) = layer(
        query_rows[0], context_grad[0], key_matrix_all[0], value_matrix_all[0], rows,
        gate_weight[0], up_weight[0], down_weight[0], dispatch,
    )
    back_route = route_home[:, :, 0].astype(BF).astype(F32)
    route_token = jnp.sum(placement * back_route[None], axis=2)
    route_grad = jnp.sum(route_owner * route_token[:, None, :], axis=2).astype(BF)
    return (
        dq_home[None],
        dk_home[None],
        dv_home[None],
        input_grad[None],
        route_grad[None],
        gate_grad[None],
        up_grad[None],
        down_grad[None],
    )


def solution(mesh):
    spec = P("exp", "ctx", None)
    return jax.shard_map(
        per_device,
        mesh=mesh,
        in_specs=(spec,) * 11,
        out_specs=(spec,) * 8,
        check_vma=False,
    )
```

```python
import math

import jax
import jax.numpy as jnp
from jax import lax
from jax.experimental import pallas as pl
from jax.experimental.pallas import tpu as pltpu
from jax.sharding import PartitionSpec as P

D = 2048
QUERY_HEADS = 32
KEY_VALUE_HEADS = 4
HEAD_SIZE = 128
FF = 768
EXPERTS = 128
TOPK = 8
CAP = 8
NY = 4
NZ = 8
NE = 8
TOK = 128
GW = QUERY_HEADS // KEY_VALUE_HEADS * HEAD_SIZE
DS = D // NY
WD = D // (NY * NZ)
KC = 512
HALF = 4
ROWS = HALF * TOK
STEPS = NY * (GW // (HALF * HEAD_SIZE))
MESH = pl.DeviceIdType.MESH
VMEM_MOST = 60 * 1024 * 1024
BF = jnp.bfloat16
F32 = jnp.float32


def places():
    ctx = lax.axis_index("ctx")
    return lax.div(ctx, NZ), lax.rem(ctx, NZ), lax.axis_index("exp")


def at_y(y, z, e, shift):
    peer = lax.rem(y + shift, NY)
    return peer, (peer * NZ + z, e)


def at_z(y, z, e, shift):
    peer = lax.rem(z + shift + NZ, NZ)
    return peer, (y * NZ + peer, e)


def at_e(y, z, e, shift):
    peer = lax.rem(e + shift, NE)
    return peer, (y * NZ + z, peer)


def greet(peers):
    barrier = pltpu.get_barrier_semaphore()
    for peer in peers:
        pl.semaphore_signal(barrier, inc=1, device_id=peer, device_id_type=MESH)
    pl.semaphore_wait(barrier, len(peers))


def remote(src, dst, send, recv, index, peer):
    return pltpu.make_async_remote_copy(
        src_ref=src,
        dst_ref=dst,
        send_sem=send.at[index],
        recv_sem=recv.at[index],
        device_id=peer,
        device_id_type=MESH,
    )


def columns(index, width):
    return pl.ds(pl.multiple_of(index * width, width), width)


def dot(a, b, left, right):
    return lax.dot_general(a, b, (((left,), (right,)), ((), ())), preferred_element_type=F32)


def layer_kernel(
    q, do, k, v, rows, wg, wu, wd, dispatch,
    dq_home, dk_home, dv_home, gg_out, gu_out, gd_out, input_grad, route_home,
    q_all, do_all, k_all, v_all, kt, q_st, do_st, s_scr, g_scr, dk_acc, dv_acc, dqt, dq,
    rows_own, xc, x_t, c_t, wg_all, wu_all, wd_all, part, parts, act, route,
    rb, rbuf, back, gg, gu, gd,
    kv_right, kv_left, g_right, g_left, u_right, u_left, d_right, d_left, kv_first, kv_sum,
    local_sem, y_send, y_recv, e_send, e_recv, x_send, x_recv, r_send, r_recv, l_send, l_recv,
    s_send, s_recv, a_send, a_recv, t_send, t_recv, q_send, q_recv, b_send, b_recv,
    i_send, i_recv, h_send, h_recv, gr_send, gr_recv, gl_send, gl_recv,
):
    y, z, e = places()
    count = NY * NE * CAP
    scale = 1.0 / math.sqrt(HEAD_SIZE)
    factor = scale * math.log2(math.e)
    greet(
        [at_y(y, z, e, d)[1] for d in range(1, NY)]
        + [at_z(y, z, e, d)[1] for d in (1, -1)]
        + [at_e(y, z, e, d)[1] for d in range(1, NE)]
    )
    right = at_z(y, z, e, 1)[1]
    left = at_z(y, z, e, -1)[1]

    def tokens():
        return [
            remote(rows.at[at_e(y, z, e, d)[0]], rows_own.at[e], e_send, e_recv, d - 1,
                   at_e(y, z, e, d)[1])
            for d in range(1, NE)
        ]

    def slices():
        return [
            remote(rows_own.at[:, :, columns(at_y(y, z, e, d)[0], DS)], xc.at[y], x_send, x_recv,
                   d - 1, at_y(y, z, e, d)[1])
            for d in range(1, NY)
        ]

    def y_exchange(src, target, width, base):
        return [
            remote(src.at[:, columns(at_y(y, z, e, d)[0], width)], target, y_send, y_recv,
                   base + d - 1, at_y(y, z, e, d)[1])
            for d in range(1, NY)
        ]

    def kv_exchange():
        return y_exchange(k, k_all.at[y, z], HEAD_SIZE, 0) + y_exchange(
            v, v_all.at[y, z], HEAD_SIZE, 3
        )

    def q_exchange():
        return y_exchange(q, q_all.at[y], GW, 6) + y_exchange(do, do_all.at[y], GW, 9)

    gathered = (
        lambda b: wg_all.at[b],
        lambda b: wu_all.at[b],
        lambda b: wd_all.at[b],
        lambda b: k_all.at[:, b],
        lambda b: v_all.at[:, b],
    )

    def gather(index, step):
        block = gathered[index]
        here = block(lax.rem(z - step + NZ, NZ))
        pair = [remote(here, here, r_send, r_recv, index * 4 + step, right)]
        if step < 3:
            there = block(lax.rem(z + step, NZ))
            pair.append(remote(there, there, l_send, l_recv, index * 3 + step, left))
        return pair

    def gather_step(indices, step):
        for index in indices:
            if step > 0:
                for c in gather(index, step - 1):
                    c.wait_recv()
            if step < 4:
                for c in gather(index, step):
                    c.start()

    def here(src, dst, index):
        return pltpu.make_async_copy(src, dst, local_sem.at[index])

    for c in tokens() + kv_exchange():
        c.start()
    own = [
        here(rows.at[e], rows_own.at[e], 0),
        here(k.at[:, columns(y, HEAD_SIZE)], k_all.at[y, z], 1),
        here(v.at[:, columns(y, HEAD_SIZE)], v_all.at[y, z], 2),
        here(q.at[:, columns(y, GW)], q_all.at[y], 3),
        here(do.at[:, columns(y, GW)], do_all.at[y], 4),
        here(wg, wg_all.at[z], 5),
        here(wu, wu_all.at[z], 6),
        here(wd, wd_all.at[z], 7),
    ]
    for c in own:
        c.start()
    for c in own[5:]:
        c.wait()
    gather_step((0, 1, 2), 0)
    for c in kv_exchange():
        c.wait_recv()
    for c in own[:5]:
        c.wait()
    gather_step((3, 4), 0)
    for c in q_exchange():
        c.start()
    for c in tokens():
        c.wait_recv()
    for c in slices():
        c.start()
    own_xc = here(rows_own.at[:, :, columns(y, DS)], xc.at[y], 8)
    own_xc.start()
    dk_acc[...] = jnp.zeros_like(dk_acc)
    dv_acc[...] = jnp.zeros_like(dv_acc)
    for step in range(1, 4):
        gather_step((3, 4), step)
    gather_step((0, 1, 2), 1)
    own_xc.wait()
    for c in slices():
        c.wait_recv()
    both = xc[...].astype(F32)
    x_t[...] = both[:, :, :CAP, :].reshape(count, DS).T.astype(BF)
    c_t[...] = both[:, :, CAP:, :].reshape(count, DS).T.astype(BF)
    gather_step((3, 4), 4)
    for c in q_exchange():
        c.wait_recv()

    def chunk(c):
        return lax.div(c, 2), pl.ds(lax.rem(c, 2) * (KC // TOK), KC // TOK)

    def chunk_rows(ref, c):
        a, b = chunk(c)
        return ref[a, b].reshape(KC, HEAD_SIZE)

    def at(c):
        return pl.ds(pl.multiple_of(c * KC, KC), KC)

    def turn(c, carry):
        kt[:, at(c)] = chunk_rows(k_all, c).astype(F32).T.astype(BF)
        return carry

    lax.fori_loop(0, NY * NZ * TOK // KC, turn, 0)

    def fold(values, op):
        return op(values.reshape(KC // 8, 8, ROWS), axis=0)

    def attend(block, half, event):
        position = block * NZ + z
        chunks = lax.div(position * TOK + TOK + KC - 1, KC)
        for h in range(HALF):
            cols = pl.ds(
                pl.multiple_of(half * (HALF * HEAD_SIZE) + h * HEAD_SIZE, HEAD_SIZE), HEAD_SIZE
            )
            q_st[h * TOK : (h + 1) * TOK, :] = q_all[block, :, cols]
            do_st[h * TOK : (h + 1) * TOK, :] = do_all[block, :, cols]

        def scores(c, peak, masked):
            s = dot(chunk_rows(k_all, c), q_st[...], 1, 1) * factor
            if masked:
                key_pos = c * KC + lax.broadcasted_iota(jnp.int32, (KC, ROWS), 0)
                query_pos = position * TOK + lax.rem(
                    lax.broadcasted_iota(jnp.int32, (KC, ROWS), 1), TOK
                )
                s = jnp.where(key_pos <= query_pos, s, -1e30)
            s_scr[at(c), :] = s
            return jnp.maximum(peak, fold(s, jnp.max))

        peak = lax.fori_loop(
            0, chunks - 1, lambda c, m: scores(c, m, False), jnp.full((8, ROWS), -1e30, F32)
        )
        peak = scores(chunks - 1, peak, True)
        peak = jnp.max(peak, axis=0, keepdims=True)
        event(0)

        def weigh(c, carry):
            total, paired = carry
            p = jnp.exp2(s_scr[at(c), :] - peak)
            g = dot(chunk_rows(v_all, c), do_st[...], 1, 1)
            s_scr[at(c), :] = p
            g_scr[at(c), :] = g
            return total + fold(p, jnp.sum), paired + fold(p * g, jnp.sum)

        zero = jnp.zeros((8, ROWS), F32)
        total, paired = lax.fori_loop(0, chunks, weigh, (zero, zero))
        inverse = 1.0 / jnp.sum(total, axis=0, keepdims=True)
        row_dot = jnp.sum(paired, axis=0, keepdims=True) * inverse
        event(1)

        dqt[...] = jnp.zeros_like(dqt)

        def gradients(c, carry):
            a, b = chunk(c)
            p = s_scr[at(c), :] * inverse
            ds = (p * (g_scr[at(c), :] - row_dot)).astype(BF)
            shape = (KC // TOK, TOK, HEAD_SIZE)
            dv_acc[a, b] += dot(p.astype(BF), do_st[...], 1, 0).reshape(shape)
            dk_acc[a, b] += dot(ds, q_st[...], 1, 0).reshape(shape)
            dqt[...] += dot(kt[:, at(c)], ds, 1, 0)
            return carry

        lax.fori_loop(0, chunks, gradients, 0)
        for h in range(HALF):
            cols = pl.ds(
                pl.multiple_of(half * (HALF * HEAD_SIZE) + h * HEAD_SIZE, HEAD_SIZE), HEAD_SIZE
            )
            dq[block, :, cols] = (dqt[:, h * TOK : (h + 1) * TOK] * scale).T.astype(BF)
        event(2)

    def swaps():
        return [
            remote(part.at[at_y(y, z, e, d)[0]], parts.at[d - 1], s_send, s_recv, d - 1,
                   at_y(y, z, e, d)[1])
            for d in range(1, NY)
        ]

    def spreads():
        return [
            remote(act.at[y], act.at[y], a_send, a_recv, d - 1, at_y(y, z, e, d)[1])
            for d in range(1, NY)
        ]

    def routes():
        return [
            remote(route.at[at_e(y, z, e, d)[0]], route_home.at[e], t_send, t_recv, d - 1,
                   at_e(y, z, e, d)[1])
            for d in range(1, NE)
        ]

    def row_swaps():
        return [
            remote(rb.at[at_y(y, z, e, d)[0]], rbuf.at[y], b_send, b_recv, d - 1,
                   at_y(y, z, e, d)[1])
            for d in range(1, NY)
        ]

    def quarter(block):
        def value(b):
            return jnp.stack([dk_acc[block, b] * scale, dv_acc[block, b]])

        return value

    summed = [
        (lambda b: gg[b].astype(F32), lambda t: g_right.at[t], lambda t: g_left.at[t], gg_out),
        (lambda b: gu[b].astype(F32), lambda t: u_right.at[t], lambda t: u_left.at[t], gu_out),
        (lambda b: gd[b].astype(F32), lambda t: d_right.at[t], lambda t: d_left.at[t], gd_out),
    ]
    for block in range(NY):
        summed.append(
            (
                quarter(block),
                lambda t, block=block: kv_right.at[t, block],
                lambda t, block=block: kv_left.at[t, block],
                kv_sum.at[block],
            )
        )
    first = (
        lambda way: gg.at[lax.rem(z + (4, NZ - 3)[way], NZ)],
        lambda way: gu.at[lax.rem(z + (4, NZ - 3)[way], NZ)],
        lambda way: gd.at[lax.rem(z + (4, NZ - 3)[way], NZ)],
        lambda way: kv_first.at[0, way],
        lambda way: kv_first.at[1, way],
        lambda way: kv_first.at[2, way],
        lambda way: kv_first.at[3, way],
    )

    def to_right(index, step):
        buffer = summed[index][1]
        src = first[index](0) if step == 0 else buffer(step - 1)
        return remote(src, buffer(step), gr_send, gr_recv, index * 4 + step, right)

    def to_left(index, step):
        buffer = summed[index][2]
        src = first[index](1) if step == 0 else buffer(step - 1)
        return remote(src, buffer(step), gl_send, gl_recv, index * 3 + step, left)

    def ring_first(index):
        to_right(index, 0).start()
        to_left(index, 0).start()

    def ring_next(index, step):
        value, r_buffer, l_buffer, _ = summed[index]
        to_right(index, step - 1).wait_recv()
        got = r_buffer(step - 1)
        got[...] = (got[...].astype(F32) + value(lax.rem(z + 4 - step, NZ))).astype(BF)
        to_right(index, step).start()
        if step < 3:
            to_left(index, step - 1).wait_recv()
            got = l_buffer(step - 1)
            got[...] = (got[...].astype(F32) + value(lax.rem(z + NZ - 3 + step, NZ))).astype(BF)
            to_left(index, step).start()

    def ring_last(index):
        value, r_buffer, l_buffer, out = summed[index]
        to_right(index, 3).wait_recv()
        to_left(index, 2).wait_recv()
        out[...] = (
            value(z) + r_buffer(3)[...].astype(F32) + l_buffer(2)[...].astype(F32)
        ).astype(BF)

    def project():
        gather_step((0, 1, 2), 4)
        rows_in = xc[...].astype(F32)
        x = rows_in[:, :, :CAP, :].reshape(count, DS).astype(BF)
        c = rows_in[:, :, CAP:, :].reshape(count, DS).astype(BF)
        for index, (left_side, w) in enumerate(((x, wg_all), (x, wu_all), (c, wd_all))):
            product = dot(left_side, w[...].reshape(DS, FF), 1, 0)
            part[:, :, index * FF : (index + 1) * FF] = product.reshape(
                NY, NE * CAP, FF
            ).astype(BF)
        for copy in swaps():
            copy.start()

    def activate():
        for copy in swaps():
            copy.wait_recv()
        sums = part[y].astype(F32)
        for d in range(NY - 1):
            sums = sums + parts[d].astype(F32)
        gate_act = sums[:, :FF]
        up_act = sums[:, FF : 2 * FF]
        cot_down = sums[:, 2 * FF :]
        w = rows_own[:, :, D:].astype(F32)[:, :CAP, :].reshape(NE * CAP, 128)[:, :1]
        sigma = 1.0 / (1.0 + jnp.exp(-gate_act))
        silu = gate_act * sigma
        hidden = (silu * up_act).astype(BF).astype(F32)
        hidden_grad = w * cot_down
        act[y, :, :FF] = (
            hidden_grad * up_act * sigma * (1.0 + gate_act * (1.0 - sigma))
        ).astype(BF)
        act[y, :, FF : 2 * FF] = (hidden_grad * silu).astype(BF)
        act[y, :, 2 * FF :] = (w * hidden).astype(BF)
        for copy in spreads():
            copy.start()
        values = jnp.sum(hidden * cot_down, axis=1, keepdims=True)
        route[...] = jnp.broadcast_to(values, (NE * CAP, 128)).reshape(NE, CAP, 128)
        for copy in routes():
            copy.start()
        here(route.at[e], route_home.at[e], 9).start()

    def differentiate():
        for copy in spreads():
            copy.wait_recv()
        blocks = (NZ, WD, FF)
        act_all = act[...].reshape(count, 3 * FF)
        gate_pre = act_all[:, :FF]
        up_pre = act_all[:, FF : 2 * FF]
        gg[...] = dot(x_t[...], gate_pre, 1, 0).astype(BF).reshape(blocks)
        ring_first(0)
        gu[...] = dot(x_t[...], up_pre, 1, 0).astype(BF).reshape(blocks)
        ring_first(1)
        gd[...] = dot(c_t[...], act_all[:, 2 * FF :], 1, 0).astype(BF).reshape(blocks)
        ring_first(2)
        row_grad = dot(gate_pre, wg_all[...].reshape(DS, FF), 1, 1) + dot(
            up_pre, wu_all[...].reshape(DS, FF), 1, 1
        )
        row_grad = row_grad.reshape(NY, NE, CAP, DS)
        rb[...] = jnp.concatenate(
            [row_grad[:, :, :, i * 128 : (i + 1) * 128] for i in range(DS // 128)], axis=2
        ).astype(BF)
        for copy in row_swaps():
            copy.start()
        here(rb.at[y], rbuf.at[y], 10).start()

    def quarter_first(block):
        for way in range(2):
            b = lax.rem(z + (4, NZ - 3)[way], NZ)
            kv_first[block, way] = summed[3 + block][0](b).astype(BF)
        ring_first(3 + block)

    def q_home(block):
        return pltpu.make_async_remote_copy(
            src_ref=dq.at[block],
            dst_ref=dq_home.at[:, columns(y, GW)],
            send_sem=q_send.at[block],
            recv_sem=q_recv.at[y],
            device_id=(block * NZ + z, e),
            device_id_type=MESH,
        )

    def q_from(block):
        return pltpu.make_async_remote_copy(
            src_ref=dq.at[block],
            dst_ref=dq_home.at[:, block * GW : (block + 1) * GW],
            send_sem=q_send.at[block],
            recv_sem=q_recv.at[block],
            device_id=(block * NZ + z, e),
            device_id_type=MESH,
        )

    def send_q(block):
        pl.when(y != block)(lambda: q_home(block).start())

    def weights_next(step):
        for index in (0, 1, 2):
            ring_next(index, step)

    def mixed():
        differentiate()
        send_q(3)
        send_q(2)

    def second_end():
        ring_last(6)
        quarter_first(2)

    def third_end():
        ring_last(5)
        quarter_first(1)
        send_q(1)

    events = (
        (0, 0, lambda: gather_step((0, 1, 2), 2)),
        (0, 2, lambda: gather_step((0, 1, 2), 3)),
        (1, 1, project),
        (1, 2, lambda: quarter_first(3)),
        (2, 0, lambda: ring_next(6, 1)),
        (2, 2, activate),
        (3, 0, lambda: ring_next(6, 2)),
        (3, 1, lambda: ring_next(6, 3)),
        (3, 2, second_end),
        (4, 0, lambda: ring_next(5, 1)),
        (4, 2, mixed),
        (5, 0, lambda: ring_next(5, 2)),
        (5, 1, lambda: ring_next(5, 3)),
        (5, 2, third_end),
        (6, 0, lambda: weights_next(1)),
        (6, 1, lambda: ring_next(4, 1)),
        (7, 0, lambda: ring_next(4, 2)),
        (7, 1, lambda: weights_next(2)),
    )

    def work(i, carry):
        def event(sweep):
            for step, when, act_now in events:
                if when == sweep:
                    pl.when(i == step)(act_now)

        attend(NY - 1 - lax.div(i, 2), lax.rem(i, 2), event)
        return carry

    lax.fori_loop(0, STEPS, work, 0)
    quarter_first(0)
    send_q(0)
    own_q = here(dq.at[y], dq_home.at[:, columns(y, GW)], 11)
    own_q.start()

    def row_homes():
        return [
            remote(rbuf.at[:, at_e(y, z, e, d)[0]], back.at[e], i_send, i_recv, d - 1,
                   at_e(y, z, e, d)[1])
            for d in range(1, NE)
        ]

    here(rb.at[y], rbuf.at[y], 10).wait()
    for c in row_swaps():
        c.wait_recv()
    for c in row_homes():
        c.start()
    own_back = here(rbuf.at[:, e], back.at[e], 12)
    own_back.start()

    ring_next(4, 3)
    ring_next(3, 1)
    weights_next(3)
    ring_next(3, 2)
    ring_next(3, 3)
    ring_last(4)

    own_back.wait()
    for c in row_homes():
        c.wait_recv()
    pieces = back[...].astype(F32).reshape(NE, NY, DS // 128, CAP, 128)
    for block in range(NY):
        for i in range(DS // 128):
            piece = pieces[:, block, i].reshape(NE * CAP, 128).astype(BF)
            start = block * DS + i * 128
            input_grad[:, start : start + 128] = dot(dispatch[...], piece, 1, 0).astype(BF)

    def homes():
        copies = []
        for kind, out in enumerate((dk_home, dv_home)):
            target = out.at[:, columns(y, HEAD_SIZE)]
            for d in range(1, NY):
                peer, dev = at_y(y, z, e, d)
                copies.append(
                    remote(kv_sum.at[peer, kind], target, h_send, h_recv, kind * 3 + d - 1, dev)
                )
            copies.append(here(kv_sum.at[y, kind], target, 13 + kind))
        return copies

    ring_last(3)
    for c in homes():
        c.start()
    for index in (0, 1, 2):
        ring_last(index)
    for c in homes():
        c.wait()
    for block in range(NY):
        pl.when(y != block)(lambda block=block: q_home(block).wait_send())
        pl.when(y != block)(lambda block=block: q_from(block).wait_recv())
    own_q.wait()
    here(route.at[e], route_home.at[e], 9).wait()
    for c in routes():
        c.wait()
    for c in tokens() + kv_exchange() + q_exchange() + slices() + swaps() + spreads():
        c.wait_send()
    for c in row_swaps() + row_homes():
        c.wait_send()
    for index in range(5):
        for step in range(4):
            for c in gather(index, step):
                c.wait_send()
    for index in range(3 + NY):
        for step in range(4):
            to_right(index, step).wait_send()
            if step < 3:
                to_left(index, step).wait_send()


def layer(q, do, k, v, rows, wg, wu, wd, dispatch):
    sd = jax.ShapeDtypeStruct
    any_spec = pl.BlockSpec(memory_space=pl.ANY)
    vmem = pl.BlockSpec(memory_space=pltpu.VMEM)
    dma = pltpu.SemaphoreType.DMA
    scratch = pltpu.VMEM
    whole = (NY, NZ, TOK, HEAD_SIZE)
    length = NY * NZ * TOK
    slots = NE * CAP
    blocks = (NZ, WD, FF)
    rings = []
    pair = (2, TOK, HEAD_SIZE)
    for shape in ((NY,) + pair, (WD, FF), (WD, FF), (WD, FF)):
        rings += [scratch((4,) + shape, BF), scratch((3,) + shape, BF)]
    return pl.pallas_call(
        layer_kernel,
        out_shape=[
            sd((TOK, QUERY_HEADS * HEAD_SIZE), BF),
            sd((TOK, KEY_VALUE_HEADS * HEAD_SIZE), BF),
            sd((TOK, KEY_VALUE_HEADS * HEAD_SIZE), BF),
            sd((WD, FF), BF),
            sd((WD, FF), BF),
            sd((WD, FF), BF),
            sd((TOK, D), BF),
            sd((NE, CAP, 128), F32),
        ],
        in_specs=[any_spec] * 8 + [vmem],
        out_specs=[any_spec] * 3 + [vmem] * 5,
        scratch_shapes=[
            scratch((NY, TOK, GW), BF), scratch((NY, TOK, GW), BF),
            scratch(whole, BF), scratch(whole, BF), scratch((HEAD_SIZE, length), BF),
            scratch((ROWS, HEAD_SIZE), BF), scratch((ROWS, HEAD_SIZE), BF),
            scratch((length, ROWS), F32), scratch((length, ROWS), F32),
            scratch(whole, F32), scratch(whole, F32), scratch((HEAD_SIZE, ROWS), F32),
            scratch((NY, TOK, GW), BF),
            scratch((NE, 16, D + 128), BF), scratch((NY, NE, 16, DS), BF),
            scratch((DS, NY * slots), BF), scratch((DS, NY * slots), BF),
            scratch(blocks, BF), scratch(blocks, BF), scratch(blocks, BF),
            scratch((NY, slots, 3 * FF), BF), scratch((NY - 1, slots, 3 * FF), BF),
            scratch((NY, slots, 3 * FF), BF), scratch((NE, CAP, 128), F32),
            scratch((NY, NE, 32, 128), BF), scratch((NY, NE, 32, 128), BF),
            scratch((NE, NY, 32, 128), BF),
            scratch(blocks, BF), scratch(blocks, BF), scratch(blocks, BF),
        ]
        + rings
        + [
            scratch((NY, 2) + pair, BF), scratch((NY,) + pair, BF),
            dma((16,)), dma((12,)), dma((12,)), dma((7,)), dma((7,)), dma((3,)), dma((3,)),
            dma((20,)), dma((20,)), dma((15,)), dma((15,)),
            dma((3,)), dma((3,)), dma((3,)), dma((3,)), dma((7,)), dma((7,)),
            dma((4,)), dma((4,)), dma((3,)), dma((3,)), dma((7,)), dma((7,)), dma((6,)), dma((6,)),
            dma((28,)), dma((28,)), dma((21,)), dma((21,)),
        ],
        compiler_params=pltpu.CompilerParams(
            collective_id=0, has_side_effects=True, vmem_limit_bytes=VMEM_MOST
        ),
        name="layer",
    )(q, do, k, v, rows, wg, wu, wd, dispatch)


def per_device(
    query_rows,
    key_matrix_all,
    value_matrix_all,
    context_grad,
    mixture_input,
    mixture_grad,
    expert_ids,
    route_weight,
    gate_weight,
    up_weight,
    down_weight,
):
    per_owner = EXPERTS // NE
    tokens = mixture_input[0]
    cotangent = mixture_grad[0]
    routes = expert_ids[0]
    in_window = routes % per_owner == 0
    route_owner = (
        in_window[:, :, None]
        & ((routes // per_owner)[:, :, None] == jnp.arange(NE)[None, None, :])
    ).astype(F32)
    token_owner = jnp.sum(route_owner, axis=1)
    earlier = (jnp.arange(TOK)[:, None] > jnp.arange(TOK)[None, :]).astype(BF)
    slot_index = jnp.dot(earlier, token_owner.astype(BF), preferred_element_type=F32)
    placement = token_owner[:, :, None] * (
        slot_index[:, :, None] == jnp.arange(CAP, dtype=F32)[None, None, :]
    ).astype(F32)
    dispatch = placement.reshape(TOK, NE * CAP).astype(BF)
    weight_owner = jnp.sum(route_owner * route_weight[0].astype(F32)[:, :, None], axis=1)
    slot_weight = jnp.sum(placement * weight_owner[:, :, None], axis=0).astype(BF)
    x_rows = jnp.einsum("tr,td->rd", dispatch, tokens, preferred_element_type=F32).astype(BF)
    c_rows = jnp.einsum("tr,td->rd", dispatch, cotangent, preferred_element_type=F32).astype(BF)
    rows = jnp.concatenate(
        (x_rows.reshape(NE, CAP, D), c_rows.reshape(NE, CAP, D)), axis=1
    )
    weight_cols = jnp.broadcast_to(
        jnp.concatenate((slot_weight, slot_weight), axis=1)[:, :, None], (NE, 2 * CAP, 128)
    )
    rows = jnp.concatenate((rows, weight_cols), axis=2)

    (
        dq_home, dk_home, dv_home, gate_grad, up_grad, down_grad, input_grad, route_home,
    ) = layer(
        query_rows[0], context_grad[0], key_matrix_all[0], value_matrix_all[0], rows,
        gate_weight[0], up_weight[0], down_weight[0], dispatch,
    )
    back_route = route_home[:, :, 0].astype(BF).astype(F32)
    route_token = jnp.sum(placement * back_route[None], axis=2)
    route_grad = jnp.sum(route_owner * route_token[:, None, :], axis=2).astype(BF)
    return (
        dq_home[None],
        dk_home[None],
        dv_home[None],
        input_grad[None],
        route_grad[None],
        gate_grad[None],
        up_grad[None],
        down_grad[None],
    )


def solution(mesh):
    spec = P("exp", "ctx", None)
    return jax.shard_map(
        per_device,
        mesh=mesh,
        in_specs=(spec,) * 11,
        out_specs=(spec,) * 8,
        check_vma=False,
    )
```

```python
import math

import jax
import jax.numpy as jnp
from jax import lax
from jax.experimental import pallas as pl
from jax.experimental.pallas import tpu as pltpu
from jax.sharding import PartitionSpec as P

D = 2048
QUERY_HEADS = 32
KEY_VALUE_HEADS = 4
HEAD_SIZE = 128
FF = 768
EXPERTS = 128
TOPK = 8
CAP = 8
NY = 4
NZ = 8
NE = 8
TOK = 128
GW = QUERY_HEADS // KEY_VALUE_HEADS * HEAD_SIZE
DS = D // NY
WD = D // (NY * NZ)
KC = 512
HALF = 4
ROWS = HALF * TOK
STEPS = NY * (GW // (HALF * HEAD_SIZE))
MESH = pl.DeviceIdType.MESH
VMEM_MOST = 60 * 1024 * 1024
BF = jnp.bfloat16
F32 = jnp.float32


def places():
    ctx = lax.axis_index("ctx")
    return lax.div(ctx, NZ), lax.rem(ctx, NZ), lax.axis_index("exp")


def at_y(y, z, e, shift):
    peer = lax.rem(y + shift, NY)
    return peer, (peer * NZ + z, e)


def at_z(y, z, e, shift):
    peer = lax.rem(z + shift + NZ, NZ)
    return peer, (y * NZ + peer, e)


def at_e(y, z, e, shift):
    peer = lax.rem(e + shift, NE)
    return peer, (y * NZ + z, peer)


def greet(peers):
    barrier = pltpu.get_barrier_semaphore()
    for peer in peers:
        pl.semaphore_signal(barrier, inc=1, device_id=peer, device_id_type=MESH)
    pl.semaphore_wait(barrier, len(peers))


def remote(src, dst, send, recv, index, peer):
    return pltpu.make_async_remote_copy(
        src_ref=src,
        dst_ref=dst,
        send_sem=send.at[index],
        recv_sem=recv.at[index],
        device_id=peer,
        device_id_type=MESH,
    )


def columns(index, width):
    return pl.ds(pl.multiple_of(index * width, width), width)


def dot(a, b, left, right):
    return lax.dot_general(a, b, (((left,), (right,)), ((), ())), preferred_element_type=F32)


def layer_kernel(
    q, do, k, v, wg, wu, wd, x_in, c_in, ids, route_weight,
    dq_home, dk_home, dv_home, gg_out, gu_out, gd_out, input_grad, route_grad,
    rows, dispatch, route_home,
    q_all, do_all, k_all, v_all, kt, q_st, do_st, s_scr, g_scr, dk_acc, dv_acc, dqt, dq,
    rows_own, xc, x_t, c_t, wg_all, wu_all, wd_all, part, parts, act, route,
    rb, rbuf, back, gg, gu, gd,
    kv_right, kv_left, g_right, g_left, u_right, u_left, d_right, d_left, kv_first, kv_sum,
    local_sem, y_send, y_recv, e_send, e_recv, x_send, x_recv, r_send, r_recv, l_send, l_recv,
    s_send, s_recv, a_send, a_recv, t_send, t_recv, q_send, q_recv, b_send, b_recv,
    i_send, i_recv, h_send, h_recv, gr_send, gr_recv, gl_send, gl_recv,
):
    y, z, e = places()
    count = NY * NE * CAP
    scale = 1.0 / math.sqrt(HEAD_SIZE)
    factor = scale * math.log2(math.e)
    greet(
        [at_y(y, z, e, d)[1] for d in range(1, NY)]
        + [at_z(y, z, e, d)[1] for d in (1, -1)]
        + [at_e(y, z, e, d)[1] for d in range(1, NE)]
    )
    right = at_z(y, z, e, 1)[1]
    left = at_z(y, z, e, -1)[1]

    def tokens():
        return [
            remote(rows.at[at_e(y, z, e, d)[0]], rows_own.at[e], e_send, e_recv, d - 1,
                   at_e(y, z, e, d)[1])
            for d in range(1, NE)
        ]

    def slices():
        return [
            remote(rows_own.at[:, :, columns(at_y(y, z, e, d)[0], DS)], xc.at[y], x_send, x_recv,
                   d - 1, at_y(y, z, e, d)[1])
            for d in range(1, NY)
        ]

    def y_exchange(src, target, width, base):
        return [
            remote(src.at[:, columns(at_y(y, z, e, d)[0], width)], target, y_send, y_recv,
                   base + d - 1, at_y(y, z, e, d)[1])
            for d in range(1, NY)
        ]

    def kv_exchange():
        return y_exchange(k, k_all.at[y, z], HEAD_SIZE, 0) + y_exchange(
            v, v_all.at[y, z], HEAD_SIZE, 3
        )

    def q_exchange():
        return y_exchange(q, q_all.at[y], GW, 6) + y_exchange(do, do_all.at[y], GW, 9)

    gathered = (
        lambda b: wg_all.at[b],
        lambda b: wu_all.at[b],
        lambda b: wd_all.at[b],
        lambda b: k_all.at[:, b],
        lambda b: v_all.at[:, b],
    )

    def gather(index, step):
        block = gathered[index]
        here = block(lax.rem(z - step + NZ, NZ))
        pair = [remote(here, here, r_send, r_recv, index * 4 + step, right)]
        if step < 3:
            there = block(lax.rem(z + step, NZ))
            pair.append(remote(there, there, l_send, l_recv, index * 3 + step, left))
        return pair

    def gather_step(indices, step):
        for index in indices:
            if step > 0:
                for c in gather(index, step - 1):
                    c.wait_recv()
            if step < 4:
                for c in gather(index, step):
                    c.start()

    def here(src, dst, index):
        return pltpu.make_async_copy(src, dst, local_sem.at[index])

    for c in kv_exchange():
        c.start()
    own = [
        here(k.at[:, columns(y, HEAD_SIZE)], k_all.at[y, z], 1),
        here(v.at[:, columns(y, HEAD_SIZE)], v_all.at[y, z], 2),
        here(q.at[:, columns(y, GW)], q_all.at[y], 3),
        here(do.at[:, columns(y, GW)], do_all.at[y], 4),
        here(wg, wg_all.at[z], 5),
        here(wu, wu_all.at[z], 6),
        here(wd, wd_all.at[z], 7),
    ]
    for c in own:
        c.start()
    for c in own[4:]:
        c.wait()
    gather_step((0, 1, 2), 0)

    slot = lax.broadcasted_iota(jnp.int32, (NE * CAP, TOK), 0)
    expert = lax.div(slot, CAP) * (EXPERTS // NE)

    def named(j):
        return (ids[j : j + 1, :] == expert).astype(F32)

    combine = route_weight[...].astype(F32)
    taken = jnp.zeros((NE * CAP, TOK), F32)
    weights = jnp.zeros((NE * CAP, TOK), F32)
    for j in range(TOPK):
        hit = named(j)
        taken += hit
        weights += hit * combine[j : j + 1, :]
    earlier = (
        lax.broadcasted_iota(jnp.int32, (TOK, TOK), 0)
        < lax.broadcasted_iota(jnp.int32, (TOK, TOK), 1)
    ).astype(F32)
    place = dot(taken.astype(BF), earlier.astype(BF), 1, 0)
    placed = taken * (place == lax.rem(slot, CAP).astype(F32)).astype(F32)
    dispatch[...] = placed.T.astype(BF)
    collect = placed.astype(BF)
    rows[:, :, :D] = jnp.concatenate(
        [dot(collect, r[...], 1, 0).reshape(NE, CAP, D) for r in (x_in, c_in)], axis=1
    ).astype(BF)
    weight_col = jnp.sum(placed * weights, axis=1, keepdims=True)
    weight_col = jnp.broadcast_to(weight_col, (NE * CAP, 128)).reshape(NE, CAP, 128)
    rows[:, :, D:] = jnp.concatenate([weight_col, weight_col], axis=1).astype(BF)
    for c in tokens():
        c.start()
    own_rows = here(rows.at[e], rows_own.at[e], 0)
    own_rows.start()

    for c in kv_exchange():
        c.wait_recv()
    for c in own[:4]:
        c.wait()
    gather_step((3, 4), 0)
    for c in q_exchange():
        c.start()
    for c in tokens():
        c.wait_recv()
    own_rows.wait()
    for c in slices():
        c.start()
    own_xc = here(rows_own.at[:, :, columns(y, DS)], xc.at[y], 8)
    own_xc.start()
    dk_acc[...] = jnp.zeros_like(dk_acc)
    dv_acc[...] = jnp.zeros_like(dv_acc)
    for step in range(1, 4):
        gather_step((3, 4), step)
    gather_step((0, 1, 2), 1)
    own_xc.wait()
    for c in slices():
        c.wait_recv()
    both = xc[...].astype(F32)
    x_t[...] = both[:, :, :CAP, :].reshape(count, DS).T.astype(BF)
    c_t[...] = both[:, :, CAP:, :].reshape(count, DS).T.astype(BF)
    gather_step((3, 4), 4)
    for c in q_exchange():
        c.wait_recv()

    def chunk(c):
        return lax.div(c, 2), pl.ds(lax.rem(c, 2) * (KC // TOK), KC // TOK)

    def chunk_rows(ref, c):
        a, b = chunk(c)
        return ref[a, b].reshape(KC, HEAD_SIZE)

    def at(c):
        return pl.ds(pl.multiple_of(c * KC, KC), KC)

    def turn(c, carry):
        kt[:, at(c)] = chunk_rows(k_all, c).astype(F32).T.astype(BF)
        return carry

    lax.fori_loop(0, NY * NZ * TOK // KC, turn, 0)

    def fold(values, op):
        return op(values.reshape(KC // 8, 8, ROWS), axis=0)

    def attend(block, half, event):
        position = block * NZ + z
        chunks = lax.div(position * TOK + TOK + KC - 1, KC)
        for h in range(HALF):
            cols = pl.ds(
                pl.multiple_of(half * (HALF * HEAD_SIZE) + h * HEAD_SIZE, HEAD_SIZE), HEAD_SIZE
            )
            q_st[h * TOK : (h + 1) * TOK, :] = q_all[block, :, cols]
            do_st[h * TOK : (h + 1) * TOK, :] = do_all[block, :, cols]

        def scores(c, peak, masked):
            s = dot(chunk_rows(k_all, c), q_st[...], 1, 1) * factor
            if masked:
                key_pos = c * KC + lax.broadcasted_iota(jnp.int32, (KC, ROWS), 0)
                query_pos = position * TOK + lax.rem(
                    lax.broadcasted_iota(jnp.int32, (KC, ROWS), 1), TOK
                )
                s = jnp.where(key_pos <= query_pos, s, -1e30)
            s_scr[at(c), :] = s
            return jnp.maximum(peak, fold(s, jnp.max))

        peak = lax.fori_loop(
            0, chunks - 1, lambda c, m: scores(c, m, False), jnp.full((8, ROWS), -1e30, F32)
        )
        peak = scores(chunks - 1, peak, True)
        peak = jnp.max(peak, axis=0, keepdims=True)
        event(0)

        def weigh(c, carry):
            total, paired = carry
            p = jnp.exp2(s_scr[at(c), :] - peak)
            g = dot(chunk_rows(v_all, c), do_st[...], 1, 1)
            s_scr[at(c), :] = p
            g_scr[at(c), :] = g
            return total + fold(p, jnp.sum), paired + fold(p * g, jnp.sum)

        zero = jnp.zeros((8, ROWS), F32)
        total, paired = lax.fori_loop(0, chunks, weigh, (zero, zero))
        inverse = 1.0 / jnp.sum(total, axis=0, keepdims=True)
        row_dot = jnp.sum(paired, axis=0, keepdims=True) * inverse
        event(1)

        dqt[...] = jnp.zeros_like(dqt)

        def gradients(c, carry):
            a, b = chunk(c)
            p = s_scr[at(c), :] * inverse
            ds = (p * (g_scr[at(c), :] - row_dot)).astype(BF)
            shape = (KC // TOK, TOK, HEAD_SIZE)
            dv_acc[a, b] += dot(p.astype(BF), do_st[...], 1, 0).reshape(shape)
            dk_acc[a, b] += dot(ds, q_st[...], 1, 0).reshape(shape)
            dqt[...] += dot(kt[:, at(c)], ds, 1, 0)
            return carry

        lax.fori_loop(0, chunks, gradients, 0)
        for h in range(HALF):
            cols = pl.ds(
                pl.multiple_of(half * (HALF * HEAD_SIZE) + h * HEAD_SIZE, HEAD_SIZE), HEAD_SIZE
            )
            dq[block, :, cols] = (dqt[:, h * TOK : (h + 1) * TOK] * scale).T.astype(BF)
        event(2)

    def swaps():
        return [
            remote(part.at[at_y(y, z, e, d)[0]], parts.at[d - 1], s_send, s_recv, d - 1,
                   at_y(y, z, e, d)[1])
            for d in range(1, NY)
        ]

    def spreads():
        return [
            remote(act.at[y], act.at[y], a_send, a_recv, d - 1, at_y(y, z, e, d)[1])
            for d in range(1, NY)
        ]

    def routes():
        return [
            remote(route.at[at_e(y, z, e, d)[0]], route_home.at[e], t_send, t_recv, d - 1,
                   at_e(y, z, e, d)[1])
            for d in range(1, NE)
        ]

    def row_swaps():
        return [
            remote(rb.at[at_y(y, z, e, d)[0]], rbuf.at[y], b_send, b_recv, d - 1,
                   at_y(y, z, e, d)[1])
            for d in range(1, NY)
        ]

    def quarter(block):
        def value(b):
            return jnp.stack([dk_acc[block, b] * scale, dv_acc[block, b]])

        return value

    summed = [
        (lambda b: gg[b].astype(F32), lambda t: g_right.at[t], lambda t: g_left.at[t], gg_out),
        (lambda b: gu[b].astype(F32), lambda t: u_right.at[t], lambda t: u_left.at[t], gu_out),
        (lambda b: gd[b].astype(F32), lambda t: d_right.at[t], lambda t: d_left.at[t], gd_out),
    ]
    for block in range(NY):
        summed.append(
            (
                quarter(block),
                lambda t, block=block: kv_right.at[t, block],
                lambda t, block=block: kv_left.at[t, block],
                kv_sum.at[block],
            )
        )
    first = (
        lambda way: gg.at[lax.rem(z + (4, NZ - 3)[way], NZ)],
        lambda way: gu.at[lax.rem(z + (4, NZ - 3)[way], NZ)],
        lambda way: gd.at[lax.rem(z + (4, NZ - 3)[way], NZ)],
        lambda way: kv_first.at[0, way],
        lambda way: kv_first.at[1, way],
        lambda way: kv_first.at[2, way],
        lambda way: kv_first.at[3, way],
    )

    def to_right(index, step):
        buffer = summed[index][1]
        src = first[index](0) if step == 0 else buffer(step - 1)
        return remote(src, buffer(step), gr_send, gr_recv, index * 4 + step, right)

    def to_left(index, step):
        buffer = summed[index][2]
        src = first[index](1) if step == 0 else buffer(step - 1)
        return remote(src, buffer(step), gl_send, gl_recv, index * 3 + step, left)

    def ring_first(index):
        to_right(index, 0).start()
        to_left(index, 0).start()

    def ring_next(index, step):
        value, r_buffer, l_buffer, _ = summed[index]
        to_right(index, step - 1).wait_recv()
        got = r_buffer(step - 1)
        got[...] = (got[...].astype(F32) + value(lax.rem(z + 4 - step, NZ))).astype(BF)
        to_right(index, step).start()
        if step < 3:
            to_left(index, step - 1).wait_recv()
            got = l_buffer(step - 1)
            got[...] = (got[...].astype(F32) + value(lax.rem(z + NZ - 3 + step, NZ))).astype(BF)
            to_left(index, step).start()

    def ring_last(index):
        value, r_buffer, l_buffer, out = summed[index]
        to_right(index, 3).wait_recv()
        to_left(index, 2).wait_recv()
        out[...] = (
            value(z) + r_buffer(3)[...].astype(F32) + l_buffer(2)[...].astype(F32)
        ).astype(BF)

    def project():
        gather_step((0, 1, 2), 4)
        rows_in = xc[...].astype(F32)
        x = rows_in[:, :, :CAP, :].reshape(count, DS).astype(BF)
        c = rows_in[:, :, CAP:, :].reshape(count, DS).astype(BF)
        for index, (left_side, w) in enumerate(((x, wg_all), (x, wu_all), (c, wd_all))):
            product = dot(left_side, w[...].reshape(DS, FF), 1, 0)
            part[:, :, index * FF : (index + 1) * FF] = product.reshape(
                NY, NE * CAP, FF
            ).astype(BF)
        for copy in swaps():
            copy.start()

    def activate():
        for copy in swaps():
            copy.wait_recv()
        sums = part[y].astype(F32)
        for d in range(NY - 1):
            sums = sums + parts[d].astype(F32)
        gate_act = sums[:, :FF]
        up_act = sums[:, FF : 2 * FF]
        cot_down = sums[:, 2 * FF :]
        w = rows_own[:, :, D:].astype(F32)[:, :CAP, :].reshape(NE * CAP, 128)[:, :1]
        sigma = 1.0 / (1.0 + jnp.exp(-gate_act))
        silu = gate_act * sigma
        hidden = (silu * up_act).astype(BF).astype(F32)
        hidden_grad = w * cot_down
        act[y, :, :FF] = (
            hidden_grad * up_act * sigma * (1.0 + gate_act * (1.0 - sigma))
        ).astype(BF)
        act[y, :, FF : 2 * FF] = (hidden_grad * silu).astype(BF)
        act[y, :, 2 * FF :] = (w * hidden).astype(BF)
        for copy in spreads():
            copy.start()
        values = jnp.sum(hidden * cot_down, axis=1, keepdims=True)
        route[...] = jnp.broadcast_to(values, (NE * CAP, 128)).reshape(NE, CAP, 128)
        for copy in routes():
            copy.start()
        here(route.at[e], route_home.at[e], 9).start()

    def differentiate():
        for copy in spreads():
            copy.wait_recv()
        blocks = (NZ, WD, FF)
        act_all = act[...].reshape(count, 3 * FF)
        gate_pre = act_all[:, :FF]
        up_pre = act_all[:, FF : 2 * FF]
        gg[...] = dot(x_t[...], gate_pre, 1, 0).astype(BF).reshape(blocks)
        ring_first(0)
        gu[...] = dot(x_t[...], up_pre, 1, 0).astype(BF).reshape(blocks)
        ring_first(1)
        gd[...] = dot(c_t[...], act_all[:, 2 * FF :], 1, 0).astype(BF).reshape(blocks)
        ring_first(2)
        row_grad = dot(gate_pre, wg_all[...].reshape(DS, FF), 1, 1) + dot(
            up_pre, wu_all[...].reshape(DS, FF), 1, 1
        )
        row_grad = row_grad.reshape(NY, NE, CAP, DS)
        rb[...] = jnp.concatenate(
            [row_grad[:, :, :, i * 128 : (i + 1) * 128] for i in range(DS // 128)], axis=2
        ).astype(BF)
        for copy in row_swaps():
            copy.start()
        here(rb.at[y], rbuf.at[y], 10).start()

    def quarter_first(block):
        for way in range(2):
            b = lax.rem(z + (4, NZ - 3)[way], NZ)
            kv_first[block, way] = summed[3 + block][0](b).astype(BF)
        ring_first(3 + block)

    def q_home(block):
        return pltpu.make_async_remote_copy(
            src_ref=dq.at[block],
            dst_ref=dq_home.at[:, columns(y, GW)],
            send_sem=q_send.at[block],
            recv_sem=q_recv.at[y],
            device_id=(block * NZ + z, e),
            device_id_type=MESH,
        )

    def q_from(block):
        return pltpu.make_async_remote_copy(
            src_ref=dq.at[block],
            dst_ref=dq_home.at[:, block * GW : (block + 1) * GW],
            send_sem=q_send.at[block],
            recv_sem=q_recv.at[block],
            device_id=(block * NZ + z, e),
            device_id_type=MESH,
        )

    def send_q(block):
        pl.when(y != block)(lambda: q_home(block).start())

    def weights_next(step):
        for index in (0, 1, 2):
            ring_next(index, step)

    def mixed():
        differentiate()
        send_q(3)
        send_q(2)

    def second_end():
        ring_last(6)
        quarter_first(2)

    def third_end():
        ring_last(5)
        quarter_first(1)
        send_q(1)

    events = (
        (0, 0, lambda: gather_step((0, 1, 2), 2)),
        (0, 2, lambda: gather_step((0, 1, 2), 3)),
        (1, 1, project),
        (1, 2, lambda: quarter_first(3)),
        (2, 0, lambda: ring_next(6, 1)),
        (2, 2, activate),
        (3, 0, lambda: ring_next(6, 2)),
        (3, 1, lambda: ring_next(6, 3)),
        (3, 2, second_end),
        (4, 0, lambda: ring_next(5, 1)),
        (4, 2, mixed),
        (5, 0, lambda: ring_next(5, 2)),
        (5, 1, lambda: ring_next(5, 3)),
        (5, 2, third_end),
        (6, 0, lambda: weights_next(1)),
        (6, 1, lambda: ring_next(4, 1)),
        (7, 0, lambda: ring_next(4, 2)),
        (7, 1, lambda: weights_next(2)),
    )

    def work(i, carry):
        def event(sweep):
            for step, when, act_now in events:
                if when == sweep:
                    pl.when(i == step)(act_now)

        attend(NY - 1 - lax.div(i, 2), lax.rem(i, 2), event)
        return carry

    lax.fori_loop(0, STEPS, work, 0)
    quarter_first(0)
    send_q(0)
    own_q = here(dq.at[y], dq_home.at[:, columns(y, GW)], 11)
    own_q.start()

    def row_homes():
        return [
            remote(rbuf.at[:, at_e(y, z, e, d)[0]], back.at[e], i_send, i_recv, d - 1,
                   at_e(y, z, e, d)[1])
            for d in range(1, NE)
        ]

    here(rb.at[y], rbuf.at[y], 10).wait()
    for c in row_swaps():
        c.wait_recv()
    for c in row_homes():
        c.start()
    own_back = here(rbuf.at[:, e], back.at[e], 12)
    own_back.start()

    ring_next(4, 3)
    ring_next(3, 1)
    weights_next(3)
    ring_next(3, 2)
    ring_next(3, 3)
    ring_last(4)

    own_back.wait()
    for c in row_homes():
        c.wait_recv()
    pieces = back[...].astype(F32).reshape(NE, NY, DS // 128, CAP, 128)
    for block in range(NY):
        for i in range(DS // 128):
            piece = pieces[:, block, i].reshape(NE * CAP, 128).astype(BF)
            start = block * DS + i * 128
            input_grad[:, start : start + 128] = dot(dispatch[...], piece, 1, 0).astype(BF)

    def homes():
        copies = []
        for kind, out in enumerate((dk_home, dv_home)):
            target = out.at[:, columns(y, HEAD_SIZE)]
            for d in range(1, NY):
                peer, dev = at_y(y, z, e, d)
                copies.append(
                    remote(kv_sum.at[peer, kind], target, h_send, h_recv, kind * 3 + d - 1, dev)
                )
            copies.append(here(kv_sum.at[y, kind], target, 13 + kind))
        return copies

    here(route.at[e], route_home.at[e], 9).wait()
    for c in routes():
        c.wait()
    values = route_home[...].reshape(NE * CAP, 128)
    spread_values = dispatch[...].astype(F32).T * values.astype(BF).astype(F32)
    column = lax.broadcasted_iota(jnp.int32, (TOPK, TOK), 0)
    routed = jnp.zeros((TOPK, TOK), F32)
    for j in range(TOPK):
        total = jnp.sum(spread_values * named(j), axis=0, keepdims=True)
        routed += jnp.where(column == j, total, 0.0)
    route_grad[...] = routed.astype(BF)

    ring_last(3)
    for c in homes():
        c.start()
    for index in (0, 1, 2):
        ring_last(index)
    for c in homes():
        c.wait()
    for block in range(NY):
        pl.when(y != block)(lambda block=block: q_home(block).wait_send())
        pl.when(y != block)(lambda block=block: q_from(block).wait_recv())
    own_q.wait()
    for c in tokens() + kv_exchange() + q_exchange() + slices() + swaps() + spreads():
        c.wait_send()
    for c in row_swaps() + row_homes():
        c.wait_send()
    for index in range(5):
        for step in range(4):
            for c in gather(index, step):
                c.wait_send()
    for index in range(3 + NY):
        for step in range(4):
            to_right(index, step).wait_send()
            if step < 3:
                to_left(index, step).wait_send()


def layer(*arrays):
    sd = jax.ShapeDtypeStruct
    any_spec = pl.BlockSpec(memory_space=pl.ANY)
    vmem = pl.BlockSpec(memory_space=pltpu.VMEM)
    dma = pltpu.SemaphoreType.DMA
    scratch = pltpu.VMEM
    whole = (NY, NZ, TOK, HEAD_SIZE)
    length = NY * NZ * TOK
    slots = NE * CAP
    blocks = (NZ, WD, FF)
    rings = []
    pair = (2, TOK, HEAD_SIZE)
    for shape in ((NY,) + pair, (WD, FF), (WD, FF), (WD, FF)):
        rings += [scratch((4,) + shape, BF), scratch((3,) + shape, BF)]
    return pl.pallas_call(
        layer_kernel,
        out_shape=[
            sd((TOK, QUERY_HEADS * HEAD_SIZE), BF),
            sd((TOK, KEY_VALUE_HEADS * HEAD_SIZE), BF),
            sd((TOK, KEY_VALUE_HEADS * HEAD_SIZE), BF),
            sd((WD, FF), BF),
            sd((WD, FF), BF),
            sd((WD, FF), BF),
            sd((TOK, D), BF),
            sd((TOPK, TOK), BF),
        ],
        in_specs=[any_spec] * 7 + [vmem] * 4,
        out_specs=[any_spec] * 3 + [vmem] * 5,
        scratch_shapes=[
            scratch((NE, 16, D + 128), BF), scratch((TOK, slots), BF), scratch((NE, CAP, 128), F32),
            scratch((NY, TOK, GW), BF), scratch((NY, TOK, GW), BF),
            scratch(whole, BF), scratch(whole, BF), scratch((HEAD_SIZE, length), BF),
            scratch((ROWS, HEAD_SIZE), BF), scratch((ROWS, HEAD_SIZE), BF),
            scratch((length, ROWS), F32), scratch((length, ROWS), F32),
            scratch(whole, F32), scratch(whole, F32), scratch((HEAD_SIZE, ROWS), F32),
            scratch((NY, TOK, GW), BF),
            scratch((NE, 16, D + 128), BF), scratch((NY, NE, 16, DS), BF),
            scratch((DS, NY * slots), BF), scratch((DS, NY * slots), BF),
            scratch(blocks, BF), scratch(blocks, BF), scratch(blocks, BF),
            scratch((NY, slots, 3 * FF), BF), scratch((NY - 1, slots, 3 * FF), BF),
            scratch((NY, slots, 3 * FF), BF), scratch((NE, CAP, 128), F32),
            scratch((NY, NE, 32, 128), BF), scratch((NY, NE, 32, 128), BF),
            scratch((NE, NY, 32, 128), BF),
            scratch(blocks, BF), scratch(blocks, BF), scratch(blocks, BF),
        ]
        + rings
        + [
            scratch((NY, 2) + pair, BF), scratch((NY,) + pair, BF),
            dma((16,)), dma((12,)), dma((12,)), dma((7,)), dma((7,)), dma((3,)), dma((3,)),
            dma((20,)), dma((20,)), dma((15,)), dma((15,)),
            dma((3,)), dma((3,)), dma((3,)), dma((3,)), dma((7,)), dma((7,)),
            dma((4,)), dma((4,)), dma((3,)), dma((3,)), dma((7,)), dma((7,)), dma((6,)), dma((6,)),
            dma((28,)), dma((28,)), dma((21,)), dma((21,)),
        ],
        compiler_params=pltpu.CompilerParams(
            collective_id=0, has_side_effects=True, vmem_limit_bytes=VMEM_MOST
        ),
        name="layer",
    )(*arrays)


def finish_kernel(*refs):
    half = len(refs) // 2
    copies = [
        pltpu.make_async_copy(refs[i], refs[half + i], refs[-1].at[i]) for i in range(half)
    ]
    for c in copies:
        c.start()
    for c in copies:
        c.wait()


def finish(*arrays):
    any_spec = pl.BlockSpec(memory_space=pl.ANY)
    return pl.pallas_call(
        finish_kernel,
        out_shape=[jax.ShapeDtypeStruct(a.shape, a.dtype) for a in arrays],
        in_specs=[any_spec] * len(arrays),
        out_specs=[any_spec] * len(arrays),
        scratch_shapes=[pltpu.SemaphoreType.DMA((len(arrays),))],
        compiler_params=pltpu.CompilerParams(vmem_limit_bytes=VMEM_MOST),
        name="finish",
    )(*arrays)


def per_device(
    query_rows,
    key_matrix_all,
    value_matrix_all,
    context_grad,
    mixture_input,
    mixture_grad,
    expert_ids,
    route_weight,
    gate_weight,
    up_weight,
    down_weight,
):
    outputs = layer(
        query_rows[0], context_grad[0], key_matrix_all[0], value_matrix_all[0],
        gate_weight[0], up_weight[0], down_weight[0],
        mixture_input[0], mixture_grad[0], expert_ids[0].T, route_weight[0].T,
    )
    (
        dq_home, dk_home, dv_home, gate_grad, up_grad, down_grad, input_grad,
    ) = finish(*outputs[:7])
    route_grad = outputs[7].T
    return (
        dq_home[None],
        dk_home[None],
        dv_home[None],
        input_grad[None],
        route_grad[None],
        gate_grad[None],
        up_grad[None],
        down_grad[None],
    )


def solution(mesh):
    spec = P("exp", "ctx", None)
    return jax.shard_map(
        per_device,
        mesh=mesh,
        in_specs=(spec,) * 11,
        out_specs=(spec,) * 8,
        check_vma=False,
    )
```

```python
import math

import jax
import jax.numpy as jnp
from jax import lax
from jax.experimental import pallas as pl
from jax.experimental.pallas import tpu as pltpu
from jax.sharding import PartitionSpec as P

D = 2048
QUERY_HEADS = 32
KEY_VALUE_HEADS = 4
HEAD_SIZE = 128
FF = 768
EXPERTS = 128
TOPK = 8
CAP = 8
NY = 4
NZ = 8
NE = 8
TOK = 128
GW = QUERY_HEADS // KEY_VALUE_HEADS * HEAD_SIZE
DS = D // NY
WD = D // (NY * NZ)
KC = 512
HALF = 4
ROWS = HALF * TOK
STEPS = NY * (GW // (HALF * HEAD_SIZE))
MESH = pl.DeviceIdType.MESH
VMEM_MOST = 60 * 1024 * 1024
BF = jnp.bfloat16
F32 = jnp.float32


def places():
    ctx = lax.axis_index("ctx")
    return lax.div(ctx, NZ), lax.rem(ctx, NZ), lax.axis_index("exp")


def at_y(y, z, e, shift):
    peer = lax.rem(y + shift, NY)
    return peer, (peer * NZ + z, e)


def at_z(y, z, e, shift):
    peer = lax.rem(z + shift + NZ, NZ)
    return peer, (y * NZ + peer, e)


def at_e(y, z, e, shift):
    peer = lax.rem(e + shift, NE)
    return peer, (y * NZ + z, peer)


def greet(peers):
    barrier = pltpu.get_barrier_semaphore()
    for peer in peers:
        pl.semaphore_signal(barrier, inc=1, device_id=peer, device_id_type=MESH)
    pl.semaphore_wait(barrier, len(peers))


def remote(src, dst, send, recv, index, peer):
    return pltpu.make_async_remote_copy(
        src_ref=src,
        dst_ref=dst,
        send_sem=send.at[index],
        recv_sem=recv.at[index],
        device_id=peer,
        device_id_type=MESH,
    )


def columns(index, width):
    return pl.ds(pl.multiple_of(index * width, width), width)


def dot(a, b, left, right):
    return lax.dot_general(a, b, (((left,), (right,)), ((), ())), preferred_element_type=F32)


def layer_kernel(
    q, do, k, v, wg, wu, wd, x_in, c_in, ids, route_weight,
    dq_home, dk_home, dv_home, gg_out, gu_out, gd_out, input_grad, route_grad,
    rows, dispatch, route_home,
    q_all, do_all, k_all, v_all, kt, q_st, do_st, s_scr, g_scr, dk_acc, dv_acc, dqt, dq,
    rows_own, xc, x_t, c_t, wg_all, wu_all, wd_all, part, parts, act, route,
    rb, rbuf, back, gg, gu, gd,
    kv_right, kv_left, g_right, g_left, u_right, u_left, d_right, d_left, kv_first, kv_sum,
    local_sem, y_send, y_recv, e_send, e_recv, x_send, x_recv, r_send, r_recv, l_send, l_recv,
    s_send, s_recv, a_send, a_recv, t_send, t_recv, q_send, q_recv, b_send, b_recv,
    i_send, i_recv, h_send, h_recv, gr_send, gr_recv, gl_send, gl_recv,
):
    y, z, e = places()
    count = NY * NE * CAP
    scale = 1.0 / math.sqrt(HEAD_SIZE)
    factor = scale * math.log2(math.e)
    greet(
        [at_y(y, z, e, d)[1] for d in range(1, NY)]
        + [at_z(y, z, e, d)[1] for d in (1, -1)]
        + [at_e(y, z, e, d)[1] for d in range(1, NE)]
    )
    right = at_z(y, z, e, 1)[1]
    left = at_z(y, z, e, -1)[1]

    def tokens():
        return [
            remote(rows.at[at_e(y, z, e, d)[0]], rows_own.at[e], e_send, e_recv, d - 1,
                   at_e(y, z, e, d)[1])
            for d in range(1, NE)
        ]

    def slices():
        return [
            remote(rows_own.at[:, :, columns(at_y(y, z, e, d)[0], DS)], xc.at[y], x_send, x_recv,
                   d - 1, at_y(y, z, e, d)[1])
            for d in range(1, NY)
        ]

    def y_exchange(src, target, width, base):
        return [
            remote(src.at[:, columns(at_y(y, z, e, d)[0], width)], target, y_send, y_recv,
                   base + d - 1, at_y(y, z, e, d)[1])
            for d in range(1, NY)
        ]

    def kv_exchange():
        return y_exchange(k, k_all.at[y, z], HEAD_SIZE, 0) + y_exchange(
            v, v_all.at[y, z], HEAD_SIZE, 3
        )

    def q_exchange():
        return y_exchange(q, q_all.at[y], GW, 6) + y_exchange(do, do_all.at[y], GW, 9)

    gathered = (
        lambda b: wg_all.at[b],
        lambda b: wu_all.at[b],
        lambda b: wd_all.at[b],
        lambda b: k_all.at[:, b],
        lambda b: v_all.at[:, b],
    )

    def gather(index, step):
        block = gathered[index]
        here = block(lax.rem(z - step + NZ, NZ))
        pair = [remote(here, here, r_send, r_recv, index * 4 + step, right)]
        if step < 3:
            there = block(lax.rem(z + step, NZ))
            pair.append(remote(there, there, l_send, l_recv, index * 3 + step, left))
        return pair

    def gather_step(indices, step):
        for index in indices:
            if step > 0:
                for c in gather(index, step - 1):
                    c.wait_recv()
            if step < 4:
                for c in gather(index, step):
                    c.start()

    def here(src, dst, index):
        return pltpu.make_async_copy(src, dst, local_sem.at[index])

    for c in kv_exchange():
        c.start()
    own = [
        here(k.at[:, columns(y, HEAD_SIZE)], k_all.at[y, z], 1),
        here(v.at[:, columns(y, HEAD_SIZE)], v_all.at[y, z], 2),
        here(q.at[:, columns(y, GW)], q_all.at[y], 3),
        here(do.at[:, columns(y, GW)], do_all.at[y], 4),
        here(wg, wg_all.at[z], 5),
        here(wu, wu_all.at[z], 6),
        here(wd, wd_all.at[z], 7),
    ]
    for c in own:
        c.start()
    for c in own[4:]:
        c.wait()
    gather_step((0, 1, 2), 0)

    slot = lax.broadcasted_iota(jnp.int32, (NE * CAP, TOK), 0)
    expert = lax.div(slot, CAP) * (EXPERTS // NE)

    def named(j):
        return (ids[j : j + 1, :] == expert).astype(F32)

    combine = route_weight[...].astype(F32)
    taken = jnp.zeros((NE * CAP, TOK), F32)
    weights = jnp.zeros((NE * CAP, TOK), F32)
    for j in range(TOPK):
        hit = named(j)
        taken += hit
        weights += hit * combine[j : j + 1, :]
    earlier = (
        lax.broadcasted_iota(jnp.int32, (TOK, TOK), 0)
        < lax.broadcasted_iota(jnp.int32, (TOK, TOK), 1)
    ).astype(F32)
    place = dot(taken.astype(BF), earlier.astype(BF), 1, 0)
    placed = taken * (place == lax.rem(slot, CAP).astype(F32)).astype(F32)
    dispatch[...] = placed.T.astype(BF)
    collect = placed.astype(BF)
    rows[:, :, :D] = jnp.concatenate(
        [dot(collect, r[...], 1, 0).reshape(NE, CAP, D) for r in (x_in, c_in)], axis=1
    ).astype(BF)
    weight_col = jnp.sum(placed * weights, axis=1, keepdims=True)
    weight_col = jnp.broadcast_to(weight_col, (NE * CAP, 128)).reshape(NE, CAP, 128)
    rows[:, :, D:] = jnp.concatenate([weight_col, weight_col], axis=1).astype(BF)
    for c in tokens():
        c.start()
    own_rows = here(rows.at[e], rows_own.at[e], 0)
    own_rows.start()

    gather_step((0, 1, 2), 1)
    for c in tokens():
        c.wait_recv()
    own_rows.wait()
    for c in slices():
        c.start()
    own_xc = here(rows_own.at[:, :, columns(y, DS)], xc.at[y], 8)
    own_xc.start()
    for c in q_exchange():
        c.start()
    gather_step((0, 1, 2), 2)
    for c in kv_exchange():
        c.wait_recv()
    for c in own[:4]:
        c.wait()
    dk_acc[...] = jnp.zeros_like(dk_acc)
    dv_acc[...] = jnp.zeros_like(dv_acc)
    gather_step((0, 1, 2), 3)
    gather_step((3, 4), 0)
    own_xc.wait()
    for c in slices():
        c.wait_recv()
    both = xc[...].astype(F32)
    x_t[...] = both[:, :, :CAP, :].reshape(count, DS).T.astype(BF)
    c_t[...] = both[:, :, CAP:, :].reshape(count, DS).T.astype(BF)

    def chunk(c):
        per = NZ * TOK // KC
        return lax.div(c, per), pl.ds(lax.rem(c, per) * (KC // TOK), KC // TOK)

    def chunk_rows(ref, c):
        a, b = chunk(c)
        return ref[a, b].reshape(KC, HEAD_SIZE)

    def at(c):
        return pl.ds(pl.multiple_of(c * KC, KC), KC)

    def turn(c, carry):
        kt[:, at(c)] = chunk_rows(k_all, c).astype(F32).T.astype(BF)
        return carry

    def fold(values, op):
        return op(values.reshape(KC // 8, 8, ROWS), axis=0)

    def attend(block, half, event):
        position = block * NZ + z
        chunks = lax.div(position * TOK + TOK + KC - 1, KC)
        for h in range(HALF):
            cols = pl.ds(
                pl.multiple_of(half * (HALF * HEAD_SIZE) + h * HEAD_SIZE, HEAD_SIZE), HEAD_SIZE
            )
            q_st[h * TOK : (h + 1) * TOK, :] = q_all[block, :, cols]
            do_st[h * TOK : (h + 1) * TOK, :] = do_all[block, :, cols]

        def scores(c, peak, masked):
            s = dot(chunk_rows(k_all, c), q_st[...], 1, 1) * factor
            if masked:
                key_pos = c * KC + lax.broadcasted_iota(jnp.int32, (KC, ROWS), 0)
                query_pos = position * TOK + lax.rem(
                    lax.broadcasted_iota(jnp.int32, (KC, ROWS), 1), TOK
                )
                s = jnp.where(key_pos <= query_pos, s, -1e30)
            s_scr[at(c), :] = s
            return jnp.maximum(peak, fold(s, jnp.max))

        peak = lax.fori_loop(
            0, chunks - 1, lambda c, m: scores(c, m, False), jnp.full((8, ROWS), -1e30, F32)
        )
        peak = scores(chunks - 1, peak, True)
        peak = jnp.max(peak, axis=0, keepdims=True)
        event(0)

        def weigh(c, carry):
            total, paired = carry
            p = jnp.exp2(s_scr[at(c), :] - peak)
            g = dot(chunk_rows(v_all, c), do_st[...], 1, 1)
            s_scr[at(c), :] = p
            g_scr[at(c), :] = g
            return total + fold(p, jnp.sum), paired + fold(p * g, jnp.sum)

        zero = jnp.zeros((8, ROWS), F32)
        total, paired = lax.fori_loop(0, chunks, weigh, (zero, zero))
        inverse = 1.0 / jnp.sum(total, axis=0, keepdims=True)
        row_dot = jnp.sum(paired, axis=0, keepdims=True) * inverse
        event(1)

        dqt[...] = jnp.zeros_like(dqt)

        def gradients(c, carry):
            a, b = chunk(c)
            p = s_scr[at(c), :] * inverse
            ds = (p * (g_scr[at(c), :] - row_dot)).astype(BF)
            shape = (KC // TOK, TOK, HEAD_SIZE)
            dv_acc[a, b] += dot(p.astype(BF), do_st[...], 1, 0).reshape(shape)
            dk_acc[a, b] += dot(ds, q_st[...], 1, 0).reshape(shape)
            dqt[...] += dot(kt[:, at(c)], ds, 1, 0)
            return carry

        lax.fori_loop(0, chunks, gradients, 0)
        for h in range(HALF):
            cols = pl.ds(
                pl.multiple_of(half * (HALF * HEAD_SIZE) + h * HEAD_SIZE, HEAD_SIZE), HEAD_SIZE
            )
            dq[block, :, cols] = (dqt[:, h * TOK : (h + 1) * TOK] * scale).T.astype(BF)
        event(2)

    def swaps():
        return [
            remote(part.at[at_y(y, z, e, d)[0]], parts.at[d - 1], s_send, s_recv, d - 1,
                   at_y(y, z, e, d)[1])
            for d in range(1, NY)
        ]

    def spreads():
        return [
            remote(act.at[y], act.at[y], a_send, a_recv, d - 1, at_y(y, z, e, d)[1])
            for d in range(1, NY)
        ]

    def routes():
        return [
            remote(route.at[at_e(y, z, e, d)[0]], route_home.at[e], t_send, t_recv, d - 1,
                   at_e(y, z, e, d)[1])
            for d in range(1, NE)
        ]

    def row_swaps():
        return [
            remote(rb.at[at_y(y, z, e, d)[0]], rbuf.at[y], b_send, b_recv, d - 1,
                   at_y(y, z, e, d)[1])
            for d in range(1, NY)
        ]

    def quarter(block):
        def value(b):
            return jnp.stack([dk_acc[block, b] * scale, dv_acc[block, b]])

        return value

    summed = [
        (lambda b: gg[b].astype(F32), lambda t: g_right.at[t], lambda t: g_left.at[t], gg_out),
        (lambda b: gu[b].astype(F32), lambda t: u_right.at[t], lambda t: u_left.at[t], gu_out),
        (lambda b: gd[b].astype(F32), lambda t: d_right.at[t], lambda t: d_left.at[t], gd_out),
    ]
    for block in range(NY):
        summed.append(
            (
                quarter(block),
                lambda t, block=block: kv_right.at[t, block],
                lambda t, block=block: kv_left.at[t, block],
                kv_sum.at[block],
            )
        )
    first = (
        lambda way: gg.at[lax.rem(z + (4, NZ - 3)[way], NZ)],
        lambda way: gu.at[lax.rem(z + (4, NZ - 3)[way], NZ)],
        lambda way: gd.at[lax.rem(z + (4, NZ - 3)[way], NZ)],
        lambda way: kv_first.at[0, way],
        lambda way: kv_first.at[1, way],
        lambda way: kv_first.at[2, way],
        lambda way: kv_first.at[3, way],
    )

    def to_right(index, step):
        buffer = summed[index][1]
        src = first[index](0) if step == 0 else buffer(step - 1)
        return remote(src, buffer(step), gr_send, gr_recv, index * 4 + step, right)

    def to_left(index, step):
        buffer = summed[index][2]
        src = first[index](1) if step == 0 else buffer(step - 1)
        return remote(src, buffer(step), gl_send, gl_recv, index * 3 + step, left)

    def ring_first(index):
        to_right(index, 0).start()
        to_left(index, 0).start()

    def ring_next(index, step):
        value, r_buffer, l_buffer, _ = summed[index]
        to_right(index, step - 1).wait_recv()
        got = r_buffer(step - 1)
        got[...] = (got[...].astype(F32) + value(lax.rem(z + 4 - step, NZ))).astype(BF)
        to_right(index, step).start()
        if step < 3:
            to_left(index, step - 1).wait_recv()
            got = l_buffer(step - 1)
            got[...] = (got[...].astype(F32) + value(lax.rem(z + NZ - 3 + step, NZ))).astype(BF)
            to_left(index, step).start()

    def ring_last(index):
        value, r_buffer, l_buffer, out = summed[index]
        to_right(index, 3).wait_recv()
        to_left(index, 2).wait_recv()
        out[...] = (
            value(z) + r_buffer(3)[...].astype(F32) + l_buffer(2)[...].astype(F32)
        ).astype(BF)

    def project():
        gather_step((0, 1, 2), 4)
        rows_in = xc[...].astype(F32)
        x = rows_in[:, :, :CAP, :].reshape(count, DS).astype(BF)
        c = rows_in[:, :, CAP:, :].reshape(count, DS).astype(BF)
        for index, (left_side, w) in enumerate(((x, wg_all), (x, wu_all), (c, wd_all))):
            product = dot(left_side, w[...].reshape(DS, FF), 1, 0)
            part[:, :, index * FF : (index + 1) * FF] = product.reshape(
                NY, NE * CAP, FF
            ).astype(BF)
        for copy in swaps():
            copy.start()

    def activate():
        for copy in swaps():
            copy.wait_recv()
        sums = part[y].astype(F32)
        for d in range(NY - 1):
            sums = sums + parts[d].astype(F32)
        gate_act = sums[:, :FF]
        up_act = sums[:, FF : 2 * FF]
        cot_down = sums[:, 2 * FF :]
        w = rows_own[:, :, D:].astype(F32)[:, :CAP, :].reshape(NE * CAP, 128)[:, :1]
        sigma = 1.0 / (1.0 + jnp.exp(-gate_act))
        silu = gate_act * sigma
        hidden = (silu * up_act).astype(BF).astype(F32)
        hidden_grad = w * cot_down
        act[y, :, :FF] = (
            hidden_grad * up_act * sigma * (1.0 + gate_act * (1.0 - sigma))
        ).astype(BF)
        act[y, :, FF : 2 * FF] = (hidden_grad * silu).astype(BF)
        act[y, :, 2 * FF :] = (w * hidden).astype(BF)
        for copy in spreads():
            copy.start()
        values = jnp.sum(hidden * cot_down, axis=1, keepdims=True)
        route[...] = jnp.broadcast_to(values, (NE * CAP, 128)).reshape(NE, CAP, 128)
        for copy in routes():
            copy.start()
        here(route.at[e], route_home.at[e], 9).start()

    def differentiate():
        for copy in spreads():
            copy.wait_recv()
        blocks = (NZ, WD, FF)
        act_all = act[...].reshape(count, 3 * FF)
        gate_pre = act_all[:, :FF]
        up_pre = act_all[:, FF : 2 * FF]
        gg[...] = dot(x_t[...], gate_pre, 1, 0).astype(BF).reshape(blocks)
        ring_first(0)
        gu[...] = dot(x_t[...], up_pre, 1, 0).astype(BF).reshape(blocks)
        ring_first(1)
        gd[...] = dot(c_t[...], act_all[:, 2 * FF :], 1, 0).astype(BF).reshape(blocks)
        ring_first(2)
        row_grad = dot(gate_pre, wg_all[...].reshape(DS, FF), 1, 1) + dot(
            up_pre, wu_all[...].reshape(DS, FF), 1, 1
        )
        row_grad = row_grad.reshape(NY, NE, CAP, DS)
        rb[...] = jnp.concatenate(
            [row_grad[:, :, :, i * 128 : (i + 1) * 128] for i in range(DS // 128)], axis=2
        ).astype(BF)
        for copy in row_swaps():
            copy.start()
        here(rb.at[y], rbuf.at[y], 10).start()

    def quarter_first(block):
        for way in range(2):
            b = lax.rem(z + (4, NZ - 3)[way], NZ)
            kv_first[block, way] = summed[3 + block][0](b).astype(BF)
        ring_first(3 + block)

    def q_home(block):
        return pltpu.make_async_remote_copy(
            src_ref=dq.at[block],
            dst_ref=dq_home.at[:, columns(y, GW)],
            send_sem=q_send.at[block],
            recv_sem=q_recv.at[y],
            device_id=(block * NZ + z, e),
            device_id_type=MESH,
        )

    def q_from(block):
        return pltpu.make_async_remote_copy(
            src_ref=dq.at[block],
            dst_ref=dq_home.at[:, block * GW : (block + 1) * GW],
            send_sem=q_send.at[block],
            recv_sem=q_recv.at[block],
            device_id=(block * NZ + z, e),
            device_id_type=MESH,
        )

    def send_q(block):
        pl.when(y != block)(lambda: q_home(block).start())

    def weights_next(step):
        for index in (0, 1, 2):
            ring_next(index, step)

    def row_homes():
        return [
            remote(rbuf.at[:, at_e(y, z, e, d)[0]], back.at[e], i_send, i_recv, d - 1,
                   at_e(y, z, e, d)[1])
            for d in range(1, NE)
        ]

    def rows_home():
        here(rb.at[y], rbuf.at[y], 10).wait()
        for c in row_swaps():
            c.wait_recv()
        for c in row_homes():
            c.start()
        here(rbuf.at[:, e], back.at[e], 12).start()

    def block_end(block):
        if block < NY - 1:
            ring_last(3 + block + 1)
        quarter_first(block)
        send_q(block)

    events = (
        (0, 0, differentiate),
        (0, 2, lambda: weights_next(1)),
        (1, 1, lambda: weights_next(2)),
        (1, 2, lambda: block_end(3)),
        (2, 0, lambda: weights_next(3)),
        (2, 1, lambda: ring_next(6, 1)),
        (2, 2, lambda: ring_next(6, 2)),
        (3, 0, lambda: ring_next(6, 3)),
        (3, 1, rows_home),
        (3, 2, lambda: block_end(2)),
        (4, 0, lambda: ring_next(5, 1)),
        (4, 2, lambda: ring_next(5, 2)),
        (5, 0, lambda: ring_next(5, 3)),
        (5, 2, lambda: block_end(1)),
        (6, 0, lambda: ring_next(4, 1)),
        (6, 2, lambda: ring_next(4, 2)),
        (7, 1, lambda: ring_next(4, 3)),
    )

    project()
    gather_step((3, 4), 1)
    gather_step((3, 4), 2)
    activate()
    gather_step((3, 4), 3)
    gather_step((3, 4), 4)
    for c in q_exchange():
        c.wait_recv()
    lax.fori_loop(0, NY * NZ * TOK // KC, turn, 0)

    def work(i, carry):
        def event(sweep):
            for step, when, act_now in events:
                if when == sweep:
                    pl.when(i == step)(act_now)

        attend(NY - 1 - lax.div(i, 2), lax.rem(i, 2), event)
        return carry

    lax.fori_loop(0, STEPS, work, 0)
    quarter_first(0)
    send_q(0)
    own_q = here(dq.at[y], dq_home.at[:, columns(y, GW)], 11)
    own_q.start()

    ring_next(3, 1)
    here(rbuf.at[:, e], back.at[e], 12).wait()
    for c in row_homes():
        c.wait_recv()
    pieces = back[...].astype(F32).reshape(NE, NY, DS // 128, CAP, 128)
    for block in range(NY):
        for i in range(DS // 128):
            piece = pieces[:, block, i].reshape(NE * CAP, 128).astype(BF)
            start = block * DS + i * 128
            input_grad[:, start : start + 128] = dot(dispatch[...], piece, 1, 0).astype(BF)
    ring_next(3, 2)

    def homes():
        copies = []
        for kind, out in enumerate((dk_home, dv_home)):
            target = out.at[:, columns(y, HEAD_SIZE)]
            for d in range(1, NY):
                peer, dev = at_y(y, z, e, d)
                copies.append(
                    remote(kv_sum.at[peer, kind], target, h_send, h_recv, kind * 3 + d - 1, dev)
                )
            copies.append(here(kv_sum.at[y, kind], target, 13 + kind))
        return copies

    here(route.at[e], route_home.at[e], 9).wait()
    for c in routes():
        c.wait()
    values = route_home[...].reshape(NE * CAP, 128)
    spread_values = dispatch[...].astype(F32).T * values.astype(BF).astype(F32)
    column = lax.broadcasted_iota(jnp.int32, (TOPK, TOK), 0)
    routed = jnp.zeros((TOPK, TOK), F32)
    for j in range(TOPK):
        total = jnp.sum(spread_values * named(j), axis=0, keepdims=True)
        routed += jnp.where(column == j, total, 0.0)
    route_grad[...] = routed.astype(BF)

    ring_next(3, 3)
    for index in (0, 1, 2, 4):
        ring_last(index)
    ring_last(3)
    for c in homes():
        c.start()
    for c in homes():
        c.wait()
    for block in range(NY):
        pl.when(y != block)(lambda block=block: q_home(block).wait_send())
        pl.when(y != block)(lambda block=block: q_from(block).wait_recv())
    own_q.wait()
    for c in tokens() + kv_exchange() + q_exchange() + slices() + swaps() + spreads():
        c.wait_send()
    for c in row_swaps() + row_homes():
        c.wait_send()
    for index in range(5):
        for step in range(4):
            for c in gather(index, step):
                c.wait_send()
    for index in range(3 + NY):
        for step in range(4):
            to_right(index, step).wait_send()
            if step < 3:
                to_left(index, step).wait_send()


def layer(*arrays):
    sd = jax.ShapeDtypeStruct
    any_spec = pl.BlockSpec(memory_space=pl.ANY)
    vmem = pl.BlockSpec(memory_space=pltpu.VMEM)
    dma = pltpu.SemaphoreType.DMA
    scratch = pltpu.VMEM
    whole = (NY, NZ, TOK, HEAD_SIZE)
    length = NY * NZ * TOK
    slots = NE * CAP
    blocks = (NZ, WD, FF)
    rings = []
    pair = (2, TOK, HEAD_SIZE)
    for shape in ((NY,) + pair, (WD, FF), (WD, FF), (WD, FF)):
        rings += [scratch((4,) + shape, BF), scratch((3,) + shape, BF)]
    return pl.pallas_call(
        layer_kernel,
        out_shape=[
            sd((TOK, QUERY_HEADS * HEAD_SIZE), BF),
            sd((TOK, KEY_VALUE_HEADS * HEAD_SIZE), BF),
            sd((TOK, KEY_VALUE_HEADS * HEAD_SIZE), BF),
            sd((WD, FF), BF),
            sd((WD, FF), BF),
            sd((WD, FF), BF),
            sd((TOK, D), BF),
            sd((TOPK, TOK), BF),
        ],
        in_specs=[any_spec] * 7 + [vmem] * 4,
        out_specs=[any_spec] * 3 + [vmem] * 5,
        scratch_shapes=[
            scratch((NE, 16, D + 128), BF), scratch((TOK, slots), BF), scratch((NE, CAP, 128), F32),
            scratch((NY, TOK, GW), BF), scratch((NY, TOK, GW), BF),
            scratch(whole, BF), scratch(whole, BF), scratch((HEAD_SIZE, length), BF),
            scratch((ROWS, HEAD_SIZE), BF), scratch((ROWS, HEAD_SIZE), BF),
            scratch((length, ROWS), F32), scratch((length, ROWS), F32),
            scratch(whole, F32), scratch(whole, F32), scratch((HEAD_SIZE, ROWS), F32),
            scratch((NY, TOK, GW), BF),
            scratch((NE, 16, D + 128), BF), scratch((NY, NE, 16, DS), BF),
            scratch((DS, NY * slots), BF), scratch((DS, NY * slots), BF),
            scratch(blocks, BF), scratch(blocks, BF), scratch(blocks, BF),
            scratch((NY, slots, 3 * FF), BF), scratch((NY - 1, slots, 3 * FF), BF),
            scratch((NY, slots, 3 * FF), BF), scratch((NE, CAP, 128), F32),
            scratch((NY, NE, 32, 128), BF), scratch((NY, NE, 32, 128), BF),
            scratch((NE, NY, 32, 128), BF),
            scratch(blocks, BF), scratch(blocks, BF), scratch(blocks, BF),
        ]
        + rings
        + [
            scratch((NY, 2) + pair, BF), scratch((NY,) + pair, BF),
            dma((16,)), dma((12,)), dma((12,)), dma((7,)), dma((7,)), dma((3,)), dma((3,)),
            dma((20,)), dma((20,)), dma((15,)), dma((15,)),
            dma((3,)), dma((3,)), dma((3,)), dma((3,)), dma((7,)), dma((7,)),
            dma((4,)), dma((4,)), dma((3,)), dma((3,)), dma((7,)), dma((7,)), dma((6,)), dma((6,)),
            dma((28,)), dma((28,)), dma((21,)), dma((21,)),
        ],
        compiler_params=pltpu.CompilerParams(
            collective_id=0, has_side_effects=True, vmem_limit_bytes=VMEM_MOST
        ),
        name="layer",
    )(*arrays)


def finish_kernel(*refs):
    half = (len(refs) - 2) // 3
    held = refs[2 * half : 3 * half]
    arriving = [
        pltpu.make_async_copy(refs[i], held[i], refs[-2].at[i]) for i in range(half)
    ]
    leaving = [
        pltpu.make_async_copy(held[i], refs[half + i], refs[-1].at[i]) for i in range(half)
    ]
    for c in arriving:
        c.start()
    for first, second in zip(arriving, leaving):
        first.wait()
        second.start()
    for c in leaving:
        c.wait()


def finish(*arrays):
    any_spec = pl.BlockSpec(memory_space=pl.ANY)
    dma = pltpu.SemaphoreType.DMA
    return pl.pallas_call(
        finish_kernel,
        out_shape=[jax.ShapeDtypeStruct(a.shape, a.dtype) for a in arrays],
        in_specs=[any_spec] * len(arrays),
        out_specs=[any_spec] * len(arrays),
        scratch_shapes=[pltpu.VMEM(a.shape, a.dtype) for a in arrays]
        + [dma((len(arrays),)), dma((len(arrays),))],
        compiler_params=pltpu.CompilerParams(vmem_limit_bytes=VMEM_MOST),
        name="finish",
    )(*arrays)


def per_device(
    query_rows,
    key_matrix_all,
    value_matrix_all,
    context_grad,
    mixture_input,
    mixture_grad,
    expert_ids,
    route_weight,
    gate_weight,
    up_weight,
    down_weight,
):
    outputs = layer(
        query_rows[0], context_grad[0], key_matrix_all[0], value_matrix_all[0],
        gate_weight[0], up_weight[0], down_weight[0],
        mixture_input[0], mixture_grad[0], expert_ids[0].T, route_weight[0].T,
    )
    (
        dq_home, dk_home, dv_home, gate_grad, up_grad, down_grad, input_grad,
    ) = finish(*outputs[:7])
    route_grad = outputs[7].T
    return (
        dq_home[None],
        dk_home[None],
        dv_home[None],
        input_grad[None],
        route_grad[None],
        gate_grad[None],
        up_grad[None],
        down_grad[None],
    )


def solution(mesh):
    spec = P("exp", "ctx", None)
    return jax.shard_map(
        per_device,
        mesh=mesh,
        in_specs=(spec,) * 11,
        out_specs=(spec,) * 8,
        check_vma=False,
    )
```

```python
import math

import jax
import jax.numpy as jnp
from jax import lax
from jax.experimental import pallas as pl
from jax.experimental.pallas import tpu as pltpu
from jax.sharding import PartitionSpec as P

D = 2048
QUERY_HEADS = 32
KEY_VALUE_HEADS = 4
HEAD_SIZE = 128
FF = 768
EXPERTS = 128
TOPK = 8
CAP = 8
NY = 4
NZ = 8
NE = 8
TOK = 128
GW = QUERY_HEADS // KEY_VALUE_HEADS * HEAD_SIZE
DS = D // NY
WD = D // (NY * NZ)
KC = 512
HALF = 4
ROWS = HALF * TOK
STEPS = NY * (GW // (HALF * HEAD_SIZE))
MESH = pl.DeviceIdType.MESH
VMEM_MOST = 60 * 1024 * 1024
BF = jnp.bfloat16
F32 = jnp.float32


def places():
    ctx = lax.axis_index("ctx")
    return lax.div(ctx, NZ), lax.rem(ctx, NZ), lax.axis_index("exp")


def at_y(y, z, e, shift):
    peer = lax.rem(y + shift, NY)
    return peer, (peer * NZ + z, e)


def at_z(y, z, e, shift):
    peer = lax.rem(z + shift + NZ, NZ)
    return peer, (y * NZ + peer, e)


def at_e(y, z, e, shift):
    peer = lax.rem(e + shift, NE)
    return peer, (y * NZ + z, peer)


def greet(peers):
    barrier = pltpu.get_barrier_semaphore()
    for peer in peers:
        pl.semaphore_signal(barrier, inc=1, device_id=peer, device_id_type=MESH)
    pl.semaphore_wait(barrier, len(peers))


def remote(src, dst, send, recv, index, peer):
    return pltpu.make_async_remote_copy(
        src_ref=src,
        dst_ref=dst,
        send_sem=send.at[index],
        recv_sem=recv.at[index],
        device_id=peer,
        device_id_type=MESH,
    )


def columns(index, width):
    return pl.ds(pl.multiple_of(index * width, width), width)


def dot(a, b, left, right):
    return lax.dot_general(a, b, (((left,), (right,)), ((), ())), preferred_element_type=F32)


def layer_kernel(
    q, do, k, v, wg, wu, wd, x_in, c_in, ids, route_weight,
    dq_home, dk_home, dv_home, gg_out, gu_out, gd_out, input_grad, route_grad,
    rows, dispatch, route_home,
    q_all, do_all, k_all, v_all, kt, q_st, do_st, s_scr, g_scr, dk_acc, dv_acc, dqt, dq,
    rows_own, xc, x_t, c_t, wg_all, wu_all, wd_all, part, parts, act, route,
    rb, rbuf, back, gg, gu, gd,
    kv_right, kv_left, g_right, g_left, u_right, u_left, d_right, d_left, kv_first, kv_sum,
    local_sem, y_send, y_recv, e_send, e_recv, x_send, x_recv, r_send, r_recv, l_send, l_recv,
    s_send, s_recv, a_send, a_recv, t_send, t_recv, q_send, q_recv, b_send, b_recv,
    i_send, i_recv, h_send, h_recv, gr_send, gr_recv, gl_send, gl_recv,
):
    y, z, e = places()
    count = NY * NE * CAP
    scale = 1.0 / math.sqrt(HEAD_SIZE)
    factor = scale * math.log2(math.e)
    greet(
        [at_y(y, z, e, d)[1] for d in range(1, NY)]
        + [at_z(y, z, e, d)[1] for d in (1, -1)]
        + [at_e(y, z, e, d)[1] for d in range(1, NE)]
    )
    right = at_z(y, z, e, 1)[1]
    left = at_z(y, z, e, -1)[1]

    def tokens():
        return [
            remote(rows.at[at_e(y, z, e, d)[0]], rows_own.at[e], e_send, e_recv, d - 1,
                   at_e(y, z, e, d)[1])
            for d in range(1, NE)
        ]

    def slices():
        return [
            remote(rows_own.at[:, :, columns(at_y(y, z, e, d)[0], DS)], xc.at[y], x_send, x_recv,
                   d - 1, at_y(y, z, e, d)[1])
            for d in range(1, NY)
        ]

    def y_exchange(src, target, width, base):
        return [
            remote(src.at[:, columns(at_y(y, z, e, d)[0], width)], target, y_send, y_recv,
                   base + d - 1, at_y(y, z, e, d)[1])
            for d in range(1, NY)
        ]

    def kv_exchange():
        return y_exchange(k, k_all.at[y, z], HEAD_SIZE, 0) + y_exchange(
            v, v_all.at[y, z], HEAD_SIZE, 3
        )

    def q_exchange():
        return y_exchange(q, q_all.at[y], GW, 6) + y_exchange(do, do_all.at[y], GW, 9)

    gathered = (
        lambda b: wg_all.at[b],
        lambda b: wu_all.at[b],
        lambda b: wd_all.at[b],
        lambda b: k_all.at[:, b],
        lambda b: v_all.at[:, b],
    )

    def gather(index, step):
        block = gathered[index]
        here = block(lax.rem(z - step + NZ, NZ))
        pair = [remote(here, here, r_send, r_recv, index * 4 + step, right)]
        if step < 3:
            there = block(lax.rem(z + step, NZ))
            pair.append(remote(there, there, l_send, l_recv, index * 3 + step, left))
        return pair

    def gather_step(indices, step):
        for index in indices:
            if step > 0:
                for c in gather(index, step - 1):
                    c.wait_recv()
            if step < 4:
                for c in gather(index, step):
                    c.start()

    def here(src, dst, index):
        return pltpu.make_async_copy(src, dst, local_sem.at[index])

    for c in kv_exchange():
        c.start()
    own = [
        here(k.at[:, columns(y, HEAD_SIZE)], k_all.at[y, z], 1),
        here(v.at[:, columns(y, HEAD_SIZE)], v_all.at[y, z], 2),
        here(q.at[:, columns(y, GW)], q_all.at[y], 3),
        here(do.at[:, columns(y, GW)], do_all.at[y], 4),
        here(wg, wg_all.at[z], 5),
        here(wu, wu_all.at[z], 6),
        here(wd, wd_all.at[z], 7),
    ]
    for c in own:
        c.start()
    for c in own[4:]:
        c.wait()
    gather_step((0, 1, 2), 0)

    slot = lax.broadcasted_iota(jnp.int32, (NE * CAP, TOK), 0)
    expert = lax.div(slot, CAP) * (EXPERTS // NE)

    def named(j):
        return (ids[j : j + 1, :] == expert).astype(F32)

    combine = route_weight[...].astype(F32)
    taken = jnp.zeros((NE * CAP, TOK), F32)
    weights = jnp.zeros((NE * CAP, TOK), F32)
    for j in range(TOPK):
        hit = named(j)
        taken += hit
        weights += hit * combine[j : j + 1, :]
    earlier = (
        lax.broadcasted_iota(jnp.int32, (TOK, TOK), 0)
        < lax.broadcasted_iota(jnp.int32, (TOK, TOK), 1)
    ).astype(F32)
    place = dot(taken.astype(BF), earlier.astype(BF), 1, 0)
    placed = taken * (place == lax.rem(slot, CAP).astype(F32)).astype(F32)
    dispatch[...] = placed.T.astype(BF)
    collect = placed.astype(BF)
    rows[:, :, :D] = jnp.concatenate(
        [dot(collect, r[...], 1, 0).reshape(NE, CAP, D) for r in (x_in, c_in)], axis=1
    ).astype(BF)
    weight_col = jnp.sum(placed * weights, axis=1, keepdims=True)
    weight_col = jnp.broadcast_to(weight_col, (NE * CAP, 128)).reshape(NE, CAP, 128)
    rows[:, :, D:] = jnp.concatenate([weight_col, weight_col], axis=1).astype(BF)
    for c in tokens():
        c.start()
    own_rows = here(rows.at[e], rows_own.at[e], 0)
    own_rows.start()

    for c in kv_exchange():
        c.wait_recv()
    for c in own[:4]:
        c.wait()
    gather_step((3, 4), 0)
    for c in q_exchange():
        c.start()
    for c in tokens():
        c.wait_recv()
    own_rows.wait()
    for c in slices():
        c.start()
    own_xc = here(rows_own.at[:, :, columns(y, DS)], xc.at[y], 8)
    own_xc.start()
    dk_acc[...] = jnp.zeros_like(dk_acc)
    dv_acc[...] = jnp.zeros_like(dv_acc)
    for step in range(1, 4):
        gather_step((3, 4), step)
    gather_step((0, 1, 2), 1)
    own_xc.wait()
    for c in slices():
        c.wait_recv()
    both = xc[...].astype(F32)
    x_t[...] = both[:, :, :CAP, :].reshape(count, DS).T.astype(BF)
    c_t[...] = both[:, :, CAP:, :].reshape(count, DS).T.astype(BF)
    gather_step((3, 4), 4)
    for c in q_exchange():
        c.wait_recv()

    def chunk(c):
        per = NZ * TOK // KC
        return lax.div(c, per), pl.ds(lax.rem(c, per) * (KC // TOK), KC // TOK)

    def chunk_rows(ref, c):
        a, b = chunk(c)
        return ref[a, b].reshape(KC, HEAD_SIZE)

    def at(c):
        return pl.ds(pl.multiple_of(c * KC, KC), KC)

    def turn(c, carry):
        kt[:, at(c)] = chunk_rows(k_all, c).astype(F32).T.astype(BF)
        return carry

    lax.fori_loop(0, NY * NZ * TOK // KC, turn, 0)

    def fold(values, op):
        return op(values.reshape(KC // 8, 8, ROWS), axis=0)

    def attend(block, half, event):
        position = block * NZ + z
        chunks = lax.div(position * TOK + TOK + KC - 1, KC)
        for h in range(HALF):
            cols = pl.ds(
                pl.multiple_of(half * (HALF * HEAD_SIZE) + h * HEAD_SIZE, HEAD_SIZE), HEAD_SIZE
            )
            q_st[h * TOK : (h + 1) * TOK, :] = q_all[block, :, cols]
            do_st[h * TOK : (h + 1) * TOK, :] = do_all[block, :, cols]

        def scores(c, peak, masked):
            s = dot(chunk_rows(k_all, c), q_st[...], 1, 1) * factor
            if masked:
                key_pos = c * KC + lax.broadcasted_iota(jnp.int32, (KC, ROWS), 0)
                query_pos = position * TOK + lax.rem(
                    lax.broadcasted_iota(jnp.int32, (KC, ROWS), 1), TOK
                )
                s = jnp.where(key_pos <= query_pos, s, -1e30)
            s_scr[at(c), :] = s
            return jnp.maximum(peak, fold(s, jnp.max))

        peak = lax.fori_loop(
            0, chunks - 1, lambda c, m: scores(c, m, False), jnp.full((8, ROWS), -1e30, F32)
        )
        peak = scores(chunks - 1, peak, True)
        peak = jnp.max(peak, axis=0, keepdims=True)
        event(0)

        def weigh(c, carry):
            total, paired = carry
            p = jnp.exp2(s_scr[at(c), :] - peak)
            g = dot(chunk_rows(v_all, c), do_st[...], 1, 1)
            s_scr[at(c), :] = p
            g_scr[at(c), :] = g
            return total + fold(p, jnp.sum), paired + fold(p * g, jnp.sum)

        zero = jnp.zeros((8, ROWS), F32)
        total, paired = lax.fori_loop(0, chunks, weigh, (zero, zero))
        inverse = 1.0 / jnp.sum(total, axis=0, keepdims=True)
        row_dot = jnp.sum(paired, axis=0, keepdims=True) * inverse
        event(1)

        dqt[...] = jnp.zeros_like(dqt)

        def gradients(c, carry):
            a, b = chunk(c)
            p = s_scr[at(c), :] * inverse
            ds = (p * (g_scr[at(c), :] - row_dot)).astype(BF)
            shape = (KC // TOK, TOK, HEAD_SIZE)
            dv_acc[a, b] += dot(p.astype(BF), do_st[...], 1, 0).reshape(shape)
            dk_acc[a, b] += dot(ds, q_st[...], 1, 0).reshape(shape)
            dqt[...] += dot(kt[:, at(c)], ds, 1, 0)
            return carry

        lax.fori_loop(0, chunks, gradients, 0)
        for h in range(HALF):
            cols = pl.ds(
                pl.multiple_of(half * (HALF * HEAD_SIZE) + h * HEAD_SIZE, HEAD_SIZE), HEAD_SIZE
            )
            dq[block, :, cols] = (dqt[:, h * TOK : (h + 1) * TOK] * scale).T.astype(BF)
        event(2)

    def swaps():
        return [
            remote(part.at[at_y(y, z, e, d)[0]], parts.at[d - 1], s_send, s_recv, d - 1,
                   at_y(y, z, e, d)[1])
            for d in range(1, NY)
        ]

    def spreads():
        return [
            remote(act.at[y], act.at[y], a_send, a_recv, d - 1, at_y(y, z, e, d)[1])
            for d in range(1, NY)
        ]

    def routes():
        return [
            remote(route.at[at_e(y, z, e, d)[0]], route_home.at[e], t_send, t_recv, d - 1,
                   at_e(y, z, e, d)[1])
            for d in range(1, NE)
        ]

    def row_swaps():
        return [
            remote(rb.at[at_y(y, z, e, d)[0]], rbuf.at[y], b_send, b_recv, d - 1,
                   at_y(y, z, e, d)[1])
            for d in range(1, NY)
        ]

    def quarter(block):
        def value(b):
            return jnp.stack([dk_acc[block, b] * scale, dv_acc[block, b]])

        return value

    summed = [
        (lambda b: gg[b].astype(F32), lambda t: g_right.at[t], lambda t: g_left.at[t], gg_out),
        (lambda b: gu[b].astype(F32), lambda t: u_right.at[t], lambda t: u_left.at[t], gu_out),
        (lambda b: gd[b].astype(F32), lambda t: d_right.at[t], lambda t: d_left.at[t], gd_out),
    ]
    for block in range(NY):
        summed.append(
            (
                quarter(block),
                lambda t, block=block: kv_right.at[t, block],
                lambda t, block=block: kv_left.at[t, block],
                kv_sum.at[block],
            )
        )
    first = (
        lambda way: gg.at[lax.rem(z + (4, NZ - 3)[way], NZ)],
        lambda way: gu.at[lax.rem(z + (4, NZ - 3)[way], NZ)],
        lambda way: gd.at[lax.rem(z + (4, NZ - 3)[way], NZ)],
        lambda way: kv_first.at[0, way],
        lambda way: kv_first.at[1, way],
        lambda way: kv_first.at[2, way],
        lambda way: kv_first.at[3, way],
    )

    def to_right(index, step):
        buffer = summed[index][1]
        src = first[index](0) if step == 0 else buffer(step - 1)
        return remote(src, buffer(step), gr_send, gr_recv, index * 4 + step, right)

    def to_left(index, step):
        buffer = summed[index][2]
        src = first[index](1) if step == 0 else buffer(step - 1)
        return remote(src, buffer(step), gl_send, gl_recv, index * 3 + step, left)

    def ring_first(index):
        to_right(index, 0).start()
        to_left(index, 0).start()

    def ring_next(index, step):
        value, r_buffer, l_buffer, _ = summed[index]
        to_right(index, step - 1).wait_recv()
        got = r_buffer(step - 1)
        got[...] = (got[...].astype(F32) + value(lax.rem(z + 4 - step, NZ))).astype(BF)
        to_right(index, step).start()
        if step < 3:
            to_left(index, step - 1).wait_recv()
            got = l_buffer(step - 1)
            got[...] = (got[...].astype(F32) + value(lax.rem(z + NZ - 3 + step, NZ))).astype(BF)
            to_left(index, step).start()

    def ring_last(index):
        value, r_buffer, l_buffer, out = summed[index]
        to_right(index, 3).wait_recv()
        to_left(index, 2).wait_recv()
        out[...] = (
            value(z) + r_buffer(3)[...].astype(F32) + l_buffer(2)[...].astype(F32)
        ).astype(BF)

    def project():
        gather_step((0, 1, 2), 4)
        rows_in = xc[...].astype(F32)
        x = rows_in[:, :, :CAP, :].reshape(count, DS).astype(BF)
        c = rows_in[:, :, CAP:, :].reshape(count, DS).astype(BF)
        for index, (left_side, w) in enumerate(((x, wg_all), (x, wu_all), (c, wd_all))):
            product = dot(left_side, w[...].reshape(DS, FF), 1, 0)
            part[:, :, index * FF : (index + 1) * FF] = product.reshape(
                NY, NE * CAP, FF
            ).astype(BF)
        for copy in swaps():
            copy.start()

    def activate():
        for copy in swaps():
            copy.wait_recv()
        sums = part[y].astype(F32)
        for d in range(NY - 1):
            sums = sums + parts[d].astype(F32)
        gate_act = sums[:, :FF]
        up_act = sums[:, FF : 2 * FF]
        cot_down = sums[:, 2 * FF :]
        w = rows_own[:, :, D:].astype(F32)[:, :CAP, :].reshape(NE * CAP, 128)[:, :1]
        sigma = 1.0 / (1.0 + jnp.exp(-gate_act))
        silu = gate_act * sigma
        hidden = (silu * up_act).astype(BF).astype(F32)
        hidden_grad = w * cot_down
        act[y, :, :FF] = (
            hidden_grad * up_act * sigma * (1.0 + gate_act * (1.0 - sigma))
        ).astype(BF)
        act[y, :, FF : 2 * FF] = (hidden_grad * silu).astype(BF)
        act[y, :, 2 * FF :] = (w * hidden).astype(BF)
        for copy in spreads():
            copy.start()
        values = jnp.sum(hidden * cot_down, axis=1, keepdims=True)
        route[...] = jnp.broadcast_to(values, (NE * CAP, 128)).reshape(NE, CAP, 128)
        for copy in routes():
            copy.start()
        here(route.at[e], route_home.at[e], 9).start()

    def differentiate():
        for copy in spreads():
            copy.wait_recv()
        blocks = (NZ, WD, FF)
        act_all = act[...].reshape(count, 3 * FF)
        gate_pre = act_all[:, :FF]
        up_pre = act_all[:, FF : 2 * FF]
        gg[...] = dot(x_t[...], gate_pre, 1, 0).astype(BF).reshape(blocks)
        ring_first(0)
        gu[...] = dot(x_t[...], up_pre, 1, 0).astype(BF).reshape(blocks)
        ring_first(1)
        gd[...] = dot(c_t[...], act_all[:, 2 * FF :], 1, 0).astype(BF).reshape(blocks)
        ring_first(2)
        row_grad = dot(gate_pre, wg_all[...].reshape(DS, FF), 1, 1) + dot(
            up_pre, wu_all[...].reshape(DS, FF), 1, 1
        )
        row_grad = row_grad.reshape(NY, NE, CAP, DS)
        rb[...] = jnp.concatenate(
            [row_grad[:, :, :, i * 128 : (i + 1) * 128] for i in range(DS // 128)], axis=2
        ).astype(BF)
        for copy in row_swaps():
            copy.start()
        here(rb.at[y], rbuf.at[y], 10).start()

    def quarter_first(block):
        for way in range(2):
            b = lax.rem(z + (4, NZ - 3)[way], NZ)
            kv_first[block, way] = summed[3 + block][0](b).astype(BF)
        ring_first(3 + block)

    def q_home(block):
        return pltpu.make_async_remote_copy(
            src_ref=dq.at[block],
            dst_ref=dq_home.at[:, columns(y, GW)],
            send_sem=q_send.at[block],
            recv_sem=q_recv.at[y],
            device_id=(block * NZ + z, e),
            device_id_type=MESH,
        )

    def q_from(block):
        return pltpu.make_async_remote_copy(
            src_ref=dq.at[block],
            dst_ref=dq_home.at[:, block * GW : (block + 1) * GW],
            send_sem=q_send.at[block],
            recv_sem=q_recv.at[block],
            device_id=(block * NZ + z, e),
            device_id_type=MESH,
        )

    def send_q(block):
        pl.when(y != block)(lambda: q_home(block).start())

    def weights_next(step):
        for index in (0, 1, 2):
            ring_next(index, step)

    def mixed():
        differentiate()
        send_q(3)
        send_q(2)

    def second_end():
        ring_last(6)
        quarter_first(2)

    def third_end():
        ring_last(5)
        quarter_first(1)
        send_q(1)

    events = (
        (0, 0, lambda: gather_step((0, 1, 2), 2)),
        (0, 2, lambda: gather_step((0, 1, 2), 3)),
        (1, 1, project),
        (1, 2, lambda: quarter_first(3)),
        (2, 0, lambda: ring_next(6, 1)),
        (2, 2, activate),
        (3, 0, lambda: ring_next(6, 2)),
        (3, 1, lambda: ring_next(6, 3)),
        (3, 2, second_end),
        (4, 0, lambda: ring_next(5, 1)),
        (4, 2, mixed),
        (5, 0, lambda: ring_next(5, 2)),
        (5, 1, lambda: ring_next(5, 3)),
        (5, 2, third_end),
        (6, 0, lambda: weights_next(1)),
        (6, 1, lambda: ring_next(4, 1)),
        (7, 0, lambda: ring_next(4, 2)),
        (7, 1, lambda: weights_next(2)),
    )

    def work(i, carry):
        def event(sweep):
            for step, when, act_now in events:
                if when == sweep:
                    pl.when(i == step)(act_now)

        attend(NY - 1 - lax.div(i, 2), lax.rem(i, 2), event)
        return carry

    lax.fori_loop(0, STEPS, work, 0)
    quarter_first(0)
    send_q(0)
    own_q = here(dq.at[y], dq_home.at[:, columns(y, GW)], 11)
    own_q.start()

    def row_homes():
        return [
            remote(rbuf.at[:, at_e(y, z, e, d)[0]], back.at[e], i_send, i_recv, d - 1,
                   at_e(y, z, e, d)[1])
            for d in range(1, NE)
        ]

    here(rb.at[y], rbuf.at[y], 10).wait()
    for c in row_swaps():
        c.wait_recv()
    for c in row_homes():
        c.start()
    own_back = here(rbuf.at[:, e], back.at[e], 12)
    own_back.start()

    ring_next(4, 3)
    ring_next(3, 1)
    weights_next(3)
    ring_next(3, 2)
    ring_next(3, 3)
    ring_last(4)

    own_back.wait()
    for c in row_homes():
        c.wait_recv()
    pieces = back[...].astype(F32).reshape(NE, NY, DS // 128, CAP, 128)
    for block in range(NY):
        for i in range(DS // 128):
            piece = pieces[:, block, i].reshape(NE * CAP, 128).astype(BF)
            start = block * DS + i * 128
            input_grad[:, start : start + 128] = dot(dispatch[...], piece, 1, 0).astype(BF)

    def homes():
        copies = []
        for kind, out in enumerate((dk_home, dv_home)):
            target = out.at[:, columns(y, HEAD_SIZE)]
            for d in range(1, NY):
                peer, dev = at_y(y, z, e, d)
                copies.append(
                    remote(kv_sum.at[peer, kind], target, h_send, h_recv, kind * 3 + d - 1, dev)
                )
            copies.append(here(kv_sum.at[y, kind], target, 13 + kind))
        return copies

    here(route.at[e], route_home.at[e], 9).wait()
    for c in routes():
        c.wait()
    values = route_home[...].reshape(NE * CAP, 128)
    spread_values = dispatch[...].astype(F32).T * values.astype(BF).astype(F32)
    column = lax.broadcasted_iota(jnp.int32, (TOPK, TOK), 0)
    routed = jnp.zeros((TOPK, TOK), F32)
    for j in range(TOPK):
        total = jnp.sum(spread_values * named(j), axis=0, keepdims=True)
        routed += jnp.where(column == j, total, 0.0)
    route_grad[...] = routed.astype(BF)

    ring_last(3)
    for c in homes():
        c.start()
    for index in (0, 1, 2):
        ring_last(index)
    for c in homes():
        c.wait()
    for block in range(NY):
        pl.when(y != block)(lambda block=block: q_home(block).wait_send())
        pl.when(y != block)(lambda block=block: q_from(block).wait_recv())
    own_q.wait()
    for c in tokens() + kv_exchange() + q_exchange() + slices() + swaps() + spreads():
        c.wait_send()
    for c in row_swaps() + row_homes():
        c.wait_send()
    for index in range(5):
        for step in range(4):
            for c in gather(index, step):
                c.wait_send()
    for index in range(3 + NY):
        for step in range(4):
            to_right(index, step).wait_send()
            if step < 3:
                to_left(index, step).wait_send()


def layer(*arrays):
    sd = jax.ShapeDtypeStruct
    any_spec = pl.BlockSpec(memory_space=pl.ANY)
    vmem = pl.BlockSpec(memory_space=pltpu.VMEM)
    dma = pltpu.SemaphoreType.DMA
    scratch = pltpu.VMEM
    whole = (NY, NZ, TOK, HEAD_SIZE)
    length = NY * NZ * TOK
    slots = NE * CAP
    blocks = (NZ, WD, FF)
    rings = []
    pair = (2, TOK, HEAD_SIZE)
    for shape in ((NY,) + pair, (WD, FF), (WD, FF), (WD, FF)):
        rings += [scratch((4,) + shape, BF), scratch((3,) + shape, BF)]
    return pl.pallas_call(
        layer_kernel,
        out_shape=[
            sd((TOK, QUERY_HEADS * HEAD_SIZE), BF),
            sd((TOK, KEY_VALUE_HEADS * HEAD_SIZE), BF),
            sd((TOK, KEY_VALUE_HEADS * HEAD_SIZE), BF),
            sd((WD, FF), BF),
            sd((WD, FF), BF),
            sd((WD, FF), BF),
            sd((TOK, D), BF),
            sd((TOPK, TOK), BF),
        ],
        in_specs=[any_spec] * 7 + [vmem] * 4,
        out_specs=[any_spec] * 3 + [vmem] * 5,
        scratch_shapes=[
            scratch((NE, 16, D + 128), BF), scratch((TOK, slots), BF), scratch((NE, CAP, 128), F32),
            scratch((NY, TOK, GW), BF), scratch((NY, TOK, GW), BF),
            scratch(whole, BF), scratch(whole, BF), scratch((HEAD_SIZE, length), BF),
            scratch((ROWS, HEAD_SIZE), BF), scratch((ROWS, HEAD_SIZE), BF),
            scratch((length, ROWS), F32), scratch((length, ROWS), F32),
            scratch(whole, F32), scratch(whole, F32), scratch((HEAD_SIZE, ROWS), F32),
            scratch((NY, TOK, GW), BF),
            scratch((NE, 16, D + 128), BF), scratch((NY, NE, 16, DS), BF),
            scratch((DS, NY * slots), BF), scratch((DS, NY * slots), BF),
            scratch(blocks, BF), scratch(blocks, BF), scratch(blocks, BF),
            scratch((NY, slots, 3 * FF), BF), scratch((NY - 1, slots, 3 * FF), BF),
            scratch((NY, slots, 3 * FF), BF), scratch((NE, CAP, 128), F32),
            scratch((NY, NE, 32, 128), BF), scratch((NY, NE, 32, 128), BF),
            scratch((NE, NY, 32, 128), BF),
            scratch(blocks, BF), scratch(blocks, BF), scratch(blocks, BF),
        ]
        + rings
        + [
            scratch((NY, 2) + pair, BF), scratch((NY,) + pair, BF),
            dma((16,)), dma((12,)), dma((12,)), dma((7,)), dma((7,)), dma((3,)), dma((3,)),
            dma((20,)), dma((20,)), dma((15,)), dma((15,)),
            dma((3,)), dma((3,)), dma((3,)), dma((3,)), dma((7,)), dma((7,)),
            dma((4,)), dma((4,)), dma((3,)), dma((3,)), dma((7,)), dma((7,)), dma((6,)), dma((6,)),
            dma((28,)), dma((28,)), dma((21,)), dma((21,)),
        ],
        compiler_params=pltpu.CompilerParams(
            collective_id=0, has_side_effects=True, vmem_limit_bytes=VMEM_MOST
        ),
        name="layer",
    )(*arrays)


def finish_kernel(*refs):
    half = (len(refs) - 2) // 3
    held = refs[2 * half : 3 * half]
    arriving = [
        pltpu.make_async_copy(refs[i], held[i], refs[-2].at[i]) for i in range(half)
    ]
    leaving = [
        pltpu.make_async_copy(held[i], refs[half + i], refs[-1].at[i]) for i in range(half)
    ]
    for c in arriving:
        c.start()
    for first, second in zip(arriving, leaving):
        first.wait()
        second.start()
    for c in leaving:
        c.wait()


def finish(*arrays):
    any_spec = pl.BlockSpec(memory_space=pl.ANY)
    dma = pltpu.SemaphoreType.DMA
    return pl.pallas_call(
        finish_kernel,
        out_shape=[jax.ShapeDtypeStruct(a.shape, a.dtype) for a in arrays],
        in_specs=[any_spec] * len(arrays),
        out_specs=[any_spec] * len(arrays),
        scratch_shapes=[pltpu.VMEM(a.shape, a.dtype) for a in arrays]
        + [dma((len(arrays),)), dma((len(arrays),))],
        compiler_params=pltpu.CompilerParams(vmem_limit_bytes=VMEM_MOST),
        name="finish",
    )(*arrays)


def per_device(
    query_rows,
    key_matrix_all,
    value_matrix_all,
    context_grad,
    mixture_input,
    mixture_grad,
    expert_ids,
    route_weight,
    gate_weight,
    up_weight,
    down_weight,
):
    outputs = layer(
        query_rows[0], context_grad[0], key_matrix_all[0], value_matrix_all[0],
        gate_weight[0], up_weight[0], down_weight[0],
        mixture_input[0], mixture_grad[0], expert_ids[0].T, route_weight[0].T,
    )
    (
        dq_home, dk_home, dv_home, gate_grad, up_grad, down_grad, input_grad,
    ) = finish(*outputs[:7])
    route_grad = outputs[7].T
    return (
        dq_home[None],
        dk_home[None],
        dv_home[None],
        input_grad[None],
        route_grad[None],
        gate_grad[None],
        up_grad[None],
        down_grad[None],
    )


def solution(mesh):
    spec = P("exp", "ctx", None)
    return jax.shard_map(
        per_device,
        mesh=mesh,
        in_specs=(spec,) * 11,
        out_specs=(spec,) * 8,
        check_vma=False,
    )
```

```python
import math

import jax
import jax.numpy as jnp
from jax import lax
from jax.experimental import pallas as pl
from jax.experimental.pallas import tpu as pltpu
from jax.sharding import PartitionSpec as P

D = 2048
QUERY_HEADS = 32
KEY_VALUE_HEADS = 4
HEAD_SIZE = 128
FF = 768
EXPERTS = 128
TOPK = 8
CAP = 8
NY = 4
NZ = 8
NE = 8
TOK = 128
GW = QUERY_HEADS // KEY_VALUE_HEADS * HEAD_SIZE
DS = D // NY
WD = D // (NY * NZ)
KC = 512
HALF = 4
ROWS = HALF * TOK
STEPS = NY * (GW // (HALF * HEAD_SIZE))
MESH = pl.DeviceIdType.MESH
VMEM_MOST = 60 * 1024 * 1024
BF = jnp.bfloat16
F32 = jnp.float32


def places():
    ctx = lax.axis_index("ctx")
    return lax.div(ctx, NZ), lax.rem(ctx, NZ), lax.axis_index("exp")


def at_y(y, z, e, shift):
    peer = lax.rem(y + shift, NY)
    return peer, (peer * NZ + z, e)


def at_z(y, z, e, shift):
    peer = lax.rem(z + shift + NZ, NZ)
    return peer, (y * NZ + peer, e)


def at_e(y, z, e, shift):
    peer = lax.rem(e + shift, NE)
    return peer, (y * NZ + z, peer)


def greet(peers):
    barrier = pltpu.get_barrier_semaphore()
    for peer in peers:
        pl.semaphore_signal(barrier, inc=1, device_id=peer, device_id_type=MESH)
    pl.semaphore_wait(barrier, len(peers))


def remote(src, dst, send, recv, index, peer):
    return pltpu.make_async_remote_copy(
        src_ref=src,
        dst_ref=dst,
        send_sem=send.at[index],
        recv_sem=recv.at[index],
        device_id=peer,
        device_id_type=MESH,
    )


def columns(index, width):
    return pl.ds(pl.multiple_of(index * width, width), width)


def dot(a, b, left, right):
    return lax.dot_general(a, b, (((left,), (right,)), ((), ())), preferred_element_type=F32)


def layer_kernel(
    q, do, k, v, wg, wu, wd, x_in, c_in, ids, route_weight,
    dq_home, dk_home, dv_home, gg_out, gu_out, gd_out, input_grad, route_grad,
    rows, dispatch, route_home,
    q_all, do_all, k_all, v_all, kt, q_st, do_st, s_scr, g_scr, dk_acc, dv_acc, dqt, dq,
    rows_own, xc, x_t, c_t, wg_all, wu_all, wd_all, part, parts, act, route,
    rb, rbuf, back, gg, gu, gd,
    kv_right, kv_left, g_right, g_left, u_right, u_left, d_right, d_left, kv_first, kv_sum,
    local_sem, y_send, y_recv, e_send, e_recv, x_send, x_recv, r_send, r_recv, l_send, l_recv,
    s_send, s_recv, a_send, a_recv, t_send, t_recv, q_send, q_recv, b_send, b_recv,
    i_send, i_recv, h_send, h_recv, gr_send, gr_recv, gl_send, gl_recv,
):
    y, z, e = places()
    count = NY * NE * CAP
    scale = 1.0 / math.sqrt(HEAD_SIZE)
    factor = scale * math.log2(math.e)
    greet(
        [at_y(y, z, e, d)[1] for d in range(1, NY)]
        + [at_z(y, z, e, d)[1] for d in (1, -1)]
        + [at_e(y, z, e, d)[1] for d in range(1, NE)]
    )
    right = at_z(y, z, e, 1)[1]
    left = at_z(y, z, e, -1)[1]

    def tokens():
        return [
            remote(rows.at[at_e(y, z, e, d)[0]], rows_own.at[e], e_send, e_recv, d - 1,
                   at_e(y, z, e, d)[1])
            for d in range(1, NE)
        ]

    def slices():
        return [
            remote(rows_own.at[:, :, columns(at_y(y, z, e, d)[0], DS)], xc.at[y], x_send, x_recv,
                   d - 1, at_y(y, z, e, d)[1])
            for d in range(1, NY)
        ]

    def y_exchange(src, target, width, base):
        return [
            remote(src.at[:, columns(at_y(y, z, e, d)[0], width)], target, y_send, y_recv,
                   base + d - 1, at_y(y, z, e, d)[1])
            for d in range(1, NY)
        ]

    def kv_exchange():
        return y_exchange(k, k_all.at[y, z], HEAD_SIZE, 0) + y_exchange(
            v, v_all.at[y, z], HEAD_SIZE, 3
        )

    def q_exchange():
        return y_exchange(q, q_all.at[y], GW, 6) + y_exchange(do, do_all.at[y], GW, 9)

    gathered = (
        lambda b: wg_all.at[b],
        lambda b: wu_all.at[b],
        lambda b: wd_all.at[b],
        lambda b: k_all.at[:, b],
        lambda b: v_all.at[:, b],
    )

    def gather(index, step):
        block = gathered[index]
        here = block(lax.rem(z - step + NZ, NZ))
        pair = [remote(here, here, r_send, r_recv, index * 4 + step, right)]
        if step < 3:
            there = block(lax.rem(z + step, NZ))
            pair.append(remote(there, there, l_send, l_recv, index * 3 + step, left))
        return pair

    def gather_step(indices, step):
        for index in indices:
            if step > 0:
                for c in gather(index, step - 1):
                    c.wait_recv()
            if step < 4:
                for c in gather(index, step):
                    c.start()

    def here(src, dst, index):
        return pltpu.make_async_copy(src, dst, local_sem.at[index])

    for c in kv_exchange():
        c.start()
    own = [
        here(k.at[:, columns(y, HEAD_SIZE)], k_all.at[y, z], 1),
        here(v.at[:, columns(y, HEAD_SIZE)], v_all.at[y, z], 2),
        here(q.at[:, columns(y, GW)], q_all.at[y], 3),
        here(do.at[:, columns(y, GW)], do_all.at[y], 4),
        here(wg, wg_all.at[z], 5),
        here(wu, wu_all.at[z], 6),
        here(wd, wd_all.at[z], 7),
    ]
    for c in own:
        c.start()
    for c in own[4:]:
        c.wait()
    gather_step((0, 1, 2), 0)

    slot = lax.broadcasted_iota(jnp.int32, (NE * CAP, TOK), 0)
    expert = lax.div(slot, CAP) * (EXPERTS // NE)

    def named(j):
        return (ids[j : j + 1, :] == expert).astype(F32)

    combine = route_weight[...].astype(F32)
    taken = jnp.zeros((NE * CAP, TOK), F32)
    weights = jnp.zeros((NE * CAP, TOK), F32)
    for j in range(TOPK):
        hit = named(j)
        taken += hit
        weights += hit * combine[j : j + 1, :]
    earlier = (
        lax.broadcasted_iota(jnp.int32, (TOK, TOK), 0)
        < lax.broadcasted_iota(jnp.int32, (TOK, TOK), 1)
    ).astype(F32)
    place = dot(taken.astype(BF), earlier.astype(BF), 1, 0)
    placed = taken * (place == lax.rem(slot, CAP).astype(F32)).astype(F32)
    dispatch[...] = placed.T.astype(BF)
    collect = placed.astype(BF)
    rows[:, :, :D] = jnp.concatenate(
        [dot(collect, r[...], 1, 0).reshape(NE, CAP, D) for r in (x_in, c_in)], axis=1
    ).astype(BF)
    weight_col = jnp.sum(placed * weights, axis=1, keepdims=True)
    weight_col = jnp.broadcast_to(weight_col, (NE * CAP, 128)).reshape(NE, CAP, 128)
    rows[:, :, D:] = jnp.concatenate([weight_col, weight_col], axis=1).astype(BF)
    for c in tokens():
        c.start()
    own_rows = here(rows.at[e], rows_own.at[e], 0)
    own_rows.start()

    for c in kv_exchange():
        c.wait_recv()
    for c in own[:4]:
        c.wait()
    gather_step((3, 4), 0)
    for c in q_exchange():
        c.start()
    for c in tokens():
        c.wait_recv()
    own_rows.wait()
    for c in slices():
        c.start()
    own_xc = here(rows_own.at[:, :, columns(y, DS)], xc.at[y], 8)
    own_xc.start()
    dk_acc[...] = jnp.zeros_like(dk_acc)
    dv_acc[...] = jnp.zeros_like(dv_acc)
    gather_step((3, 4), 1)
    gather_step((0, 1, 2), 1)
    gather_step((3, 4), 2)
    gather_step((3, 4), 3)
    gather_step((0, 1, 2), 2)
    own_xc.wait()
    for c in slices():
        c.wait_recv()
    both = xc[...].astype(F32)
    x_t[...] = both[:, :, :CAP, :].reshape(count, DS).T.astype(BF)
    c_t[...] = both[:, :, CAP:, :].reshape(count, DS).T.astype(BF)
    gather_step((3, 4), 4)
    for c in q_exchange():
        c.wait_recv()

    def chunk(c):
        per = NZ * TOK // KC
        return lax.div(c, per), pl.ds(lax.rem(c, per) * (KC // TOK), KC // TOK)

    def chunk_rows(ref, c):
        a, b = chunk(c)
        return ref[a, b].reshape(KC, HEAD_SIZE)

    def at(c):
        return pl.ds(pl.multiple_of(c * KC, KC), KC)

    def turn(c, carry):
        kt[:, at(c)] = chunk_rows(k_all, c).astype(F32).T.astype(BF)
        return carry

    lax.fori_loop(0, NY * NZ * TOK // KC, turn, 0)

    def fold(values, op):
        return op(values.reshape(KC // 8, 8, ROWS), axis=0)

    def attend(block, half, event):
        position = block * NZ + z
        chunks = lax.div(position * TOK + TOK + KC - 1, KC)
        for h in range(HALF):
            cols = pl.ds(
                pl.multiple_of(half * (HALF * HEAD_SIZE) + h * HEAD_SIZE, HEAD_SIZE), HEAD_SIZE
            )
            q_st[h * TOK : (h + 1) * TOK, :] = q_all[block, :, cols]
            do_st[h * TOK : (h + 1) * TOK, :] = do_all[block, :, cols]

        def scores(c, peak, masked):
            s = dot(chunk_rows(k_all, c), q_st[...], 1, 1) * factor
            if masked:
                key_pos = c * KC + lax.broadcasted_iota(jnp.int32, (KC, ROWS), 0)
                query_pos = position * TOK + lax.rem(
                    lax.broadcasted_iota(jnp.int32, (KC, ROWS), 1), TOK
                )
                s = jnp.where(key_pos <= query_pos, s, -1e30)
            s_scr[at(c), :] = s
            return jnp.maximum(peak, fold(s, jnp.max))

        peak = lax.fori_loop(
            0, chunks - 1, lambda c, m: scores(c, m, False), jnp.full((8, ROWS), -1e30, F32)
        )
        peak = scores(chunks - 1, peak, True)
        peak = jnp.max(peak, axis=0, keepdims=True)
        event(0)

        def weigh(c, carry):
            total, paired = carry
            p = jnp.exp2(s_scr[at(c), :] - peak)
            g = dot(chunk_rows(v_all, c), do_st[...], 1, 1)
            s_scr[at(c), :] = p
            g_scr[at(c), :] = g
            return total + fold(p, jnp.sum), paired + fold(p * g, jnp.sum)

        zero = jnp.zeros((8, ROWS), F32)
        total, paired = lax.fori_loop(0, chunks, weigh, (zero, zero))
        inverse = 1.0 / jnp.sum(total, axis=0, keepdims=True)
        row_dot = jnp.sum(paired, axis=0, keepdims=True) * inverse
        event(1)

        dqt[...] = jnp.zeros_like(dqt)

        def gradients(c, carry):
            a, b = chunk(c)
            p = s_scr[at(c), :] * inverse
            ds = (p * (g_scr[at(c), :] - row_dot)).astype(BF)
            shape = (KC // TOK, TOK, HEAD_SIZE)
            dv_acc[a, b] += dot(p.astype(BF), do_st[...], 1, 0).reshape(shape)
            dk_acc[a, b] += dot(ds, q_st[...], 1, 0).reshape(shape)
            dqt[...] += dot(kt[:, at(c)], ds, 1, 0)
            return carry

        lax.fori_loop(0, chunks, gradients, 0)
        for h in range(HALF):
            cols = pl.ds(
                pl.multiple_of(half * (HALF * HEAD_SIZE) + h * HEAD_SIZE, HEAD_SIZE), HEAD_SIZE
            )
            dq[block, :, cols] = (dqt[:, h * TOK : (h + 1) * TOK] * scale).T.astype(BF)
        event(2)

    def swaps():
        return [
            remote(part.at[at_y(y, z, e, d)[0]], parts.at[d - 1], s_send, s_recv, d - 1,
                   at_y(y, z, e, d)[1])
            for d in range(1, NY)
        ]

    def spreads():
        return [
            remote(act.at[y], act.at[y], a_send, a_recv, d - 1, at_y(y, z, e, d)[1])
            for d in range(1, NY)
        ]

    def routes():
        return [
            remote(route.at[at_e(y, z, e, d)[0]], route_home.at[e], t_send, t_recv, d - 1,
                   at_e(y, z, e, d)[1])
            for d in range(1, NE)
        ]

    def row_swaps():
        return [
            remote(rb.at[at_y(y, z, e, d)[0]], rbuf.at[y], b_send, b_recv, d - 1,
                   at_y(y, z, e, d)[1])
            for d in range(1, NY)
        ]

    def quarter(block):
        def value(b):
            return jnp.stack([dk_acc[block, b] * scale, dv_acc[block, b]])

        return value

    summed = [
        (lambda b: gg[b].astype(F32), lambda t: g_right.at[t], lambda t: g_left.at[t], gg_out),
        (lambda b: gu[b].astype(F32), lambda t: u_right.at[t], lambda t: u_left.at[t], gu_out),
        (lambda b: gd[b].astype(F32), lambda t: d_right.at[t], lambda t: d_left.at[t], gd_out),
    ]
    for block in range(NY):
        summed.append(
            (
                quarter(block),
                lambda t, block=block: kv_right.at[t, block],
                lambda t, block=block: kv_left.at[t, block],
                kv_sum.at[block],
            )
        )
    first = (
        lambda way: gg.at[lax.rem(z + (4, NZ - 3)[way], NZ)],
        lambda way: gu.at[lax.rem(z + (4, NZ - 3)[way], NZ)],
        lambda way: gd.at[lax.rem(z + (4, NZ - 3)[way], NZ)],
        lambda way: kv_first.at[0, way],
        lambda way: kv_first.at[1, way],
        lambda way: kv_first.at[2, way],
        lambda way: kv_first.at[3, way],
    )

    def to_right(index, step):
        buffer = summed[index][1]
        src = first[index](0) if step == 0 else buffer(step - 1)
        return remote(src, buffer(step), gr_send, gr_recv, index * 4 + step, right)

    def to_left(index, step):
        buffer = summed[index][2]
        src = first[index](1) if step == 0 else buffer(step - 1)
        return remote(src, buffer(step), gl_send, gl_recv, index * 3 + step, left)

    def ring_first(index):
        to_right(index, 0).start()
        to_left(index, 0).start()

    def ring_next(index, step):
        value, r_buffer, l_buffer, _ = summed[index]
        to_right(index, step - 1).wait_recv()
        got = r_buffer(step - 1)
        got[...] = (got[...].astype(F32) + value(lax.rem(z + 4 - step, NZ))).astype(BF)
        to_right(index, step).start()
        if step < 3:
            to_left(index, step - 1).wait_recv()
            got = l_buffer(step - 1)
            got[...] = (got[...].astype(F32) + value(lax.rem(z + NZ - 3 + step, NZ))).astype(BF)
            to_left(index, step).start()

    def ring_last(index):
        value, r_buffer, l_buffer, out = summed[index]
        to_right(index, 3).wait_recv()
        to_left(index, 2).wait_recv()
        out[...] = (
            value(z) + r_buffer(3)[...].astype(F32) + l_buffer(2)[...].astype(F32)
        ).astype(BF)

    def project():
        gather_step((0, 1, 2), 4)
        rows_in = xc[...].astype(F32)
        x = rows_in[:, :, :CAP, :].reshape(count, DS).astype(BF)
        c = rows_in[:, :, CAP:, :].reshape(count, DS).astype(BF)
        for index, (left_side, w) in enumerate(((x, wg_all), (x, wu_all), (c, wd_all))):
            product = dot(left_side, w[...].reshape(DS, FF), 1, 0)
            part[:, :, index * FF : (index + 1) * FF] = product.reshape(
                NY, NE * CAP, FF
            ).astype(BF)
        for copy in swaps():
            copy.start()

    def activate():
        for copy in swaps():
            copy.wait_recv()
        sums = part[y].astype(F32)
        for d in range(NY - 1):
            sums = sums + parts[d].astype(F32)
        gate_act = sums[:, :FF]
        up_act = sums[:, FF : 2 * FF]
        cot_down = sums[:, 2 * FF :]
        w = rows_own[:, :, D:].astype(F32)[:, :CAP, :].reshape(NE * CAP, 128)[:, :1]
        sigma = 1.0 / (1.0 + jnp.exp(-gate_act))
        silu = gate_act * sigma
        hidden = (silu * up_act).astype(BF).astype(F32)
        hidden_grad = w * cot_down
        act[y, :, :FF] = (
            hidden_grad * up_act * sigma * (1.0 + gate_act * (1.0 - sigma))
        ).astype(BF)
        act[y, :, FF : 2 * FF] = (hidden_grad * silu).astype(BF)
        act[y, :, 2 * FF :] = (w * hidden).astype(BF)
        for copy in spreads():
            copy.start()
        values = jnp.sum(hidden * cot_down, axis=1, keepdims=True)
        route[...] = jnp.broadcast_to(values, (NE * CAP, 128)).reshape(NE, CAP, 128)
        for copy in routes():
            copy.start()
        here(route.at[e], route_home.at[e], 9).start()

    def differentiate():
        for copy in spreads():
            copy.wait_recv()
        blocks = (NZ, WD, FF)
        act_all = act[...].reshape(count, 3 * FF)
        gate_pre = act_all[:, :FF]
        up_pre = act_all[:, FF : 2 * FF]
        gg[...] = dot(x_t[...], gate_pre, 1, 0).astype(BF).reshape(blocks)
        ring_first(0)
        gu[...] = dot(x_t[...], up_pre, 1, 0).astype(BF).reshape(blocks)
        ring_first(1)
        gd[...] = dot(c_t[...], act_all[:, 2 * FF :], 1, 0).astype(BF).reshape(blocks)
        ring_first(2)
        row_grad = dot(gate_pre, wg_all[...].reshape(DS, FF), 1, 1) + dot(
            up_pre, wu_all[...].reshape(DS, FF), 1, 1
        )
        row_grad = row_grad.reshape(NY, NE, CAP, DS)
        rb[...] = jnp.concatenate(
            [row_grad[:, :, :, i * 128 : (i + 1) * 128] for i in range(DS // 128)], axis=2
        ).astype(BF)
        for copy in row_swaps():
            copy.start()
        here(rb.at[y], rbuf.at[y], 10).start()

    def quarter_first(block):
        for way in range(2):
            b = lax.rem(z + (4, NZ - 3)[way], NZ)
            kv_first[block, way] = summed[3 + block][0](b).astype(BF)
        ring_first(3 + block)

    def q_home(block):
        return pltpu.make_async_remote_copy(
            src_ref=dq.at[block],
            dst_ref=dq_home.at[:, columns(y, GW)],
            send_sem=q_send.at[block],
            recv_sem=q_recv.at[y],
            device_id=(block * NZ + z, e),
            device_id_type=MESH,
        )

    def q_from(block):
        return pltpu.make_async_remote_copy(
            src_ref=dq.at[block],
            dst_ref=dq_home.at[:, block * GW : (block + 1) * GW],
            send_sem=q_send.at[block],
            recv_sem=q_recv.at[block],
            device_id=(block * NZ + z, e),
            device_id_type=MESH,
        )

    def send_q(block):
        pl.when(y != block)(lambda: q_home(block).start())

    def weights_next(step):
        for index in (0, 1, 2):
            ring_next(index, step)

    def mixed():
        weights_next(1)
        send_q(3)
        send_q(2)

    def second_end():
        ring_last(6)
        quarter_first(2)

    def third_end():
        ring_last(5)
        quarter_first(1)
        send_q(1)

    events = (
        (0, 0, lambda: gather_step((0, 1, 2), 3)),
        (0, 2, project),
        (1, 2, lambda: quarter_first(3)),
        (2, 0, lambda: ring_next(6, 1)),
        (2, 0, activate),
        (3, 0, lambda: ring_next(6, 2)),
        (3, 1, lambda: ring_next(6, 3)),
        (3, 2, second_end),
        (4, 0, lambda: ring_next(5, 1)),
        (3, 2, differentiate),
        (4, 2, mixed),
        (5, 0, lambda: ring_next(5, 2)),
        (5, 1, lambda: ring_next(5, 3)),
        (5, 2, third_end),
        (6, 0, lambda: weights_next(2)),
        (6, 1, lambda: ring_next(4, 1)),
        (7, 0, lambda: ring_next(4, 2)),
        (7, 1, lambda: weights_next(3)),
    )

    def work(i, carry):
        def event(sweep):
            for step, when, act_now in events:
                if when == sweep:
                    pl.when(i == step)(act_now)

        attend(NY - 1 - lax.div(i, 2), lax.rem(i, 2), event)
        return carry

    lax.fori_loop(0, STEPS, work, 0)
    quarter_first(0)
    send_q(0)
    own_q = here(dq.at[y], dq_home.at[:, columns(y, GW)], 11)
    own_q.start()

    def row_homes():
        return [
            remote(rbuf.at[:, at_e(y, z, e, d)[0]], back.at[e], i_send, i_recv, d - 1,
                   at_e(y, z, e, d)[1])
            for d in range(1, NE)
        ]

    here(rb.at[y], rbuf.at[y], 10).wait()
    for c in row_swaps():
        c.wait_recv()
    for c in row_homes():
        c.start()
    own_back = here(rbuf.at[:, e], back.at[e], 12)
    own_back.start()

    ring_next(4, 3)
    ring_next(3, 1)
    ring_next(3, 2)
    ring_next(3, 3)
    ring_last(4)

    own_back.wait()
    for c in row_homes():
        c.wait_recv()
    pieces = back[...].astype(F32).reshape(NE, NY, DS // 128, CAP, 128)
    for block in range(NY):
        for i in range(DS // 128):
            piece = pieces[:, block, i].reshape(NE * CAP, 128).astype(BF)
            start = block * DS + i * 128
            input_grad[:, start : start + 128] = dot(dispatch[...], piece, 1, 0).astype(BF)

    def homes():
        copies = []
        for kind, out in enumerate((dk_home, dv_home)):
            target = out.at[:, columns(y, HEAD_SIZE)]
            for d in range(1, NY):
                peer, dev = at_y(y, z, e, d)
                copies.append(
                    remote(kv_sum.at[peer, kind], target, h_send, h_recv, kind * 3 + d - 1, dev)
                )
            copies.append(here(kv_sum.at[y, kind], target, 13 + kind))
        return copies

    here(route.at[e], route_home.at[e], 9).wait()
    for c in routes():
        c.wait()
    values = route_home[...].reshape(NE * CAP, 128)
    spread_values = dispatch[...].astype(F32).T * values.astype(BF).astype(F32)
    column = lax.broadcasted_iota(jnp.int32, (TOPK, TOK), 0)
    routed = jnp.zeros((TOPK, TOK), F32)
    for j in range(TOPK):
        total = jnp.sum(spread_values * named(j), axis=0, keepdims=True)
        routed += jnp.where(column == j, total, 0.0)
    route_grad[...] = routed.astype(BF)

    ring_last(3)
    for c in homes():
        c.start()
    for index in (0, 1, 2):
        ring_last(index)
    for c in homes():
        c.wait()
    for block in range(NY):
        pl.when(y != block)(lambda block=block: q_home(block).wait_send())
        pl.when(y != block)(lambda block=block: q_from(block).wait_recv())
    own_q.wait()
    for c in tokens() + kv_exchange() + q_exchange() + slices() + swaps() + spreads():
        c.wait_send()
    for c in row_swaps() + row_homes():
        c.wait_send()
    for index in range(5):
        for step in range(4):
            for c in gather(index, step):
                c.wait_send()
    for index in range(3 + NY):
        for step in range(4):
            to_right(index, step).wait_send()
            if step < 3:
                to_left(index, step).wait_send()


def layer(*arrays):
    sd = jax.ShapeDtypeStruct
    any_spec = pl.BlockSpec(memory_space=pl.ANY)
    vmem = pl.BlockSpec(memory_space=pltpu.VMEM)
    dma = pltpu.SemaphoreType.DMA
    scratch = pltpu.VMEM
    whole = (NY, NZ, TOK, HEAD_SIZE)
    length = NY * NZ * TOK
    slots = NE * CAP
    blocks = (NZ, WD, FF)
    rings = []
    pair = (2, TOK, HEAD_SIZE)
    for shape in ((NY,) + pair, (WD, FF), (WD, FF), (WD, FF)):
        rings += [scratch((4,) + shape, BF), scratch((3,) + shape, BF)]
    return pl.pallas_call(
        layer_kernel,
        out_shape=[
            sd((TOK, QUERY_HEADS * HEAD_SIZE), BF),
            sd((TOK, KEY_VALUE_HEADS * HEAD_SIZE), BF),
            sd((TOK, KEY_VALUE_HEADS * HEAD_SIZE), BF),
            sd((WD, FF), BF),
            sd((WD, FF), BF),
            sd((WD, FF), BF),
            sd((TOK, D), BF),
            sd((TOPK, TOK), BF),
        ],
        in_specs=[any_spec] * 7 + [vmem] * 4,
        out_specs=[any_spec] * 3 + [vmem] * 5,
        scratch_shapes=[
            scratch((NE, 16, D + 128), BF), scratch((TOK, slots), BF), scratch((NE, CAP, 128), F32),
            scratch((NY, TOK, GW), BF), scratch((NY, TOK, GW), BF),
            scratch(whole, BF), scratch(whole, BF), scratch((HEAD_SIZE, length), BF),
            scratch((ROWS, HEAD_SIZE), BF), scratch((ROWS, HEAD_SIZE), BF),
            scratch((length, ROWS), F32), scratch((length, ROWS), F32),
            scratch(whole, F32), scratch(whole, F32), scratch((HEAD_SIZE, ROWS), F32),
            scratch((NY, TOK, GW), BF),
            scratch((NE, 16, D + 128), BF), scratch((NY, NE, 16, DS), BF),
            scratch((DS, NY * slots), BF), scratch((DS, NY * slots), BF),
            scratch(blocks, BF), scratch(blocks, BF), scratch(blocks, BF),
            scratch((NY, slots, 3 * FF), BF), scratch((NY - 1, slots, 3 * FF), BF),
            scratch((NY, slots, 3 * FF), BF), scratch((NE, CAP, 128), F32),
            scratch((NY, NE, 32, 128), BF), scratch((NY, NE, 32, 128), BF),
            scratch((NE, NY, 32, 128), BF),
            scratch(blocks, BF), scratch(blocks, BF), scratch(blocks, BF),
        ]
        + rings
        + [
            scratch((NY, 2) + pair, BF), scratch((NY,) + pair, BF),
            dma((16,)), dma((12,)), dma((12,)), dma((7,)), dma((7,)), dma((3,)), dma((3,)),
            dma((20,)), dma((20,)), dma((15,)), dma((15,)),
            dma((3,)), dma((3,)), dma((3,)), dma((3,)), dma((7,)), dma((7,)),
            dma((4,)), dma((4,)), dma((3,)), dma((3,)), dma((7,)), dma((7,)), dma((6,)), dma((6,)),
            dma((28,)), dma((28,)), dma((21,)), dma((21,)),
        ],
        compiler_params=pltpu.CompilerParams(
            collective_id=0, has_side_effects=True, vmem_limit_bytes=VMEM_MOST
        ),
        name="layer",
    )(*arrays)


def finish_kernel(*refs):
    half = (len(refs) - 2) // 3
    held = refs[2 * half : 3 * half]
    arriving = [
        pltpu.make_async_copy(refs[i], held[i], refs[-2].at[i]) for i in range(half)
    ]
    leaving = [
        pltpu.make_async_copy(held[i], refs[half + i], refs[-1].at[i]) for i in range(half)
    ]
    for c in arriving:
        c.start()
    for first, second in zip(arriving, leaving):
        first.wait()
        second.start()
    for c in leaving:
        c.wait()


def finish(*arrays):
    any_spec = pl.BlockSpec(memory_space=pl.ANY)
    dma = pltpu.SemaphoreType.DMA
    return pl.pallas_call(
        finish_kernel,
        out_shape=[jax.ShapeDtypeStruct(a.shape, a.dtype) for a in arrays],
        in_specs=[any_spec] * len(arrays),
        out_specs=[any_spec] * len(arrays),
        scratch_shapes=[pltpu.VMEM(a.shape, a.dtype) for a in arrays]
        + [dma((len(arrays),)), dma((len(arrays),))],
        compiler_params=pltpu.CompilerParams(vmem_limit_bytes=VMEM_MOST),
        name="finish",
    )(*arrays)


def per_device(
    query_rows,
    key_matrix_all,
    value_matrix_all,
    context_grad,
    mixture_input,
    mixture_grad,
    expert_ids,
    route_weight,
    gate_weight,
    up_weight,
    down_weight,
):
    outputs = layer(
        query_rows[0], context_grad[0], key_matrix_all[0], value_matrix_all[0],
        gate_weight[0], up_weight[0], down_weight[0],
        mixture_input[0], mixture_grad[0], expert_ids[0].T, route_weight[0].T,
    )
    (
        dq_home, dk_home, dv_home, gate_grad, up_grad, down_grad, input_grad,
    ) = finish(*outputs[:7])
    route_grad = outputs[7].T
    return (
        dq_home[None],
        dk_home[None],
        dv_home[None],
        input_grad[None],
        route_grad[None],
        gate_grad[None],
        up_grad[None],
        down_grad[None],
    )


def solution(mesh):
    spec = P("exp", "ctx", None)
    return jax.shard_map(
        per_device,
        mesh=mesh,
        in_specs=(spec,) * 11,
        out_specs=(spec,) * 8,
        check_vma=False,
    )
```
